32 devices in a mesh: mesh: 16 (over z, y, core), harm: 2 (over x).
Axes of the slice: x: 2, y: 2, z: 4, core: 2. Of those that a mesh axis runs over, the one named last changes fastest.
Arguments:
- bias_source: float32 [3, 128, 16, 256], P(None, 'mesh', 'harm'), may hold values from -6 to 6
- bias_start: float32 [3, 128, 16, 256], P(None, 'mesh', 'harm'), may hold values from -6 to 6
- region: int32 [128, 16, 256], P('mesh', 'harm'), may hold values from 0 to 3
- table_index: int32 [4], replicated, may hold values from 0 to 3
- bh_base: float32 [4], replicated, may hold values from 0.5 to 2
- bh_slope: float32 [4, 8], replicated, may hold values from 0.02 to 0.2
- conductivity: float32 [4], replicated, may hold values from 0.05 to 1
- harmonic_numbers: int32 [8], replicated, may hold values from 1 to 32
- ripple_source: float32 [8, 2, 3, 128, 16, 256], P('harm', None, None, 'mesh'), may hold values from -6 to 6
- ripple_start: float32 [8, 2, 3, 128, 16, 256], P('harm', None, None, 'mesh'), may hold values from -2 to 2
Outputs:
- bias_field: float32 [3, 128, 16, 256], P(None, 'mesh', 'harm')
- ripple_field: float32 [8, 2, 3, 128, 16, 256], P('harm', None, None, 'mesh')
- loss_density: float32 [128, 16, 256], P('mesh', 'harm')
The draws below stay inside these ranges and needn't reach their ends.
All inputs are finite; a program needn't handle non-finite values.
Results may differ from the reference program's by a relative error of at most 0.0001.
Values sent between devices are 32-bit elements; how exact they have to be, the bound alone decides.
No kernel may reach another device: no remote copies, remote signals or barrier semaphores. Data moves between devices by JAX's collectives and lax.ppermute only.
A program may use at most 128 MiB of HBM per device.

```python
import math
import jax
import jax.numpy as jnp
from jax import lax

NZ = 256
H = 8
ITERS_B = 2
ITERS_R = 2
KNOTS = 8
MATS = 4
TABLES = 4
NX = 128
NY = 16


def touch_ends(drawn, key, low, high):
    longest = drawn.shape.index(max(drawn.shape))
    spots = []
    for shift in (0, 1):
        where = [jax.random.randint(jax.random.fold_in(key, axis), (), 0, length) for axis, length in enumerate(drawn.shape)]
        where[longest] = (where[longest] + shift) % drawn.shape[longest]
        spots.append(tuple(where))
    return drawn.at[spots[0]].set(low).at[spots[1]].set(high)


def level_of(key, extent, split, low, high):
    gain = 1.0
    for axis_at, shards_of in split:
        draws = jax.random.uniform(jax.random.fold_in(jax.random.fold_in(key, 6), axis_at), (shards_of,), jnp.float32, low / len(split), high / len(split))
        gain = gain * jnp.repeat(jnp.exp(draws), extent[axis_at] // shards_of).reshape((-1,) + (1,) * (len(extent) - 1 - axis_at))
    return gain


def normal_values(stream_key, extent, spread, limit, shards=(), held_as=jnp.bfloat16):
    level = level_of(stream_key, extent, shards, -0.22, 0.18) if shards else 1.0
    result = jax.random.normal(stream_key, extent, jnp.float32) * spread * level
    return jnp.minimum(jnp.maximum(result, -limit), limit).astype(held_as)


def setup_inputs(seed: int = 0) -> dict:
    keys = jax.random.split(jax.random.key(seed), 11)
    return {
        "bias_source": normal_values(keys[0], (3, NX, NY, NZ), 1.0, 6.0, ((1, 16), (2, 2)), jnp.float32),
        "bias_start": normal_values(keys[1], (3, NX, NY, NZ), 1.0, 6.0, ((1, 16), (2, 2)), jnp.float32),
        "region": touch_ends(jax.random.randint(keys[2], (NX, NY, NZ), 0, MATS), jax.random.fold_in(keys[2], 1), 0, MATS - 1).astype(jnp.int32),
        "table_index": touch_ends(jax.random.randint(keys[3], (MATS,), 0, TABLES), jax.random.fold_in(keys[3], 1), 0, TABLES - 1).astype(jnp.int32),
        "bh_base": jnp.clip(jnp.exp(jax.random.uniform(keys[4], (TABLES,), jnp.float32, math.log(0.5), math.log(2.0))), 0.5, 2.0),
        "bh_slope": jnp.clip(jnp.exp(jax.random.uniform(keys[5], (TABLES, KNOTS), jnp.float32, math.log(0.02), math.log(0.2))), 0.02, 0.2),
        "conductivity": jnp.clip(jnp.exp(jax.random.uniform(keys[6], (MATS,), jnp.float32, math.log(0.05), math.log(1.0))), 0.05, 1.0),
        "harmonic_numbers": touch_ends(jax.random.randint(keys[7], (H,), 1, 33), jax.random.fold_in(keys[7], 1), 1, 32).astype(jnp.int32),
        "ripple_source": normal_values(keys[8], (H, 2, 3, NX, NY, NZ), 1.0, 6.0, ((0, 2), (3, 16)), jnp.float32),
        "ripple_start": normal_values(keys[9], (H, 2, 3, NX, NY, NZ), 0.3, 2.0, ((0, 2), (3, 16)), jnp.float32),
    }


kappa = 0.05
knot_step = 1.5
soft_width = 0.5
omega_step = 0.25


def beside(padded):
    return [padded[..., 2:, 1:-1, 1:-1], padded[..., :-2, 1:-1, 1:-1],
            padded[..., 1:-1, 2:, 1:-1], padded[..., 1:-1, :-2, 1:-1],
            padded[..., 1:-1, 1:-1, 2:], padded[..., 1:-1, 1:-1, :-2]]


def flux_squared(padded):
    center = padded[:, 1:-1, 1:-1, 1:-1]
    along_first = padded[:, 2:, 1:-1, 1:-1] - center
    along_second = padded[:, 1:-1, 2:, 1:-1] - center
    along_third = padded[:, 1:-1, 1:-1, 2:] - center
    flux_one = along_second[2] - along_third[1]
    flux_two = along_third[0] - along_first[2]
    flux_three = along_first[1] - along_second[0]
    return flux_one * flux_one + flux_two * flux_two + flux_three * flux_three


def material(region, table_index, bh_base, bh_slope, conductivity):
    choose = (table_index[:, None] == jnp.arange(TABLES)[None, :]).astype(jnp.float32)
    region_base = jnp.sum(choose * bh_base[None, :], axis=1)
    region_slope = jnp.sum(choose[:, :, None] * bh_slope[None, :, :], axis=1)
    cell_base = jnp.zeros(region.shape, jnp.float32)
    cell_sigma = jnp.zeros(region.shape, jnp.float32)
    cell_slope = [jnp.zeros(region.shape, jnp.float32) for knot in range(KNOTS)]
    for member_id in range(MATS):
        member = (region == member_id).astype(jnp.float32)
        cell_base = cell_base + member * region_base[member_id]
        cell_sigma = cell_sigma + member * conductivity[member_id]
        for knot in range(KNOTS):
            cell_slope[knot] = cell_slope[knot] + member * region_slope[member_id, knot]
    return cell_base, cell_slope, cell_sigma


def reluctivity(flux_sq, cell_base, cell_slope):
    value = cell_base
    slope_sum = jnp.zeros_like(flux_sq)
    for knot in range(KNOTS):
        scaled = (flux_sq - knot_step * knot) / soft_width
        value = value + cell_slope[knot] * soft_width * jax.nn.softplus(scaled)
        slope_sum = slope_sum + cell_slope[knot] * jax.nn.sigmoid(scaled)
    return value, value + 2.0 * flux_sq * slope_sum


def couplings(padded_cells):
    center = padded_cells[1:-1, 1:-1, 1:-1]
    weights = [0.5 * (center + other) for other in beside(padded_cells)]
    total = weights[0]
    for weight in weights[1:]:
        total = total + weight
    return weights, total + kappa


def relax(padded_field, padded_cells, source):
    weights, total = couplings(padded_cells)
    pull = jnp.zeros_like(source)
    for weight, other in zip(weights, beside(padded_field)):
        pull = pull + weight * other
    return (source + pull) / total


def complex_relax(padded_field, source, weights, total, damping):
    pull = jnp.zeros_like(source)
    for weight, other in zip(weights, beside(padded_field)):
        pull = pull + weight * other
    rhs = source + pull
    real_part = rhs[..., 0, :, :, :, :]
    imag_part = rhs[..., 1, :, :, :, :]
    damp = damping[..., None, :, :, :]
    denom = total * total + damp * damp
    new_real = (real_part * total + imag_part * damp) / denom
    new_imag = (imag_part * total - real_part * damp) / denom
    return jnp.stack([new_real, new_imag], axis=-5)


def reference(bias_source, bias_start, region, table_index, bh_base, bh_slope, conductivity, harmonic_numbers, ripple_source, ripple_start):
    cell_base, cell_slope, cell_sigma = material(region, table_index, bh_base, bh_slope, conductivity)
    field = bias_start
    for sweep_index in range(ITERS_B):
        padded = jnp.pad(field, ((0, 0), (1, 1), (1, 1), (1, 1)))
        reluct, unused = reluctivity(flux_squared(padded), cell_base, cell_slope)
        field = relax(padded, jnp.pad(reluct, 1), bias_source)
    padded = jnp.pad(field, ((0, 0), (1, 1), (1, 1), (1, 1)))
    unused, incremental = reluctivity(flux_squared(padded), cell_base, cell_slope)
    weights, total = couplings(jnp.pad(incremental, 1))
    omegas = omega_step * harmonic_numbers.astype(jnp.float32)

    def one_harmonic(carry, items):
        source, start, omega = items
        damping = omega * cell_sigma
        ripple = start
        for sweep_index in range(ITERS_R):
            padded_ripple = jnp.pad(ripple, ((0, 0), (0, 0), (1, 1), (1, 1), (1, 1)))
            ripple = complex_relax(padded_ripple, source, weights, total, damping)
        power = jnp.sum(ripple * ripple, axis=(0, 1))
        return carry + 0.5 * omega * omega * cell_sigma * power, ripple

    loss, ripples = lax.scan(one_harmonic, jnp.zeros((NX, NY, NZ), jnp.float32), (ripple_source, ripple_start, omegas))
    return field, ripples, loss
```

```python
import functools
import math

import jax
import jax.numpy as jnp
from jax import lax
from jax.experimental import pallas as pl
from jax.experimental.pallas import tpu as pltpu
from jax.sharding import PartitionSpec as P

ITERS_B = 2
ITERS_R = 2
KNOTS = 8
MATS = 4

kappa = 0.05
knot_step = 1.5
soft_width = 0.5
omega_step = 0.25

NUD_LOW, NUD_HIGH = ITERS_R, ITERS_R
A_LOW = [NUD_LOW + ITERS_B - step for step in range(ITERS_B + 1)]
A_HIGH = [NUD_HIGH + 1 + 2 * (ITERS_B - step) for step in range(ITERS_B + 1)]
S_LOW, S_HIGH = A_LOW[1], A_HIGH[1]
G_LOW, G_HIGH = A_LOW[0], A_HIGH[0] - 1

VMEM = pl.BlockSpec(memory_space=pltpu.VMEM)
SMEM = pl.BlockSpec(memory_space=pltpu.SMEM)
ANY = pl.BlockSpec(memory_space=pl.ANY)


def up(value, axis):
    return pltpu.roll(value, value.shape[axis] - 1, axis)


def down(value, axis):
    return pltpu.roll(value, 1, axis)


def index(shape, axis):
    return lax.broadcasted_iota(jnp.int32, shape, axis)


class Edges:
    def __init__(self, shape):
        rows, lanes = index(shape, 0), index(shape, 1)
        self.last_row, self.first_row = rows == shape[0] - 1, rows == 0
        self.last_lane, self.first_lane = lanes == shape[1] - 1, lanes == 0

    def sides(self):
        return ((up, 0, self.last_row), (down, 0, self.first_row), (up, 1, self.last_lane), (down, 1, self.first_lane))


def couplings(center, above, below, edges):
    weights = [0.5 * (center + above), 0.5 * (center + below)]
    total = weights[0] + weights[1]
    for move, axis, edge in edges.sides():
        weight = 0.5 * (center + jnp.where(edge, 0.0, move(center, axis)))
        total = total + weight
        weights.append(jnp.where(edge, 0.0, weight))
    return weights, total + kappa


def pull(weights, center, above, below):
    return (
        weights[0] * above
        + weights[1] * below
        + weights[2] * up(center, 0)
        + weights[3] * down(center, 0)
        + weights[4] * up(center, 1)
        + weights[5] * down(center, 1)
    )


def flux_squared(field, plane, edges):
    ax, ay, az = (field[part, plane] for part in range(3))
    ay_first, az_first = field[1, plane + 1], field[2, plane + 1]
    second = [jnp.where(edges.last_row, 0.0, up(value, 0)) for value in (ax, az)]
    third = [jnp.where(edges.last_lane, 0.0, up(value, 1)) for value in (ax, ay)]
    flux_one = (second[1] - az) - (third[1] - ay)
    flux_two = (third[0] - ax) - (az_first - az)
    flux_three = (ay_first - ay) - (second[0] - ax)
    return flux_one * flux_one + flux_two * flux_two + flux_three * flux_three


def reluctivity(flux_sq, base, slope_of, incremental):
    doubled = flux_sq / soft_width
    rising, falling = jnp.exp(doubled), jnp.exp(-doubled)
    value, slope_sum = 0.0, 0.0
    for knot in range(KNOTS):
        slope = slope_of(knot)
        offset = knot_step * knot / soft_width
        shift = math.exp(offset)
        small = jnp.minimum(rising * (1.0 / shift), falling * shift)
        grown = 1.0 + small
        value = value + slope * (jnp.maximum(doubled - offset, 0.0) + jnp.log(grown))
        if incremental:
            part = 1.0 / grown
            slope_sum = slope_sum + slope * jnp.where(doubled >= offset, part, small * part)
    nu = base + soft_width * value
    if incremental:
        nu = nu + 2.0 * flux_sq * slope_sum
    return nu


def pack_kernel(start, source, region, whole, forward, backward):
    planes = region.shape[0]
    marks = region[...].astype(jnp.float32)
    for part in range(3):
        whole[part * planes:(part + 1) * planes] = start[part]
        whole[(3 + part) * planes:(4 + part) * planes] = source[part]
        forward[part * A_LOW[0]:(part + 1) * A_LOW[0]] = start[part, planes - A_LOW[0]:]
        at = 3 * A_LOW[0] + part * S_LOW
        forward[at:at + S_LOW] = source[part, planes - S_LOW:]
        backward[part * A_HIGH[0]:(part + 1) * A_HIGH[0]] = start[part, :A_HIGH[0]]
        at = 3 * A_HIGH[0] + part * S_HIGH
        backward[at:at + S_HIGH] = source[part, :S_HIGH]
    whole[6 * planes:] = marks
    forward[3 * (A_LOW[0] + S_LOW):] = marks[planes - G_LOW:]
    backward[3 * (A_HIGH[0] + S_HIGH):] = marks[:G_HIGH]


LOW_SIZE = 3 * (A_LOW[0] + S_LOW) + G_LOW
HIGH_SIZE = 3 * (A_HIGH[0] + S_HIGH) + G_HIGH


def bias_kernel(others, meshes, *refs):
    wholes, lows, highs = refs[:others + 1], refs[others + 1:2 * others + 2], refs[2 * others + 2:3 * others + 3]
    table_index, bh_base, bh_slope, conductivity = refs[3 * others + 3:3 * others + 7]
    field_out, nud_out, sigma_out = refs[3 * others + 7:3 * others + 10]
    a0, a1, src, marks, nu, slopes, bases = refs[3 * others + 10:]
    planes = wholes[0].shape[0] // 7
    rows_each, lanes = wholes[0].shape[1:]
    rows = rows_each * (others + 1)
    mine = lax.axis_index("harm")
    here = lax.axis_index("mesh")
    for turn in range(others + 1):
        owner = lax.rem(mine + others + 1 - turn, others + 1)
        at = pl.ds(pl.multiple_of(owner * rows_each, rows_each), rows_each)
        whole, low, high = wholes[turn], lows[turn], highs[turn]

        def place(target, part, below, own, above, first_low, first_own, first_high):
            for count, origin, first, onto in (
                (below, low, first_low, 0), (own, whole, first_own, below), (above, high, first_high, below + own)
            ):
                target[part + (slice(onto, onto + count), at, slice(None))] = origin[first:first + count]

        for part in range(3):
            place(a0, (part,), A_LOW[0], planes, A_HIGH[0], part * A_LOW[0], part * planes, part * A_HIGH[0])
            place(
                src, (part,), S_LOW, planes, S_HIGH,
                3 * A_LOW[0] + part * S_LOW, (3 + part) * planes, 3 * A_HIGH[0] + part * S_HIGH,
            )
        place(
            marks, (), G_LOW, planes, G_HIGH, 3 * (A_LOW[0] + S_LOW), 6 * planes, 3 * (A_HIGH[0] + S_HIGH)
        )

    edges = Edges((rows, lanes))
    tables = [table_index[member] for member in range(MATS)]
    base_of = [bh_base[table] for table in tables]
    slope_of = [[bh_slope[table, knot] for table in tables] for knot in range(KNOTS)]
    sigma_of = [conductivity[member] for member in range(MATS)]

    def inside(plane):
        low_ok = jnp.logical_or(plane >= 0, here > 0)
        high_ok = jnp.logical_or(plane < planes, here < meshes - 1)
        return jnp.where(jnp.logical_and(low_ok, high_ok), 1.0, 0.0)

    def choose(mark, values):
        chosen = jnp.where(mark == 1.0, values[1], values[0])
        for member in range(2, MATS):
            chosen = jnp.where(mark == float(member), values[member], chosen)
        return chosen

    def relax_into(target, step, old):
        def body(at, carry):
            plane = at - A_LOW[step]
            near = plane + A_LOW[step] + 1
            weights, total = couplings(nu[near], nu[near + 1], nu[near - 1], edges)
            scale = inside(plane) / total
            from_old = plane + A_LOW[step - 1]
            for part in range(3):
                moved = pull(weights, old[part, from_old], old[part, from_old + 1], old[part, from_old - 1])
                target[part, at] = (src[part, plane + S_LOW] + moved) * scale
            return carry

        lax.fori_loop(0, planes + A_LOW[step] + A_HIGH[step], body, 0)

    def first_nu(at, carry):
        mark = marks[at]
        bases[at] = choose(mark, base_of)
        for knot in range(KNOTS):
            slopes[knot, at] = choose(mark, slope_of[knot])
        value = reluctivity(flux_squared(a0, at, edges), bases[at], lambda knot: slopes[knot, at], False)
        nu[at] = value * inside(at - G_LOW)
        return carry

    lax.fori_loop(0, planes + G_LOW + G_HIGH, first_nu, 0)
    fields = (a0, a1)
    for step in range(1, ITERS_B + 1):
        old, new = fields[(step - 1) % 2], fields[step % 2]
        relax_into(new, step, old)
        last = step == ITERS_B
        lower = NUD_LOW if last else A_LOW[step + 1] + 1
        upper = NUD_HIGH if last else A_HIGH[step + 1] + 1

        def next_nu(at, carry):
            plane = at - lower
            known = plane + G_LOW
            value = reluctivity(
                flux_squared(new, plane + A_LOW[step], edges), bases[known], lambda knot: slopes[knot, known], last
            )
            value = value * inside(plane)
            if last:
                nud_out[at] = value
            else:
                nu[at] = value
            return carry

        lax.fori_loop(0, planes + lower + upper, next_nu, 0)

    def sigma_at(at, carry):
        sigma_out[at] = choose(marks[at - (ITERS_R - 1) + G_LOW], sigma_of)
        return carry

    lax.fori_loop(0, planes + 2 * (ITERS_R - 1), sigma_at, 0)
    own_rows = pl.ds(pl.multiple_of(mine * rows_each, rows_each), rows_each)
    final = fields[ITERS_B % 2]
    for part in range(3):
        field_out[part] = final[part, A_LOW[ITERS_B]:A_LOW[ITERS_B] + planes, own_rows, :]


def ripple_kernel(
    shares, meshes, harmonic_numbers, nud, sigma, start, source, low, high, ripple_out, loss_out, r0, r1, src, loss, sems
):
    count, planes = start.shape[0], start.shape[3]
    rows, lanes = start.shape[4:]
    mine = lax.axis_index("harm")
    here = lax.axis_index("mesh")
    copies = [
        pltpu.make_async_copy(low.at[:, :, :, 0:2], r0.at[:, :, :, 0:2], sems.at[0]),
        pltpu.make_async_copy(low.at[:, :, :, 2:3], src.at[:, :, :, 0:1], sems.at[1]),
        pltpu.make_async_copy(start, r0.at[:, :, :, 2:planes + 2], sems.at[2]),
        pltpu.make_async_copy(source, src.at[:, :, :, 1:planes + 1], sems.at[3]),
        pltpu.make_async_copy(high.at[:, :, :, 0:2], r0.at[:, :, :, planes + 2:planes + 4], sems.at[4]),
        pltpu.make_async_copy(high.at[:, :, :, 2:3], src.at[:, :, :, planes + 1:planes + 2], sems.at[5]),
    ]
    for copy in copies:
        copy.start()
    for copy in copies:
        copy.wait()
    edges = Edges((rows, lanes))
    omegas = [omega_step * harmonic_numbers[mine * count + harmonic].astype(jnp.float32) for harmonic in range(count)]

    def sweep(old, offset, plane, store):
        near = plane + NUD_LOW
        weights, total = couplings(nud[near], nud[near + 1], nud[near - 1], edges)
        conduct = sigma[plane + 1]
        for harmonic in range(count):
            damp = omegas[harmonic] * conduct
            inverse = 1.0 / (total * total + damp * damp)
            straight, turned = total * inverse, damp * inverse
            power = 0.0
            for part in range(3):
                sides = []
                for piece in range(2):
                    field = old.at[harmonic, piece, part]
                    moved = pull(weights, field[plane + offset], field[plane + offset + 1], field[plane + offset - 1])
                    sides.append(src[harmonic, piece, part, plane + 1] + moved)
                real = sides[0] * straight + sides[1] * turned
                imag = sides[1] * straight - sides[0] * turned
                power = power + (real * real + imag * imag)
                store(harmonic, part, real, imag)
            yield harmonic, conduct, power

    def first(at, carry):
        plane = at - 1
        low_ok = jnp.logical_or(plane >= 0, here > 0)
        high_ok = jnp.logical_or(plane < planes, here < meshes - 1)
        keep = jnp.where(jnp.logical_and(low_ok, high_ok), 1.0, 0.0)

        def store(harmonic, part, real, imag):
            r1[harmonic, 0, part, at] = real * keep
            r1[harmonic, 1, part, at] = imag * keep

        for unused in sweep(r0, 2, plane, store):
            pass
        return carry

    lax.fori_loop(0, planes + 2, first, 0)

    def second(plane, carry):
        def store(harmonic, part, real, imag):
            ripple_out[harmonic, 0, part, plane] = real
            ripple_out[harmonic, 1, part, plane] = imag

        summed = 0.0
        for harmonic, conduct, power in sweep(r1, 1, plane, store):
            summed = summed + (0.5 * omegas[harmonic] * omegas[harmonic]) * conduct * power
        loss[plane] = summed
        return carry

    lax.fori_loop(0, planes, second, 0)
    rows_each = rows // shares
    for turn in range(shares):
        owner = lax.rem(mine + turn, shares)
        loss_out[turn] = loss[:, pl.ds(pl.multiple_of(owner * rows_each, rows_each), rows_each), :]


def body(
    meshes, shares, bias_source, bias_start, region, table_index, bh_base, bh_slope, conductivity, harmonic_numbers,
    ripple_source, ripple_start,
):
    f32 = jnp.float32
    unused, planes, rows_each, lanes = bias_start.shape
    rows = rows_each * shares
    count = ripple_start.shape[0]
    upward = [(i, i + 1) for i in range(meshes - 1)]
    downward = [(i + 1, i) for i in range(meshes - 1)]
    turned = [[(i, (i + turn) % shares) for i in range(shares)] for turn in range(1, shares)]

    whole, forward, backward = pl.pallas_call(
        pack_kernel,
        out_shape=[jax.ShapeDtypeStruct((size, rows_each, lanes), f32) for size in (7 * planes, LOW_SIZE, HIGH_SIZE)],
        in_specs=[VMEM] * 3,
        out_specs=[VMEM] * 3,
        name="pack",
    )(bias_start, bias_source, region)
    wholes = [whole] + [lax.ppermute(whole, "harm", pairs) for pairs in turned]
    low = lax.ppermute(forward, "mesh", upward)
    high = lax.ppermute(backward, "mesh", downward)
    lows = [low] + [lax.ppermute(low, "harm", pairs) for pairs in turned]
    highs = [high] + [lax.ppermute(high, "harm", pairs) for pairs in turned]

    ripple_up = jnp.concatenate([ripple_start[:, :, :, planes - 2:], ripple_source[:, :, :, planes - 1:]], axis=3)
    ripple_down = jnp.concatenate([ripple_start[:, :, :, :2], ripple_source[:, :, :, :1]], axis=3)
    ripple_low = lax.ppermute(ripple_up, "mesh", upward)
    ripple_high = lax.ppermute(ripple_down, "mesh", downward)

    def scratch(*shape):
        return pltpu.VMEM(shape, f32)

    field, nud, sigma = pl.pallas_call(
        functools.partial(bias_kernel, shares - 1, meshes),
        out_shape=[
            jax.ShapeDtypeStruct(bias_start.shape, f32),
            jax.ShapeDtypeStruct((planes + NUD_LOW + NUD_HIGH, rows, lanes), f32),
            jax.ShapeDtypeStruct((planes + 2 * (ITERS_R - 1), rows, lanes), f32),
        ],
        in_specs=[VMEM] * (3 * shares) + [SMEM] * 4,
        out_specs=[VMEM] * 3,
        scratch_shapes=[
            scratch(3, planes + A_LOW[0] + A_HIGH[0], rows, lanes),
            scratch(3, planes + A_LOW[1] + A_HIGH[1], rows, lanes),
            scratch(3, planes + S_LOW + S_HIGH, rows, lanes),
            scratch(planes + G_LOW + G_HIGH, rows, lanes),
            scratch(planes + G_LOW + G_HIGH, rows, lanes),
            scratch(KNOTS, planes + G_LOW + G_HIGH, rows, lanes),
            scratch(planes + G_LOW + G_HIGH, rows, lanes),
        ],
        compiler_params=pltpu.CompilerParams(vmem_limit_bytes=56 * 2**20),
        name="bias",
    )(*wholes, *lows, *highs, table_index, bh_base, bh_slope, conductivity)

    ripple, losses = pl.pallas_call(
        functools.partial(ripple_kernel, shares, meshes),
        out_shape=[
            jax.ShapeDtypeStruct(ripple_start.shape, f32),
            jax.ShapeDtypeStruct((shares, planes, rows_each, lanes), f32),
        ],
        in_specs=[SMEM, VMEM, VMEM] + [ANY] * 4,
        out_specs=[VMEM] * 2,
        scratch_shapes=[
            scratch(count, 2, 3, planes + 4, rows, lanes),
            scratch(count, 2, 3, planes + 2, rows, lanes),
            scratch(count, 2, 3, planes + 2, rows, lanes),
            scratch(planes, rows, lanes),
            pltpu.SemaphoreType.DMA((6,)),
        ],
        compiler_params=pltpu.CompilerParams(vmem_limit_bytes=56 * 2**20),
        name="ripple",
    )(harmonic_numbers, nud, sigma, ripple_start, ripple_source, ripple_low, ripple_high)
    loss = losses[0]
    for turn, pairs in enumerate(turned):
        loss = loss + lax.ppermute(losses[turn + 1], "harm", pairs)
    return field, ripple, loss


def solution(mesh):
    return jax.shard_map(
        functools.partial(body, mesh.shape["mesh"], mesh.shape["harm"]),
        mesh=mesh,
        in_specs=(
            P(None, "mesh", "harm", None),
            P(None, "mesh", "harm", None),
            P("mesh", "harm", None),
            P(),
            P(),
            P(),
            P(),
            P(),
            P("harm", None, None, "mesh", None, None),
            P("harm", None, None, "mesh", None, None),
        ),
        out_specs=(
            P(None, "mesh", "harm", None),
            P("harm", None, None, "mesh", None, None),
            P("mesh", "harm", None),
        ),
        check_vma=False,
    )
```

```python
import functools
import math

import jax
import jax.numpy as jnp
from jax import lax
from jax.experimental import pallas as pl
from jax.experimental.pallas import tpu as pltpu
from jax.sharding import PartitionSpec as P

ITERS_B = 2
ITERS_R = 2
KNOTS = 8
MATS = 4

kappa = 0.05
knot_step = 1.5
soft_width = 0.5
omega_step = 0.25

NUD_LOW, NUD_HIGH = ITERS_R, ITERS_R
A_LOW = [NUD_LOW + ITERS_B - step for step in range(ITERS_B + 1)]
A_HIGH = [NUD_HIGH + 1 + 2 * (ITERS_B - step) for step in range(ITERS_B + 1)]
S_LOW, S_HIGH = A_LOW[1], A_HIGH[1]
G_LOW, G_HIGH = A_LOW[0], A_HIGH[0] - 1

BIAS_WORK = 1000000000
RP_ROOM = 58 * 2**20
PACK_ROOM = 62 * 2**20
RIPPLE_ROOM = 59 * 2**20 + 2**19
RP_WORK = 0
HOLD_WORK = 0
VMEM = pl.BlockSpec(memory_space=pltpu.VMEM)
SMEM = pl.BlockSpec(memory_space=pltpu.SMEM)
ANY = pl.BlockSpec(memory_space=pl.ANY)


def up(value, axis):
    return pltpu.roll(value, value.shape[axis] - 1, axis)


def down(value, axis):
    return pltpu.roll(value, 1, axis)


def index(shape, axis):
    return lax.broadcasted_iota(jnp.int32, shape, axis)


class Edges:
    def __init__(self, shape):
        rows, lanes = index(shape, 0), index(shape, 1)
        self.last_row, self.first_row = rows == shape[0] - 1, rows == 0
        self.last_lane, self.first_lane = lanes == shape[1] - 1, lanes == 0

    def sides(self):
        return ((up, 0, self.last_row), (down, 0, self.first_row), (up, 1, self.last_lane), (down, 1, self.first_lane))


def couplings(center, above, below, edges):
    weights = [0.5 * (center + above), 0.5 * (center + below)]
    total = weights[0] + weights[1]
    for move, axis, edge in edges.sides():
        weight = 0.5 * (center + jnp.where(edge, 0.0, move(center, axis)))
        total = total + weight
        weights.append(jnp.where(edge, 0.0, weight))
    return weights, total + kappa


def pull(weights, center, above, below):
    return (
        weights[0] * above
        + weights[1] * below
        + weights[2] * up(center, 0)
        + weights[3] * down(center, 0)
        + weights[4] * up(center, 1)
        + weights[5] * down(center, 1)
    )


def flux_squared(field, plane, edges):
    ax, ay, az = (field[part, plane] for part in range(3))
    ay_first, az_first = field[1, plane + 1], field[2, plane + 1]
    second = [jnp.where(edges.last_row, 0.0, up(value, 0)) for value in (ax, az)]
    third = [jnp.where(edges.last_lane, 0.0, up(value, 1)) for value in (ax, ay)]
    flux_one = (second[1] - az) - (third[1] - ay)
    flux_two = (third[0] - ax) - (az_first - az)
    flux_three = (ay_first - ay) - (second[0] - ax)
    return flux_one * flux_one + flux_two * flux_two + flux_three * flux_three


def reluctivity(flux_sq, base, slope_of, incremental):
    doubled = flux_sq / soft_width
    rising, falling = jnp.exp(doubled), jnp.exp(-doubled)
    value, slope_sum = 0.0, 0.0
    for knot in range(KNOTS):
        slope = slope_of(knot)
        offset = knot_step * knot / soft_width
        shift = math.exp(offset)
        small = jnp.minimum(rising * (1.0 / shift), falling * shift)
        grown = 1.0 + small
        value = value + slope * (jnp.maximum(doubled - offset, 0.0) + jnp.log(grown))
        if incremental:
            part = 1.0 / grown
            slope_sum = slope_sum + slope * jnp.where(doubled >= offset, part, small * part)
    nu = base + soft_width * value
    if incremental:
        nu = nu + 2.0 * flux_sq * slope_sum
    return nu


LOW_SIZE = 3 * (A_LOW[0] + S_LOW) + G_LOW
HIGH_SIZE = 3 * (A_HIGH[0] + S_HIGH) + G_HIGH


def edge_parts(planes, low):
    halo_of = ((A_LOW if low else A_HIGH)[0], S_LOW if low else S_HIGH, G_LOW if low else G_HIGH)
    at, parts = 0, []
    for array in range(7):
        halo = halo_of[0 if array < 3 else 1 if array < 6 else 2]
        parts.append((array * planes + (planes - halo if low else 0), at, halo))
        at += halo
    return parts


def write_edge(target, whole, low):
    for first, at, halo in edge_parts(whole.shape[0] // 7, low):
        target[at:at + halo] = whole[first:first + halo]


def is_odd():
    return lax.rem(lax.axis_index("mesh"), 2) == 1


def pack_kernel(start, source, region, whole, apart, marks, sems):
    planes = region.shape[0]
    copies = [pltpu.make_async_copy(region, marks, sems.at[0])]
    for part in range(3):
        for at, origin in ((part, start), (3 + part, source)):
            target = whole.at[at * planes:(at + 1) * planes]
            copies.append(pltpu.make_async_copy(origin.at[part], target, sems.at[at + 1]))
    for copy in copies:
        copy.start()
    for copy in copies:
        copy.wait()
    whole[6 * planes:] = marks[...].astype(jnp.float32)
    for odd in (False, True):
        pl.when(is_odd() == odd)(functools.partial(write_edge, apart, whole, odd))


def pair_kernel(*refs):
    wholes, paired = refs[:-2], refs[-1]
    for odd in (False, True):

        @pl.when(is_odd() == odd)
        def write():
            for turn, whole in enumerate(wholes):
                write_edge(paired.at[turn], whole, not odd)


def hold_kernel(apart, paired, after, apart_out, paired_out):
    pass


def ripple_pack_kernel(start, source, apart, paired, sems):
    planes = start.shape[3]
    odd = is_odd()
    copies = []
    for at, (target, top) in enumerate(((apart, odd), (paired, jnp.logical_not(odd)))):
        first = jnp.where(top, planes - 2, 0)
        copies.append(
            pltpu.make_async_copy(start.at[:, :, :, pl.ds(first, 2)], target.at[:, :, :, 0:2], sems.at[2 * at])
        )
        first = jnp.where(top, planes - 1, 0)
        copies.append(
            pltpu.make_async_copy(source.at[:, :, :, pl.ds(first, 1)], target.at[:, :, :, 2:3], sems.at[2 * at + 1])
        )
    for copy in copies:
        copy.start()
    for copy in copies:
        copy.wait()


def bias_kernel(shares, meshes, *refs):
    wholes, aparts, paired = refs[:shares], refs[shares:2 * shares], refs[2 * shares]
    table_index, bh_base, bh_slope, conductivity, field_out, nud_out, sigma_out = refs[2 * shares + 1:2 * shares + 8]
    a0, a1, src, marks, nu, slopes, bases = refs[2 * shares + 8:]
    planes = wholes[0].shape[0] // 7
    rows_each, lanes = wholes[0].shape[1:]
    rows = rows_each * shares
    mine = lax.axis_index("harm")
    here = lax.axis_index("mesh")
    arrays = [(a0.at[part], A_LOW[0]) for part in range(3)]
    arrays += [(src.at[part], S_LOW) for part in range(3)] + [(marks, G_LOW)]
    for turn in range(shares):
        owner = lax.rem(mine + shares - turn, shares)
        at = pl.ds(pl.multiple_of(owner * rows_each, rows_each), rows_each)

        def fill(low, high):
            for (target, onto), (unused, first, halo) in zip(arrays, edge_parts(planes, True)):
                target[0:halo, at, :] = low[first:first + halo]
            for (target, onto), (unused, first, halo) in zip(arrays, edge_parts(planes, False)):
                target[onto + planes:onto + planes + halo, at, :] = high[first:first + halo]

        for number, (target, onto) in enumerate(arrays):
            target[onto:onto + planes, at, :] = wholes[turn][number * planes:(number + 1) * planes]
        pl.when(is_odd())(functools.partial(fill, paired.at[turn], aparts[turn]))
        pl.when(jnp.logical_not(is_odd()))(functools.partial(fill, aparts[turn], paired.at[turn]))

    edges = Edges((rows, lanes))
    tables = [table_index[member] for member in range(MATS)]
    base_of = [bh_base[table] for table in tables]
    slope_of = [[bh_slope[table, knot] for table in tables] for knot in range(KNOTS)]
    sigma_of = [conductivity[member] for member in range(MATS)]

    def inside(plane):
        low_ok = jnp.logical_or(plane >= 0, here > 0)
        high_ok = jnp.logical_or(plane < planes, here < meshes - 1)
        return jnp.where(jnp.logical_and(low_ok, high_ok), 1.0, 0.0)

    def choose(mark, values):
        chosen = jnp.where(mark == 1.0, values[1], values[0])
        for member in range(2, MATS):
            chosen = jnp.where(mark == float(member), values[member], chosen)
        return chosen

    def relax_into(target, step, old):
        def body(at, carry):
            plane = at - A_LOW[step]
            near = plane + A_LOW[step] + 1
            weights, total = couplings(nu[near], nu[near + 1], nu[near - 1], edges)
            scale = inside(plane) / total
            from_old = plane + A_LOW[step - 1]
            for part in range(3):
                moved = pull(weights, old[part, from_old], old[part, from_old + 1], old[part, from_old - 1])
                target[part, at] = (src[part, plane + S_LOW] + moved) * scale
            return carry

        lax.fori_loop(0, planes + A_LOW[step] + A_HIGH[step], body, 0)

    def first_nu(at, carry):
        mark = marks[at]
        bases[at] = choose(mark, base_of)
        for knot in range(KNOTS):
            slopes[knot, at] = choose(mark, slope_of[knot])
        value = reluctivity(flux_squared(a0, at, edges), bases[at], lambda knot: slopes[knot, at], False)
        nu[at] = value * inside(at - G_LOW)
        return carry

    lax.fori_loop(0, planes + G_LOW + G_HIGH, first_nu, 0)
    fields = (a0, a1)
    for step in range(1, ITERS_B + 1):
        old, new = fields[(step - 1) % 2], fields[step % 2]
        relax_into(new, step, old)
        last = step == ITERS_B
        lower = NUD_LOW if last else A_LOW[step + 1] + 1
        upper = NUD_HIGH if last else A_HIGH[step + 1] + 1

        def next_nu(at, carry):
            plane = at - lower
            known = plane + G_LOW
            value = reluctivity(
                flux_squared(new, plane + A_LOW[step], edges), bases[known], lambda knot: slopes[knot, known], last
            )
            value = value * inside(plane)
            if last:
                nud_out[at] = value
            else:
                nu[at] = value
            return carry

        lax.fori_loop(0, planes + lower + upper, next_nu, 0)

    def sigma_at(at, carry):
        sigma_out[at] = choose(marks[at - (ITERS_R - 1) + G_LOW], sigma_of)
        return carry

    lax.fori_loop(0, planes + 2 * (ITERS_R - 1), sigma_at, 0)
    own_rows = pl.ds(pl.multiple_of(mine * rows_each, rows_each), rows_each)
    final = fields[ITERS_B % 2]
    for part in range(3):
        field_out[part] = final[part, A_LOW[ITERS_B]:A_LOW[ITERS_B] + planes, own_rows, :]


def ripple_kernel(shares, meshes, harmonic_numbers, nud, sigma, start, source, apart, paired, ripple_out, *refs):
    losses, (r0, r1, r2, src, loss, r_sems, s_sems, out_sems) = refs[:shares], refs[shares:]
    count, planes = start.shape[0], start.shape[3]
    rows, lanes = start.shape[4:]
    mine = lax.axis_index("harm")
    here = lax.axis_index("mesh")
    top = planes + 2

    def fetch(origin, first, target, onto, sems):
        return pltpu.make_async_copy(
            origin.at[:, :, :, pl.ds(first, 1)], target.at[:, :, :, pl.ds(onto, 1)], sems.at[onto]
        )

    odd = is_odd()
    for origin, above in ((apart, odd), (paired, jnp.logical_not(odd))):
        onto = jnp.where(above, top, 0)
        for plane in range(2):
            fetch(origin, plane, r0, onto + plane, r_sems).start()
        fetch(origin, 2, src, jnp.where(above, planes + 1, 0), s_sems).start()
    for plane in range(planes):
        fetch(start, plane, r0, plane + 2, r_sems).start()
        fetch(source, plane, src, plane + 1, s_sems).start()
    for plane in range(2):
        fetch(start, 0, r0, plane, r_sems).wait()

    def drain(plane):
        return pltpu.make_async_copy(
            r2.at[:, :, :, pl.ds(plane, 1)], ripple_out.at[:, :, :, pl.ds(plane, 1)], out_sems.at[plane]
        )

    edges = Edges((rows, lanes))
    omegas = [omega_step * harmonic_numbers[mine * count + harmonic].astype(jnp.float32) for harmonic in range(count)]

    def sweep(old, offset, plane, store):
        near = plane + NUD_LOW
        weights, total = couplings(nud[near], nud[near + 1], nud[near - 1], edges)
        conduct = sigma[plane + 1]
        for harmonic in range(count):
            damp = omegas[harmonic] * conduct
            inverse = 1.0 / (total * total + damp * damp)
            straight, turned = total * inverse, damp * inverse
            power = 0.0
            for part in range(3):
                sides = []
                for piece in range(2):
                    field = old.at[harmonic, piece, part]
                    moved = pull(weights, field[plane + offset], field[plane + offset + 1], field[plane + offset - 1])
                    sides.append(src[harmonic, piece, part, plane + 1] + moved)
                real = sides[0] * straight + sides[1] * turned
                imag = sides[1] * straight - sides[0] * turned
                power = power + (real * real + imag * imag)
                store(harmonic, part, real, imag)
            yield harmonic, conduct, power

    def first(at, carry):
        plane = at - 1
        fetch(start, 0, r0, at + 2, r_sems).wait()
        fetch(start, 0, src, at, s_sems).wait()
        low_ok = jnp.logical_or(plane >= 0, here > 0)
        high_ok = jnp.logical_or(plane < planes, here < meshes - 1)
        keep = jnp.where(jnp.logical_and(low_ok, high_ok), 1.0, 0.0)

        def store(harmonic, part, real, imag):
            r1[harmonic, 0, part, at] = real * keep
            r1[harmonic, 1, part, at] = imag * keep

        for unused in sweep(r0, 2, plane, store):
            pass
        return carry

    lax.fori_loop(0, planes + 2, first, 0)

    def second(plane, carry):
        def store(harmonic, part, real, imag):
            r2[harmonic, 0, part, plane] = real
            r2[harmonic, 1, part, plane] = imag

        summed = 0.0
        for harmonic, conduct, power in sweep(r1, 1, plane, store):
            summed = summed + (0.5 * omegas[harmonic] * omegas[harmonic]) * conduct * power
        loss[plane] = summed
        drain(plane).start()
        return carry

    lax.fori_loop(0, planes, second, 0)
    rows_each = rows // shares
    for turn in range(shares):
        owner = lax.rem(mine + turn, shares)
        losses[turn][...] = loss[:, pl.ds(pl.multiple_of(owner * rows_each, rows_each), rows_each), :]
    for plane in range(planes):
        drain(plane).wait()


def call(kernel, operands, in_specs, out_shapes, out_specs, scratch, name, work=0, aliases={}, room=0):
    f32 = jnp.float32
    shapes = [o.shape for o, spec in zip(operands, in_specs) if spec is VMEM]
    shapes += [shape for shape, spec in zip(out_shapes, out_specs) if spec is VMEM]
    shapes += [shape for shape in scratch if isinstance(shape, tuple)]
    held = 4 * sum(math.prod(shape) for shape in shapes)
    return pl.pallas_call(
        kernel,
        out_shape=[jax.ShapeDtypeStruct(shape, f32) for shape in out_shapes],
        in_specs=in_specs,
        out_specs=out_specs,
        scratch_shapes=[pltpu.VMEM(shape, f32) if isinstance(shape, tuple) else shape for shape in scratch],
        compiler_params=pltpu.CompilerParams(vmem_limit_bytes=room or held + 6 * 2**20),
        cost_estimate=pl.CostEstimate(flops=work * 300, bytes_accessed=work, transcendentals=0),
        input_output_aliases=aliases,
        name=name,
    )(*operands)


def body(
    meshes, shares, bias_source, bias_start, region, table_index, bh_base, bh_slope, conductivity, harmonic_numbers,
    ripple_source, ripple_start,
):
    unused, planes, rows_each, lanes = bias_start.shape
    rows = rows_each * shares
    count = ripple_start.shape[0]
    near = [(i, i + 1) for i in range(0, meshes - 1, 2)]
    far = [(i, i + 1) for i in range(1, meshes - 1, 2)]
    near += [(j, i) for i, j in near]
    far += [(j, i) for i, j in far]
    turned = [[(i, (i + turn) % shares) for i in range(shares)] for turn in range(1, shares)]

    def around(block):
        return [block] + [lax.ppermute(block, "harm", pairs) for pairs in turned]

    whole, apart = call(
        pack_kernel, (bias_start, bias_source, region), [ANY] * 3,
        [(7 * planes, rows_each, lanes), (HIGH_SIZE, rows_each, lanes)], [VMEM] * 2,
        [pltpu.VMEM(region.shape, region.dtype), pltpu.SemaphoreType.DMA((7,))], "pack", room=PACK_ROOM,
    )
    wholes = around(whole)
    aparts = around(lax.ppermute(apart, "mesh", far))
    edge = ripple_start.shape[:3] + (3, rows, lanes)
    ripple_apart, ripple_paired = call(
        ripple_pack_kernel, (ripple_start, ripple_source), [ANY] * 2, [edge, edge], [VMEM] * 2,
        [pltpu.SemaphoreType.DMA((4,))], "ripple_pack", RP_WORK, room=RP_ROOM,
    )
    paired, = call(
        pair_kernel, (*wholes, ripple_apart), [VMEM] * shares + [ANY], [(shares, HIGH_SIZE, rows_each, lanes)], [VMEM], [], "pair"
    )
    paired = lax.ppermute(paired, "mesh", near)

    ripple_apart, ripple_paired = call(
        hold_kernel, (ripple_apart, ripple_paired, aparts[0]), [ANY] * 3, [edge, edge], [ANY] * 2, [], "hold",
        HOLD_WORK, {0: 0, 1: 1},
    )
    ripple_apart = lax.ppermute(ripple_apart, "mesh", far)
    ripple_paired = lax.ppermute(ripple_paired, "mesh", near)

    known = (planes + G_LOW + G_HIGH, rows, lanes)
    field, nud, sigma = call(
        functools.partial(bias_kernel, shares, meshes),
        (*wholes, *aparts, paired, table_index, bh_base, bh_slope, conductivity),
        [VMEM] * (2 * shares + 1) + [SMEM] * 4,
        [
            bias_start.shape, (planes + NUD_LOW + NUD_HIGH, rows, lanes), (planes + 2 * (ITERS_R - 1), rows, lanes)
        ],
        [VMEM] * 3,
        [
            (3, planes + A_LOW[0] + A_HIGH[0], rows, lanes),
            (3, planes + A_LOW[1] + A_HIGH[1], rows, lanes),
            (3, planes + S_LOW + S_HIGH, rows, lanes),
            known,
            known,
            (KNOTS, *known),
            known,
        ],
        "bias",
        BIAS_WORK,
    )

    ripple, *losses = call(
        functools.partial(ripple_kernel, shares, meshes),
        (harmonic_numbers, nud, sigma, ripple_start, ripple_source, ripple_apart, ripple_paired),
        [SMEM, VMEM, VMEM] + [ANY] * 4,
        [ripple_start.shape] + [(planes, rows_each, lanes)] * shares,
        [ANY] + [VMEM] * shares,
        [
            (count, 2, 3, planes + 4, rows, lanes),
            (count, 2, 3, planes + 2, rows, lanes),
            (count, 2, 3, planes, rows, lanes),
            (count, 2, 3, planes + 2, rows, lanes),
            (planes, rows, lanes),
            pltpu.SemaphoreType.DMA((planes + 4,)),
            pltpu.SemaphoreType.DMA((planes + 2,)),
            pltpu.SemaphoreType.DMA((planes,)),
        ],
        "ripple",
        room=RIPPLE_ROOM,
    )
    loss = losses[0]
    for turn, pairs in enumerate(turned):
        loss = loss + lax.ppermute(losses[turn + 1], "harm", pairs)
    return field, ripple, loss


def solution(mesh):
    return jax.shard_map(
        functools.partial(body, mesh.shape["mesh"], mesh.shape["harm"]),
        mesh=mesh,
        in_specs=(
            P(None, "mesh", "harm", None),
            P(None, "mesh", "harm", None),
            P("mesh", "harm", None),
            P(),
            P(),
            P(),
            P(),
            P(),
            P("harm", None, None, "mesh", None, None),
            P("harm", None, None, "mesh", None, None),
        ),
        out_specs=(
            P(None, "mesh", "harm", None),
            P("harm", None, None, "mesh", None, None),
            P("mesh", "harm", None),
        ),
        check_vma=False,
    )
```

```python
import functools
import math

import jax
import jax.numpy as jnp
from jax import lax
from jax.experimental import pallas as pl
from jax.experimental.pallas import tpu as pltpu
from jax.sharding import PartitionSpec as P

ITERS_B = 2
ITERS_R = 2
KNOTS = 8
MATS = 4

kappa = 0.05
knot_step = 1.5
soft_width = 0.5
omega_step = 0.25
CAP = 80.0

NUD_LOW, NUD_HIGH = ITERS_R, ITERS_R
A_LOW = [NUD_LOW + ITERS_B - step for step in range(ITERS_B + 1)]
A_HIGH = [NUD_HIGH + 1 + 2 * (ITERS_B - step) for step in range(ITERS_B + 1)]
S_LOW, S_HIGH = A_LOW[1], A_HIGH[1]
G_LOW, G_HIGH = A_LOW[0], A_HIGH[0] - 1

BIAS_WORK = 1000000000
RP_ROOM = 58 * 2**20
PACK_ROOM = 62 * 2**20
RIPPLE_ROOM = 59 * 2**20 + 2**19
RP_WORK = 0
HOLD_WORK = 0
VMEM = pl.BlockSpec(memory_space=pltpu.VMEM)
SMEM = pl.BlockSpec(memory_space=pltpu.SMEM)
ANY = pl.BlockSpec(memory_space=pl.ANY)


TILE = (8, 128)


class Tiles:
    def __init__(self, rows, lanes):
        self.grid = (rows // TILE[0], lanes // TILE[1])
        self.spots = [(i, j) for i in range(self.grid[0]) for j in range(self.grid[1])]
        self.at_end, self.at_start = [], []
        for axis in range(2):
            place = lax.broadcasted_iota(jnp.int32, TILE, axis)
            self.at_end.append(place == TILE[axis] - 1)
            self.at_start.append(place == 0)

    def where(self, spot):
        return (slice(spot[0] * TILE[0], (spot[0] + 1) * TILE[0]), slice(spot[1] * TILE[1], (spot[1] + 1) * TILE[1]))

    def load(self, ref, *lead):
        return {spot: ref[lead + self.where(spot)] for spot in self.spots}

    def store(self, ref, lead, values):
        for spot in self.spots:
            ref[lead + self.where(spot)] = values[spot]

    def each(self, function, *values):
        return {spot: function(*(value[spot] for value in values)) for spot in self.spots}

    def side(self, step, axis):
        return (self.at_end if step > 0 else self.at_start)[axis]

    def is_edge(self, spot, step, axis):
        return spot[axis] == (self.grid[axis] - 1 if step > 0 else 0)

    def move(self, values, step, axis, fill):
        rolled = self.each(lambda tile: pltpu.roll(tile, TILE[axis] - 1 if step > 0 else 1, axis), values)
        side, moved = self.side(step, axis), {}
        for spot in self.spots:
            if self.is_edge(spot, step, axis):
                moved[spot] = jnp.where(side, 0.0, rolled[spot]) if fill else rolled[spot]
            else:
                other = (spot[0] + step, spot[1]) if axis == 0 else (spot[0], spot[1] + step)
                moved[spot] = jnp.where(side, rolled[other], rolled[spot])
        return moved

    def inner(self, values, step, axis):
        side = self.side(step, axis)
        return {
            spot: jnp.where(side, 0.0, values[spot]) if self.is_edge(spot, step, axis) else values[spot]
            for spot in self.spots
        }


SIDES = ((1, 0), (-1, 0), (1, 1), (-1, 1))


def double_couplings(tiles, center, above, below):
    add = lambda one, other: one + other
    weights = [tiles.each(add, center, above), tiles.each(add, center, below)]
    total = tiles.each(add, *weights)
    for step, axis in SIDES:
        weight = tiles.each(add, center, tiles.move(center, step, axis, True))
        total = tiles.each(add, total, weight)
        weights.append(tiles.inner(weight, step, axis))
    return weights, tiles.each(lambda value: value + 2.0 * kappa, total)


def pull(tiles, start, weights, center, above, below):
    moved = [above, below] + [tiles.move(center, step, axis, False) for step, axis in SIDES]
    total = start
    for weight, other in zip(weights, moved):
        total = tiles.each(lambda so_far, w, value: so_far + w * value, total, weight, other)
    return total


def flux_squared(tiles, field, plane):
    ax, ay, az = (tiles.load(field, part, plane) for part in range(3))
    ay_first, az_first = tiles.load(field, 1, plane + 1), tiles.load(field, 2, plane + 1)
    ax_second, az_second = tiles.move(ax, 1, 0, True), tiles.move(az, 1, 0, True)
    ax_third, ay_third = tiles.move(ax, 1, 1, True), tiles.move(ay, 1, 1, True)

    def square(x, y, z, y1, z1, x2, z2, x3, y3):
        flux_one = (z2 - z) - (y3 - y)
        flux_two = (x3 - x) - (z1 - z)
        flux_three = (y1 - y) - (x2 - x)
        return flux_one * flux_one + flux_two * flux_two + flux_three * flux_three

    return tiles.each(square, ax, ay, az, ay_first, az_first, ax_second, az_second, ax_third, ay_third)


def reluctivity(tiles, flux_sq, base, slope_of, slope_total, incremental):
    doubled = tiles.each(lambda value: value * (1.0 / soft_width), flux_sq)
    excess = tiles.each(lambda value: jnp.maximum(value - CAP, 0.0), doubled)
    floor = tiles.each(lambda value: jnp.exp(-value), excess)
    rising = tiles.each(lambda value: jnp.exp(jnp.minimum(value, CAP)), doubled)
    nu = tiles.each(lambda start, slope, value: start + slope * value, base, slope_total, excess)
    slope_sum = None
    for knot in range(KNOTS):
        factor = math.exp(-knot_step * knot / soft_width)
        slope = slope_of(knot)
        high = tiles.each(lambda value: value * factor, rising)
        both = tiles.each(lambda one, other: one + other, high, floor)
        nu = tiles.each(lambda so_far, weight, value: so_far + weight * jnp.log(value), nu, slope, both)
        if incremental:
            part = tiles.each(lambda weight, one, other: weight * (one / other), slope, high, both)
            slope_sum = tiles.each(lambda one, other: one + other, slope_sum, part) if knot else part
    if incremental:
        nu = tiles.each(lambda value, s, slope: value + (2.0 / soft_width) * (s * slope), nu, flux_sq, slope_sum)
    return nu


def loop_in_pairs(count, body):
    def step(at, carry):
        body(2 * at)
        body(2 * at + 1)
        return carry

    lax.fori_loop(0, count // 2, step, 0)
    if count % 2:
        body(count - 1)


LOW_SIZE = 3 * (A_LOW[0] + S_LOW) + G_LOW
HIGH_SIZE = 3 * (A_HIGH[0] + S_HIGH) + G_HIGH


def edge_parts(planes, low):
    halo_of = ((A_LOW if low else A_HIGH)[0], S_LOW if low else S_HIGH, G_LOW if low else G_HIGH)
    at, parts = 0, []
    for array in range(7):
        halo = halo_of[0 if array < 3 else 1 if array < 6 else 2]
        parts.append((array * planes + (planes - halo if low else 0), at, halo))
        at += halo
    return parts


def write_edge(target, whole, low):
    for first, at, halo in edge_parts(whole.shape[0] // 7, low):
        target[at:at + halo] = whole[first:first + halo]


def is_odd():
    return lax.rem(lax.axis_index("mesh"), 2) == 1


def pack_kernel(start, source, region, whole, apart, marks, sems):
    planes = region.shape[0]
    copies = [pltpu.make_async_copy(region, marks, sems.at[0])]
    for part in range(3):
        for at, origin in ((part, start), (3 + part, source)):
            target = whole.at[at * planes:(at + 1) * planes]
            copies.append(pltpu.make_async_copy(origin.at[part], target, sems.at[at + 1]))
    for copy in copies:
        copy.start()
    for copy in copies:
        copy.wait()
    whole[6 * planes:] = marks[...].astype(jnp.float32)
    for odd in (False, True):
        pl.when(is_odd() == odd)(functools.partial(write_edge, apart, whole, odd))


def pair_kernel(*refs):
    wholes, paired = refs[:-2], refs[-1]
    for odd in (False, True):

        @pl.when(is_odd() == odd)
        def write():
            for turn, whole in enumerate(wholes):
                write_edge(paired.at[turn], whole, not odd)


def hold_kernel(apart, paired, after, apart_out, paired_out):
    pass


def ripple_pack_kernel(start, source, apart, paired, sems):
    planes = start.shape[3]
    odd = is_odd()
    copies = []
    for at, (target, top) in enumerate(((apart, odd), (paired, jnp.logical_not(odd)))):
        first = jnp.where(top, planes - 2, 0)
        copies.append(
            pltpu.make_async_copy(start.at[:, :, :, pl.ds(first, 2)], target.at[:, :, :, 0:2], sems.at[2 * at])
        )
        first = jnp.where(top, planes - 1, 0)
        copies.append(
            pltpu.make_async_copy(source.at[:, :, :, pl.ds(first, 1)], target.at[:, :, :, 2:3], sems.at[2 * at + 1])
        )
    for copy in copies:
        copy.start()
    for copy in copies:
        copy.wait()


def bias_kernel(shares, meshes, *refs):
    wholes, aparts, paired = refs[:shares], refs[shares:2 * shares], refs[2 * shares]
    table_index, bh_base, bh_slope, conductivity, field_out, nud_out, sigma_out = refs[2 * shares + 1:2 * shares + 8]
    a0, a1, src, marks, nu, slopes, bases = refs[2 * shares + 8:]
    planes = wholes[0].shape[0] // 7
    rows_each, lanes = wholes[0].shape[1:]
    rows = rows_each * shares
    mine = lax.axis_index("harm")
    here = lax.axis_index("mesh")
    arrays = [(a0.at[part], A_LOW[0]) for part in range(3)]
    arrays += [(src.at[part], S_LOW) for part in range(3)] + [(marks, G_LOW)]
    for turn in range(shares):
        owner = lax.rem(mine + shares - turn, shares)
        at = pl.ds(pl.multiple_of(owner * rows_each, rows_each), rows_each)

        def fill(low, high):
            for (target, onto), (unused, first, halo) in zip(arrays, edge_parts(planes, True)):
                target[0:halo, at, :] = low[first:first + halo]
            for (target, onto), (unused, first, halo) in zip(arrays, edge_parts(planes, False)):
                target[onto + planes:onto + planes + halo, at, :] = high[first:first + halo]

        for number, (target, onto) in enumerate(arrays):
            target[onto:onto + planes, at, :] = wholes[turn][number * planes:(number + 1) * planes]
        pl.when(is_odd())(functools.partial(fill, paired.at[turn], aparts[turn]))
        pl.when(jnp.logical_not(is_odd()))(functools.partial(fill, aparts[turn], paired.at[turn]))

    tiles = Tiles(rows, lanes)
    tables = [table_index[member] for member in range(MATS)]
    base_of = [bh_base[table] for table in tables]
    slope_of = [[soft_width * bh_slope[table, knot] for table in tables] for knot in range(KNOTS)]
    sigma_of = [conductivity[member] for member in range(MATS)]

    def inside(plane):
        low_ok = jnp.logical_or(plane >= 0, here > 0)
        high_ok = jnp.logical_or(plane < planes, here < meshes - 1)
        return jnp.where(jnp.logical_and(low_ok, high_ok), 1.0, 0.0)

    def choose(marks_are, values):
        def one(*marked):
            chosen = jnp.where(marked[0], values[1], values[0])
            for member in range(2, MATS):
                chosen = jnp.where(marked[member - 1], values[member], chosen)
            return chosen

        return tiles.each(one, *marks_are)

    def members(mark):
        return [tiles.each(lambda value: value == float(member), mark) for member in range(1, MATS)]

    def relax_into(target, step, old):
        def body(at):
            plane = at - A_LOW[step]
            near = at + 1
            weights, total = double_couplings(
                tiles, tiles.load(nu, near), tiles.load(nu, near + 1), tiles.load(nu, near - 1)
            )
            keep = inside(plane)
            scale = tiles.each(lambda value: keep / value, total)
            from_old = plane + A_LOW[step - 1]
            for part in range(3):
                twice = tiles.each(lambda value: value + value, tiles.load(src, part, plane + S_LOW))
                near_old = [tiles.load(old, part, from_old + move) for move in (0, 1, -1)]
                moved = pull(tiles, twice, weights, *near_old)
                tiles.store(target, (part, at), tiles.each(lambda value, by: value * by, moved, scale))

        loop_in_pairs(planes + A_LOW[step] + A_HIGH[step], body)

    def first_nu(at):
        marked = members(tiles.load(marks, at))
        base, slope = choose(marked, base_of), [choose(marked, slope_of[knot]) for knot in range(KNOTS)]
        whole_slope = slope[0]
        tiles.store(bases, (at,), base)
        for knot in range(KNOTS):
            tiles.store(slopes, (knot, at), slope[knot])
            if knot:
                whole_slope = tiles.each(lambda one, other: one + other, whole_slope, slope[knot])
        tiles.store(slopes, (KNOTS, at), whole_slope)
        value = reluctivity(tiles, flux_squared(tiles, a0, at), base, lambda knot: slope[knot], whole_slope, False)
        keep = inside(at - G_LOW)
        tiles.store(nu, (at,), tiles.each(lambda one: one * keep, value))

    loop_in_pairs(planes + G_LOW + G_HIGH, first_nu)
    fields = (a0, a1)
    for step in range(1, ITERS_B + 1):
        old, new = fields[(step - 1) % 2], fields[step % 2]
        relax_into(new, step, old)
        last = step == ITERS_B
        lower = NUD_LOW if last else A_LOW[step + 1] + 1
        upper = NUD_HIGH if last else A_HIGH[step + 1] + 1

        def next_nu(at):
            plane = at - lower
            known = plane + G_LOW
            value = reluctivity(
                tiles, flux_squared(tiles, new, plane + A_LOW[step]), tiles.load(bases, known),
                lambda knot: tiles.load(slopes, knot, known), tiles.load(slopes, KNOTS, known), last,
            )
            keep = inside(plane)
            tiles.store(nud_out if last else nu, (at,), tiles.each(lambda one: one * keep, value))

        loop_in_pairs(planes + lower + upper, next_nu)

    def sigma_at(at):
        marked = members(tiles.load(marks, at - (ITERS_R - 1) + G_LOW))
        tiles.store(sigma_out, (at,), choose(marked, sigma_of))

    loop_in_pairs(planes + 2 * (ITERS_R - 1), sigma_at)
    own_rows = pl.ds(pl.multiple_of(mine * rows_each, rows_each), rows_each)
    final = fields[ITERS_B % 2]
    for part in range(3):
        field_out[part] = final[part, A_LOW[ITERS_B]:A_LOW[ITERS_B] + planes, own_rows, :]


def ripple_kernel(shares, meshes, harmonic_numbers, nud, sigma, start, source, apart, paired, ripple_out, *refs):
    losses, (r0, r1, r2, src, loss, faces, sides, answer, r_sems, s_sems, out_sems) = refs[:shares], refs[shares:]
    count, planes = start.shape[0], start.shape[3]
    rows, lanes = start.shape[4:]
    mine = lax.axis_index("harm")
    here = lax.axis_index("mesh")
    top = planes + 2

    def fetch(origin, first, target, onto, sems):
        return pltpu.make_async_copy(
            origin.at[:, :, :, pl.ds(first, 1)], target.at[:, :, :, pl.ds(onto, 1)], sems.at[onto]
        )

    odd = is_odd()
    for origin, above in ((apart, odd), (paired, jnp.logical_not(odd))):
        onto = jnp.where(above, top, 0)
        for plane in range(2):
            fetch(origin, plane, r0, onto + plane, r_sems).start()
        fetch(origin, 2, src, jnp.where(above, planes + 1, 0), s_sems).start()
    for plane in range(planes):
        fetch(start, plane, r0, plane + 2, r_sems).start()
        fetch(source, plane, src, plane + 1, s_sems).start()
    def drain(plane):
        return pltpu.make_async_copy(
            r2.at[:, :, :, pl.ds(plane, 1)], ripple_out.at[:, :, :, pl.ds(plane, 1)], out_sems.at[plane]
        )

    tiles = Tiles(rows, lanes)
    omegas = [omega_step * harmonic_numbers[mine * count + harmonic].astype(jnp.float32) for harmonic in range(count)]

    def prepare(at):
        plane = at - 1
        near = plane + NUD_LOW
        weights, total = double_couplings(
            tiles, tiles.load(nud, near), tiles.load(nud, near + 1), tiles.load(nud, near - 1)
        )
        half = [tiles.each(lambda value: 0.5 * value, weight) for weight in weights]
        tiles.store(faces, (at + 1,), half[0])
        tiles.store(faces, (at,), half[1])
        for number in range(4):
            tiles.store(sides, (number, at), half[2 + number])
        low_ok = jnp.logical_or(plane >= 0, here > 0)
        high_ok = jnp.logical_or(plane < planes, here < meshes - 1)
        keep = jnp.where(jnp.logical_and(low_ok, high_ok), 1.0, 0.0)
        total = tiles.each(lambda value: 0.5 * value, total)
        square = tiles.each(lambda value: value * value, total)
        conduct = tiles.load(sigma, at)
        for harmonic in range(count):
            damp = tiles.each(lambda value: omegas[harmonic] * value, conduct)
            inverse = tiles.each(lambda one, other: keep / (one + other * other), square, damp)
            tiles.store(answer, (harmonic, 0, at), tiles.each(lambda one, other: one * other, total, inverse))
            tiles.store(answer, (harmonic, 1, at), tiles.each(lambda one, other: one * other, damp, inverse))

    loop_in_pairs(planes + 2, prepare)

    def sweep(old, offset, plane, store):
        at = plane + 1
        weights = [tiles.load(faces, at + 1), tiles.load(faces, at)]
        weights += [tiles.load(sides, number, at) for number in range(4)]
        for harmonic in range(count):
            straight, turned = tiles.load(answer, harmonic, 0, at), tiles.load(answer, harmonic, 1, at)
            power = None
            for part in range(3):
                both = []
                for piece in range(2):
                    near_old = [tiles.load(old, harmonic, piece, part, plane + offset + move) for move in (0, 1, -1)]
                    both.append(pull(tiles, tiles.load(src, harmonic, piece, part, at), weights, *near_old))
                real = tiles.each(lambda re, im, a, b: re * a + im * b, *both, straight, turned)
                imag = tiles.each(lambda re, im, a, b: im * a - re * b, *both, straight, turned)
                store(harmonic, part, real, imag)
                squared = tiles.each(lambda re, im: re * re + im * im, real, imag)
                power = tiles.each(lambda one, other: one + other, power, squared) if part else squared
            yield harmonic, power

    for plane in range(2):
        fetch(start, 0, r0, plane, r_sems).wait()

    def first(at, carry):
        fetch(start, 0, r0, at + 2, r_sems).wait()
        fetch(start, 0, src, at, s_sems).wait()

        def store(harmonic, part, real, imag):
            tiles.store(r1, (harmonic, 0, part, at), real)
            tiles.store(r1, (harmonic, 1, part, at), imag)

        for unused in sweep(r0, 2, at - 1, store):
            pass
        return carry

    lax.fori_loop(0, planes + 2, first, 0)

    def second(plane, carry):
        def store(harmonic, part, real, imag):
            tiles.store(r2, (harmonic, 0, part, plane), real)
            tiles.store(r2, (harmonic, 1, part, plane), imag)

        summed = None
        for harmonic, power in sweep(r1, 1, plane, store):
            factor = 0.5 * omegas[harmonic] * omegas[harmonic]
            scaled = tiles.each(lambda value: factor * value, power)
            summed = tiles.each(lambda one, other: one + other, summed, scaled) if harmonic else scaled
        conduct = tiles.load(sigma, plane + 1)
        tiles.store(loss, (plane,), tiles.each(lambda one, other: one * other, conduct, summed))
        drain(plane).start()
        return carry

    lax.fori_loop(0, planes, second, 0)
    rows_each = rows // shares
    for turn in range(shares):
        owner = lax.rem(mine + turn, shares)
        losses[turn][...] = loss[:, pl.ds(pl.multiple_of(owner * rows_each, rows_each), rows_each), :]
    for plane in range(planes):
        drain(plane).wait()


def call(kernel, operands, in_specs, out_shapes, out_specs, scratch, name, work=0, aliases={}, room=0):
    f32 = jnp.float32
    shapes = [o.shape for o, spec in zip(operands, in_specs) if spec is VMEM]
    shapes += [shape for shape, spec in zip(out_shapes, out_specs) if spec is VMEM]
    shapes += [shape for shape in scratch if isinstance(shape, tuple)]
    held = 4 * sum(math.prod(shape) for shape in shapes)
    return pl.pallas_call(
        kernel,
        out_shape=[jax.ShapeDtypeStruct(shape, f32) for shape in out_shapes],
        in_specs=in_specs,
        out_specs=out_specs,
        scratch_shapes=[pltpu.VMEM(shape, f32) if isinstance(shape, tuple) else shape for shape in scratch],
        compiler_params=pltpu.CompilerParams(vmem_limit_bytes=room or held + 6 * 2**20),
        cost_estimate=pl.CostEstimate(flops=work * 300, bytes_accessed=work, transcendentals=0),
        input_output_aliases=aliases,
        name=name,
    )(*operands)


def body(
    meshes, shares, bias_source, bias_start, region, table_index, bh_base, bh_slope, conductivity, harmonic_numbers,
    ripple_source, ripple_start,
):
    unused, planes, rows_each, lanes = bias_start.shape
    rows = rows_each * shares
    count = ripple_start.shape[0]
    near = [(i, i + 1) for i in range(0, meshes - 1, 2)]
    far = [(i, i + 1) for i in range(1, meshes - 1, 2)]
    near += [(j, i) for i, j in near]
    far += [(j, i) for i, j in far]
    turned = [[(i, (i + turn) % shares) for i in range(shares)] for turn in range(1, shares)]

    def around(block):
        return [block] + [lax.ppermute(block, "harm", pairs) for pairs in turned]

    whole, apart = call(
        pack_kernel, (bias_start, bias_source, region), [ANY] * 3,
        [(7 * planes, rows_each, lanes), (HIGH_SIZE, rows_each, lanes)], [VMEM] * 2,
        [pltpu.VMEM(region.shape, region.dtype), pltpu.SemaphoreType.DMA((7,))], "pack", room=PACK_ROOM,
    )
    wholes = around(whole)
    aparts = around(lax.ppermute(apart, "mesh", far))
    edge = ripple_start.shape[:3] + (3, rows, lanes)
    ripple_apart, ripple_paired = call(
        ripple_pack_kernel, (ripple_start, ripple_source), [ANY] * 2, [edge, edge], [VMEM] * 2,
        [pltpu.SemaphoreType.DMA((4,))], "ripple_pack", RP_WORK, room=RP_ROOM,
    )
    paired, = call(
        pair_kernel, (*wholes, ripple_apart), [VMEM] * shares + [ANY], [(shares, HIGH_SIZE, rows_each, lanes)], [VMEM], [], "pair"
    )
    paired = lax.ppermute(paired, "mesh", near)

    ripple_apart, ripple_paired = call(
        hold_kernel, (ripple_apart, ripple_paired, aparts[0]), [ANY] * 3, [edge, edge], [ANY] * 2, [], "hold",
        HOLD_WORK, {0: 0, 1: 1},
    )
    ripple_apart = lax.ppermute(ripple_apart, "mesh", far)
    ripple_paired = lax.ppermute(ripple_paired, "mesh", near)

    known = (planes + G_LOW + G_HIGH, rows, lanes)
    field, nud, sigma = call(
        functools.partial(bias_kernel, shares, meshes),
        (*wholes, *aparts, paired, table_index, bh_base, bh_slope, conductivity),
        [VMEM] * (2 * shares + 1) + [SMEM] * 4,
        [
            bias_start.shape, (planes + NUD_LOW + NUD_HIGH, rows, lanes), (planes + 2 * (ITERS_R - 1), rows, lanes)
        ],
        [VMEM] * 3,
        [
            (3, planes + A_LOW[0] + A_HIGH[0], rows, lanes),
            (3, planes + A_LOW[1] + A_HIGH[1], rows, lanes),
            (3, planes + S_LOW + S_HIGH, rows, lanes),
            known,
            known,
            (KNOTS + 1, *known),
            known,
        ],
        "bias",
        BIAS_WORK,
    )

    ripple, *losses = call(
        functools.partial(ripple_kernel, shares, meshes),
        (harmonic_numbers, nud, sigma, ripple_start, ripple_source, ripple_apart, ripple_paired),
        [SMEM, VMEM, VMEM] + [ANY] * 4,
        [ripple_start.shape] + [(planes, rows_each, lanes)] * shares,
        [ANY] + [VMEM] * shares,
        [
            (count, 2, 3, planes + 4, rows, lanes),
            (count, 2, 3, planes + 2, rows, lanes),
            (count, 2, 3, planes, rows, lanes),
            (count, 2, 3, planes + 2, rows, lanes),
            (planes, rows, lanes),
            (planes + 3, rows, lanes),
            (4, planes + 2, rows, lanes),
            (count, 2, planes + 2, rows, lanes),
            pltpu.SemaphoreType.DMA((planes + 4,)),
            pltpu.SemaphoreType.DMA((planes + 2,)),
            pltpu.SemaphoreType.DMA((planes,)),
        ],
        "ripple",
        room=RIPPLE_ROOM,
    )
    loss = losses[0]
    for turn, pairs in enumerate(turned):
        loss = loss + lax.ppermute(losses[turn + 1], "harm", pairs)
    return field, ripple, loss


def solution(mesh):
    return jax.shard_map(
        functools.partial(body, mesh.shape["mesh"], mesh.shape["harm"]),
        mesh=mesh,
        in_specs=(
            P(None, "mesh", "harm", None),
            P(None, "mesh", "harm", None),
            P("mesh", "harm", None),
            P(),
            P(),
            P(),
            P(),
            P(),
            P("harm", None, None, "mesh", None, None),
            P("harm", None, None, "mesh", None, None),
        ),
        out_specs=(
            P(None, "mesh", "harm", None),
            P("harm", None, None, "mesh", None, None),
            P("mesh", "harm", None),
        ),
        check_vma=False,
    )
```

```python
import functools
import math

import jax
import jax.numpy as jnp
from jax import lax
from jax.experimental import pallas as pl
from jax.experimental.pallas import tpu as pltpu
from jax.sharding import PartitionSpec as P

ITERS_B = 2
ITERS_R = 2
KNOTS = 8
MATS = 4

kappa = 0.05
knot_step = 1.5
soft_width = 0.5
omega_step = 0.25
CAP = 80.0

NUD_LOW, NUD_HIGH = ITERS_R, ITERS_R
A_LOW = [NUD_LOW + ITERS_B - step for step in range(ITERS_B + 1)]
A_HIGH = [NUD_HIGH + 1 + 2 * (ITERS_B - step) for step in range(ITERS_B + 1)]
S_LOW, S_HIGH = A_LOW[1], A_HIGH[1]
G_LOW, G_HIGH = A_LOW[0], A_HIGH[0] - 1

BIAS_WORK = 20000000
PACK_ROOM = 62 * 2**20
RP_ROOM = 58 * 2**20
VMEM = pl.BlockSpec(memory_space=pltpu.VMEM)
SMEM = pl.BlockSpec(memory_space=pltpu.SMEM)
ANY = pl.BlockSpec(memory_space=pl.ANY)


TILE = (8, 128)


class Tiles:
    def __init__(self, rows, lanes):
        self.grid = (rows // TILE[0], lanes // TILE[1])
        self.spots = [(i, j) for i in range(self.grid[0]) for j in range(self.grid[1])]
        self.at_end, self.at_start = [], []
        for axis in range(2):
            place = lax.broadcasted_iota(jnp.int32, TILE, axis)
            self.at_end.append(place == TILE[axis] - 1)
            self.at_start.append(place == 0)

    def where(self, spot):
        return (slice(spot[0] * TILE[0], (spot[0] + 1) * TILE[0]), slice(spot[1] * TILE[1], (spot[1] + 1) * TILE[1]))

    def load(self, ref, *lead):
        return {spot: ref[lead + self.where(spot)] for spot in self.spots}

    def store(self, ref, lead, values):
        for spot in self.spots:
            ref[lead + self.where(spot)] = values[spot]

    def each(self, function, *values):
        return {spot: function(*(value[spot] for value in values)) for spot in self.spots}

    def side(self, step, axis):
        return (self.at_end if step > 0 else self.at_start)[axis]

    def is_edge(self, spot, step, axis):
        return spot[axis] == (self.grid[axis] - 1 if step > 0 else 0)

    def move(self, values, step, axis, fill):
        rolled = self.each(lambda tile: pltpu.roll(tile, TILE[axis] - 1 if step > 0 else 1, axis), values)
        side, moved = self.side(step, axis), {}
        for spot in self.spots:
            if self.is_edge(spot, step, axis):
                moved[spot] = jnp.where(side, 0.0, rolled[spot]) if fill else rolled[spot]
            else:
                other = (spot[0] + step, spot[1]) if axis == 0 else (spot[0], spot[1] + step)
                moved[spot] = jnp.where(side, rolled[other], rolled[spot])
        return moved

    def inner(self, values, step, axis):
        side = self.side(step, axis)
        return {
            spot: jnp.where(side, 0.0, values[spot]) if self.is_edge(spot, step, axis) else values[spot]
            for spot in self.spots
        }


SIDES = ((1, 0), (-1, 0), (1, 1), (-1, 1))


def double_couplings(tiles, center, above, below):
    add = lambda one, other: one + other
    weights = [tiles.each(add, center, above), tiles.each(add, center, below)]
    total = tiles.each(add, *weights)
    for step, axis in SIDES:
        weight = tiles.each(add, center, tiles.move(center, step, axis, True))
        total = tiles.each(add, total, weight)
        weights.append(tiles.inner(weight, step, axis))
    return weights, tiles.each(lambda value: value + 2.0 * kappa, total)


def pull(tiles, start, weights, center, above, below):
    moved = [above, below] + [tiles.move(center, step, axis, False) for step, axis in SIDES]
    total = start
    for weight, other in zip(weights, moved):
        total = tiles.each(lambda so_far, w, value: so_far + w * value, total, weight, other)
    return total


def flux_squared(tiles, field, plane):
    ax, ay, az = (tiles.load(field, part, plane) for part in range(3))
    ay_first, az_first = tiles.load(field, 1, plane + 1), tiles.load(field, 2, plane + 1)
    ax_second, az_second = tiles.move(ax, 1, 0, True), tiles.move(az, 1, 0, True)
    ax_third, ay_third = tiles.move(ax, 1, 1, True), tiles.move(ay, 1, 1, True)

    def square(x, y, z, y1, z1, x2, z2, x3, y3):
        flux_one = (z2 - z) - (y3 - y)
        flux_two = (x3 - x) - (z1 - z)
        flux_three = (y1 - y) - (x2 - x)
        return flux_one * flux_one + flux_two * flux_two + flux_three * flux_three

    return tiles.each(square, ax, ay, az, ay_first, az_first, ax_second, az_second, ax_third, ay_third)


def reluctivity(tiles, flux_sq, base, slope_of, slope_total, incremental):
    doubled = tiles.each(lambda value: value * (1.0 / soft_width), flux_sq)
    excess = tiles.each(lambda value: jnp.maximum(value - CAP, 0.0), doubled)
    floor = tiles.each(lambda value: jnp.exp(-value), excess)
    rising = tiles.each(lambda value: jnp.exp(jnp.minimum(value, CAP)), doubled)
    nu = tiles.each(lambda start, slope, value: start + slope * value, base, slope_total, excess)
    slope_sum = None
    for knot in range(KNOTS):
        factor = math.exp(-knot_step * knot / soft_width)
        slope = slope_of(knot)
        high = tiles.each(lambda value: value * factor, rising)
        both = tiles.each(lambda one, other: one + other, high, floor)
        nu = tiles.each(lambda so_far, weight, value: so_far + weight * jnp.log(value), nu, slope, both)
        if incremental:
            part = tiles.each(lambda weight, one, other: weight * (one / other), slope, high, both)
            slope_sum = tiles.each(lambda one, other: one + other, slope_sum, part) if knot else part
    if incremental:
        nu = tiles.each(lambda value, s, slope: value + (2.0 / soft_width) * (s * slope), nu, flux_sq, slope_sum)
    return nu


def loop_in_pairs(count, body):
    def step(at, carry):
        body(2 * at)
        body(2 * at + 1)
        return carry

    lax.fori_loop(0, count // 2, step, 0)
    if count % 2:
        body(count - 1)


LOW_SIZE = 3 * (A_LOW[0] + S_LOW) + G_LOW
HIGH_SIZE = 3 * (A_HIGH[0] + S_HIGH) + G_HIGH


def edge_parts(planes, low):
    halo_of = ((A_LOW if low else A_HIGH)[0], S_LOW if low else S_HIGH, G_LOW if low else G_HIGH)
    at, parts = 0, []
    for array in range(7):
        halo = halo_of[0 if array < 3 else 1 if array < 6 else 2]
        parts.append((array * planes + (planes - halo if low else 0), at, halo))
        at += halo
    return parts


def write_edge(target, whole, low):
    for first, at, halo in edge_parts(whole.shape[0] // 7, low):
        target[at:at + halo] = whole[first:first + halo]


def is_odd():
    return lax.rem(lax.axis_index("mesh"), 2) == 1


def pack_kernel(start, source, region, whole, apart, paired, token, marks, sems):
    token[...] = jnp.zeros(token.shape, token.dtype)
    planes = region.shape[0]
    copies = [pltpu.make_async_copy(region, marks, sems.at[0])]
    for part in range(3):
        for at, origin in ((part, start), (3 + part, source)):
            target = whole.at[at * planes:(at + 1) * planes]
            copies.append(pltpu.make_async_copy(origin.at[part], target, sems.at[at + 1]))
    for copy in copies:
        copy.start()
    for copy in copies:
        copy.wait()
    whole[6 * planes:] = marks[...].astype(jnp.float32)
    for odd in (False, True):
        pl.when(is_odd() == odd)(functools.partial(write_edge, apart, whole, odd))
        pl.when(is_odd() == odd)(functools.partial(write_edge, paired, whole, not odd))


def pair_kernel(*refs):
    wholes, paired = refs[:-2], refs[-1]
    for odd in (False, True):

        @pl.when(is_odd() == odd)
        def write():
            for turn, whole in enumerate(wholes):
                write_edge(paired.at[turn], whole, not odd)


def is_second():
    return lax.rem(lax.axis_index("mesh") + 1, 4) < 2


def edge_copies(start, source, buffer, target, top, sems):
    planes = start.shape[3]
    ways_in = []
    for part, (origin, count, onto) in enumerate(((start, 2, 0), (source, 1, 2))):
        at = jnp.where(top, planes - count, 0)
        ways_in.append(
            pltpu.make_async_copy(planes_of(origin, at, count), planes_of(buffer, onto, count), sems.at[part])
        )
        ways_in[-1].start()
    return ways_in, pltpu.make_async_copy(buffer, target, sems.at[2])


def first_edges_kernel(start, source, after, apart, paired, token, buffers, sems):
    token[...] = jnp.zeros(token.shape, token.dtype)
    odd = is_odd()
    ways_in, way_out = edge_copies(start, source, buffers.at[1], paired, jnp.logical_not(odd), sems.at[1])

    @pl.when(jnp.logical_not(is_second()))
    def send_apart():
        apart_in, apart_out = edge_copies(start, source, buffers.at[0], apart, odd, sems.at[0])
        for copy in apart_in:
            copy.wait()
        apart_out.start()
        apart_out.wait()

    for copy in ways_in:
        copy.wait()
    way_out.start()
    way_out.wait()


def second_edges_kernel(start, source, after, apart, buffer, sems):
    @pl.when(is_second())
    def send_apart():
        apart_in, apart_out = edge_copies(start, source, buffer, apart, is_odd(), sems)
        for copy in apart_in:
            copy.wait()
        apart_out.start()
        apart_out.wait()


def bias_kernel(shares, meshes, *refs):
    wholes, aparts, (paired, others) = refs[:shares], refs[shares:2 * shares], refs[2 * shares:2 * shares + 2]
    paireds = [paired] + [others.at[at] for at in range(shares - 1)]
    table_index, bh_base, bh_slope, conductivity, field_out, nud_out, sigma_out = refs[2 * shares + 2:2 * shares + 9]
    a0, a1, src, marks, nu, slopes, bases = refs[2 * shares + 9:]
    planes = wholes[0].shape[0] // 7
    rows_each, lanes = wholes[0].shape[1:]
    rows = rows_each * shares
    mine = lax.axis_index("harm")
    here = lax.axis_index("mesh")
    arrays = [(a0.at[part], A_LOW[0]) for part in range(3)]
    arrays += [(src.at[part], S_LOW) for part in range(3)] + [(marks, G_LOW)]
    for turn in range(shares):
        owner = lax.rem(mine + shares - turn, shares)
        at = pl.ds(pl.multiple_of(owner * rows_each, rows_each), rows_each)

        def fill(low, high):
            for (target, onto), (unused, first, halo) in zip(arrays, edge_parts(planes, True)):
                target[0:halo, at, :] = low[first:first + halo]
            for (target, onto), (unused, first, halo) in zip(arrays, edge_parts(planes, False)):
                target[onto + planes:onto + planes + halo, at, :] = high[first:first + halo]

        for number, (target, onto) in enumerate(arrays):
            target[onto:onto + planes, at, :] = wholes[turn][number * planes:(number + 1) * planes]
        pl.when(is_odd())(functools.partial(fill, paireds[turn], aparts[turn]))
        pl.when(jnp.logical_not(is_odd()))(functools.partial(fill, aparts[turn], paireds[turn]))

    tiles = Tiles(rows, lanes)
    tables = [table_index[member] for member in range(MATS)]
    base_of = [bh_base[table] for table in tables]
    slope_of = [[soft_width * bh_slope[table, knot] for table in tables] for knot in range(KNOTS)]
    sigma_of = [conductivity[member] for member in range(MATS)]

    def inside(plane):
        low_ok = jnp.logical_or(plane >= 0, here > 0)
        high_ok = jnp.logical_or(plane < planes, here < meshes - 1)
        return jnp.where(jnp.logical_and(low_ok, high_ok), 1.0, 0.0)

    def choose(marks_are, values):
        def one(*marked):
            chosen = jnp.where(marked[0], values[1], values[0])
            for member in range(2, MATS):
                chosen = jnp.where(marked[member - 1], values[member], chosen)
            return chosen

        return tiles.each(one, *marks_are)

    def members(mark):
        return [tiles.each(lambda value: value == float(member), mark) for member in range(1, MATS)]

    def relax_into(target, step, old):
        def body(at):
            plane = at - A_LOW[step]
            near = at + 1
            weights, total = double_couplings(
                tiles, tiles.load(nu, near), tiles.load(nu, near + 1), tiles.load(nu, near - 1)
            )
            keep = inside(plane)
            scale = tiles.each(lambda value: keep / value, total)
            from_old = plane + A_LOW[step - 1]
            for part in range(3):
                twice = tiles.each(lambda value: value + value, tiles.load(src, part, plane + S_LOW))
                near_old = [tiles.load(old, part, from_old + move) for move in (0, 1, -1)]
                moved = pull(tiles, twice, weights, *near_old)
                tiles.store(target, (part, at), tiles.each(lambda value, by: value * by, moved, scale))

        loop_in_pairs(planes + A_LOW[step] + A_HIGH[step], body)

    def first_nu(at):
        marked = members(tiles.load(marks, at))
        base, slope = choose(marked, base_of), [choose(marked, slope_of[knot]) for knot in range(KNOTS)]
        whole_slope = slope[0]
        tiles.store(bases, (at,), base)
        for knot in range(KNOTS):
            tiles.store(slopes, (knot, at), slope[knot])
            if knot:
                whole_slope = tiles.each(lambda one, other: one + other, whole_slope, slope[knot])
        tiles.store(slopes, (KNOTS, at), whole_slope)
        value = reluctivity(tiles, flux_squared(tiles, a0, at), base, lambda knot: slope[knot], whole_slope, False)
        keep = inside(at - G_LOW)
        tiles.store(nu, (at,), tiles.each(lambda one: one * keep, value))

    loop_in_pairs(planes + G_LOW + G_HIGH, first_nu)
    fields = (a0, a1)
    for step in range(1, ITERS_B + 1):
        old, new = fields[(step - 1) % 2], fields[step % 2]
        relax_into(new, step, old)
        last = step == ITERS_B
        lower = NUD_LOW if last else A_LOW[step + 1] + 1
        upper = NUD_HIGH if last else A_HIGH[step + 1] + 1

        def next_nu(at):
            plane = at - lower
            known = plane + G_LOW
            value = reluctivity(
                tiles, flux_squared(tiles, new, plane + A_LOW[step]), tiles.load(bases, known),
                lambda knot: tiles.load(slopes, knot, known), tiles.load(slopes, KNOTS, known), last,
            )
            keep = inside(plane)
            tiles.store(nud_out if last else nu, (at,), tiles.each(lambda one: one * keep, value))

        loop_in_pairs(planes + lower + upper, next_nu)

    def sigma_at(at):
        marked = members(tiles.load(marks, at - (ITERS_R - 1) + G_LOW))
        tiles.store(sigma_out, (at,), choose(marked, sigma_of))

    loop_in_pairs(planes + 2 * (ITERS_R - 1), sigma_at)
    own_rows = pl.ds(pl.multiple_of(mine * rows_each, rows_each), rows_each)
    final = fields[ITERS_B % 2]
    for part in range(3):
        field_out[part] = final[part, A_LOW[ITERS_B]:A_LOW[ITERS_B] + planes, own_rows, :]


class Ripple:
    def __init__(self, count, rows, lanes, harmonic_numbers, nud, sigma, src, sides, answer):
        self.count, self.nud, self.sigma, self.src, self.sides, self.answer = count, nud, sigma, src, sides, answer
        self.tiles = Tiles(rows, lanes)
        first = lax.axis_index("harm") * count
        self.omegas = [omega_step * harmonic_numbers[first + at].astype(jnp.float32) for at in range(count)]

    def prepare(self, slot, plane, keep):
        tiles, near = self.tiles, plane + NUD_LOW
        weights, total = double_couplings(tiles, *(tiles.load(self.nud, near + move) for move in (0, 1, -1)))
        for number, weight in enumerate(weights):
            tiles.store(self.sides, (number, slot), tiles.each(lambda value: 0.5 * value, weight))
        total = tiles.each(lambda value: 0.5 * value, total)
        square = tiles.each(lambda value: value * value, total)
        conduct = tiles.load(self.sigma, plane + ITERS_R - 1)
        for harmonic in range(self.count):
            damp = tiles.each(lambda value: self.omegas[harmonic] * value, conduct)
            inverse = tiles.each(lambda one, other: keep / (one + other * other), square, damp)
            for part, value in enumerate((total, damp)):
                scaled = tiles.each(lambda one, other: one * other, value, inverse)
                tiles.store(self.answer, (harmonic, part, slot), scaled)

    def sweep(self, slot, old, center, new, onto):
        tiles = self.tiles
        weights = [tiles.load(self.sides, number, slot) for number in range(6)]
        for harmonic in range(self.count):
            straight, turned = (tiles.load(self.answer, harmonic, part, slot) for part in range(2))
            power = None
            for part in range(3):
                both = []
                for piece in range(2):
                    near_old = [tiles.load(old, harmonic, piece, part, center + move) for move in (0, 1, -1)]
                    both.append(pull(tiles, tiles.load(self.src, harmonic, piece, part, slot), weights, *near_old))
                real = tiles.each(lambda re, im, a, b: re * a + im * b, *both, straight, turned)
                imag = tiles.each(lambda re, im, a, b: im * a - re * b, *both, straight, turned)
                tiles.store(new, (harmonic, 0, part, onto), real)
                tiles.store(new, (harmonic, 1, part, onto), imag)
                squared = tiles.each(lambda re, im: re * re + im * im, real, imag)
                power = tiles.each(lambda one, other: one + other, power, squared) if part else squared
            yield harmonic, power

    def last_sweep(self, slot, old, center, new, onto, plane, loss):
        tiles, summed = self.tiles, None
        for harmonic, power in self.sweep(slot, old, center, new, onto):
            factor = 0.5 * self.omegas[harmonic] * self.omegas[harmonic]
            scaled = tiles.each(lambda value: factor * value, power)
            summed = tiles.each(lambda one, other: one + other, summed, scaled) if harmonic else scaled
        conduct = tiles.load(self.sigma, plane + ITERS_R - 1)
        tiles.store(loss, (plane,), tiles.each(lambda one, other: one * other, conduct, summed))


def planes_of(ref, first, count):
    return ref.at[:, :, :, pl.ds(first, count)]


def inner_kernel(
    harmonic_numbers, nud_in, sigma_in, start, source, ripple_out, edge_out, loss_out,
    r0, r1, r2, src, sides, answer, nud, sigma, r_sems, s_sems, out_sems, sems,
):
    count, planes = start.shape[0], start.shape[3]

    def fetch(origin, target, plane, copy_sems):
        return pltpu.make_async_copy(planes_of(origin, plane, 1), planes_of(target, plane, 1), copy_sems.at[plane])

    def drain(plane):
        return pltpu.make_async_copy(planes_of(r2, plane, 1), planes_of(ripple_out, plane, 1), out_sems.at[plane])

    fields = [pltpu.make_async_copy(nud_in, nud, sems.at[0]), pltpu.make_async_copy(sigma_in, sigma, sems.at[1])]
    for copy in fields:
        copy.start()
    for plane in range(planes):
        fetch(start, r0, plane, r_sems).start()
        if 0 < plane < planes - 1:
            fetch(source, src, plane, s_sems).start()
    ripple = Ripple(count, *start.shape[4:], harmonic_numbers, nud, sigma, src, sides, answer)
    for copy in fields:
        copy.wait()
    loop_in_pairs(planes - 2, lambda at: ripple.prepare(at + 1, at + 1, 1.0))
    for plane in range(2):
        fetch(start, r0, plane, r_sems).wait()

    def first(at, carry):
        fetch(start, r0, at + 1, r_sems).wait()
        fetch(source, src, at, s_sems).wait()
        for unused in ripple.sweep(at, r0, at, r1, at):
            pass
        return carry

    lax.fori_loop(1, planes - 1, first, 0)
    edges = [
        pltpu.make_async_copy(planes_of(r1, place, 2), planes_of(edge_out, onto, 2), sems.at[onto // 2])
        for place, onto in ((1, 0), (planes - 3, 2))
    ]
    for copy in edges:
        copy.start()

    def second(plane, carry):
        ripple.last_sweep(plane, r1, plane, r2, plane, plane, loss_out)
        drain(plane).start()
        return carry

    lax.fori_loop(2, planes - 2, second, 0)
    for copy in edges:
        copy.wait()
    for plane in range(2, planes - 2):
        drain(plane).wait()


def outer_kernel(
    shares, meshes, harmonic_numbers, nud_in, sigma_in, start, source, first_apart, second_apart, paired, edge_in,
    loss_in, ripple_in, ripple_out, *refs
):
    losses, refs = refs[:shares], refs[shares:]
    r0, r1, r2, src, sides, answer, nud, sigma, loss, sems, halo_sems = refs
    count, planes = start.shape[0], start.shape[3]
    rows, lanes = start.shape[4:]
    here = lax.axis_index("mesh")
    copies = [
        pltpu.make_async_copy(nud_in, nud, sems.at[0]),
        pltpu.make_async_copy(sigma_in, sigma, sems.at[1]),
        pltpu.make_async_copy(loss_in, loss, sems.at[2]),
        pltpu.make_async_copy(planes_of(start, 0, 2), planes_of(r0, 2, 2), sems.at[3]),
        pltpu.make_async_copy(planes_of(start, planes - 2, 2), planes_of(r0, 4, 2), sems.at[4]),
        pltpu.make_async_copy(planes_of(source, 0, 2), planes_of(src, 1, 2), sems.at[5]),
        pltpu.make_async_copy(planes_of(source, planes - 2, 2), planes_of(src, 3, 2), sems.at[6]),
        pltpu.make_async_copy(edge_in, planes_of(r1, 2, 4), sems.at[7]),
    ]
    odd = is_odd()

    def halo(origin, above, number):
        onto = jnp.where(above, 6, 0), jnp.where(above, 5, 0)
        return [
            pltpu.make_async_copy(planes_of(origin, 0, 2), planes_of(r0, onto[0], 2), halo_sems.at[number]),
            pltpu.make_async_copy(planes_of(origin, 2, 1), planes_of(src, onto[1], 1), halo_sems.at[number + 1]),
        ]

    for second, origin in ((False, first_apart), (True, second_apart)):

        @pl.when(is_second() == second)
        def apart():
            for copy in halo(origin, odd, 0):
                copy.start()

    copies += halo(paired, jnp.logical_not(odd), 2)
    for copy in copies:
        copy.start()
    copies += halo(first_apart, odd, 0)
    ripple = Ripple(count, rows, lanes, harmonic_numbers, nud, sigma, src, sides, answer)
    for copy in copies[:2]:
        copy.wait()

    def prepare(slot):
        plane = jnp.where(slot < 3, slot - 1, planes - 5 + slot)
        low_ok = jnp.logical_or(plane >= 0, here > 0)
        high_ok = jnp.logical_or(plane < planes, here < meshes - 1)
        ripple.prepare(slot, plane, jnp.where(jnp.logical_and(low_ok, high_ok), 1.0, 0.0))

    loop_in_pairs(6, prepare)
    for copy in copies[2:]:
        copy.wait()

    def first(at, carry):
        high = at // 2
        for unused in ripple.sweep(at + 2 * high, r0, at + 1 + 2 * high, r1, at + 4 * high):
            pass
        return carry

    lax.fori_loop(0, 4, first, 0)

    def drain(at, plane):
        return pltpu.make_async_copy(planes_of(r2, at, 1), planes_of(ripple_out, plane, 1), sems.at[at])

    def second(at, carry):
        high = at // 2
        plane = jnp.where(at < 2, at, planes - 4 + at)
        ripple.last_sweep(at + 1, r1, at + 1 + 2 * high, r2, at, plane, loss)
        drain(at, plane).start()
        return carry

    lax.fori_loop(0, 4, second, 0)
    rows_each = rows // shares
    for turn in range(shares):
        owner = lax.rem(lax.axis_index("harm") + turn, shares)
        losses[turn][...] = loss[:, pl.ds(pl.multiple_of(owner * rows_each, rows_each), rows_each), :]
    for at in range(4):
        drain(at, 0).wait()


def call(kernel, operands, in_specs, out_shapes, out_specs, scratch, name, work=0, aliases={}, room=0):
    f32 = jnp.float32
    shapes = [o.shape for o, spec in zip(operands, in_specs) if spec is VMEM]
    shapes += [shape for shape, spec in zip(out_shapes, out_specs) if spec is VMEM]
    shapes += [shape for shape in scratch if isinstance(shape, tuple)]
    held = 4 * sum(math.prod(shape) for shape in shapes)
    return pl.pallas_call(
        kernel,
        out_shape=[jax.ShapeDtypeStruct(shape, f32) for shape in out_shapes],
        in_specs=in_specs,
        out_specs=out_specs,
        scratch_shapes=[pltpu.VMEM(shape, f32) if isinstance(shape, tuple) else shape for shape in scratch],
        compiler_params=pltpu.CompilerParams(vmem_limit_bytes=room or held + 4 * 2**20),
        cost_estimate=pl.CostEstimate(flops=work * 300, bytes_accessed=work, transcendentals=0),
        input_output_aliases=aliases,
        name=name,
    )(*operands)


def body(
    meshes, shares, bias_source, bias_start, region, table_index, bh_base, bh_slope, conductivity, harmonic_numbers,
    ripple_source, ripple_start,
):
    unused, planes, rows_each, lanes = bias_start.shape
    rows = rows_each * shares
    count = ripple_start.shape[0]
    near = [(i, i + 1) for i in range(0, meshes - 1, 2)]
    far = [(i, i + 1) for i in range(1, meshes - 1, 2)]
    near += [(j, i) for i, j in near]
    far += [(j, i) for i, j in far]
    turned = [[(i, (i + turn) % shares) for i in range(shares)] for turn in range(1, shares)]

    def around(block):
        return [block] + [lax.ppermute(block, "harm", pairs) for pairs in turned]

    whole, apart, paired, token = call(
        pack_kernel, (bias_start, bias_source, region), [ANY] * 3,
        [(7 * planes, rows_each, lanes), (HIGH_SIZE, rows_each, lanes), (HIGH_SIZE, rows_each, lanes), TILE], [VMEM] * 4,
        [pltpu.VMEM(region.shape, region.dtype), pltpu.SemaphoreType.DMA((7,))], "pack", room=PACK_ROOM,
    )
    wholes = around(whole)
    aparts = around(lax.ppermute(apart, "mesh", far))
    edge = ripple_start.shape[:3] + (3, rows, lanes)
    ripple_first, ripple_paired, token = call(
        first_edges_kernel, (ripple_start, ripple_source, token), [ANY] * 3, [edge, edge, TILE], [ANY, ANY, VMEM],
        [(2, *edge), pltpu.SemaphoreType.DMA((2, 3))], "first_edges", room=RP_ROOM,
    )
    ripple_second, = call(
        second_edges_kernel, (ripple_start, ripple_source, token), [ANY] * 3, [edge], [ANY],
        [edge, pltpu.SemaphoreType.DMA((3,))], "second_edges", room=RP_ROOM,
    )
    others, = call(
        pair_kernel, (*wholes[1:], aparts[0]), [VMEM] * (shares - 1) + [ANY],
        [(shares - 1, HIGH_SIZE, rows_each, lanes)], [VMEM], [], "pair",
    )
    paireds = [lax.ppermute(paired, "mesh", near), lax.ppermute(others, "mesh", near)]
    ripple_first = lax.ppermute(ripple_first, "mesh", [pair for pair in far if min(pair) % 4 == 1])
    ripple_second = lax.ppermute(ripple_second, "mesh", [pair for pair in far if min(pair) % 4 == 3])
    ripple_paired = lax.ppermute(ripple_paired, "mesh", near)

    known = (planes + G_LOW + G_HIGH, rows, lanes)
    field, nud, sigma = call(
        functools.partial(bias_kernel, shares, meshes),
        (*wholes, *aparts, *paireds, table_index, bh_base, bh_slope, conductivity),
        [VMEM] * (2 * shares + 2) + [SMEM] * 4,
        [
            bias_start.shape, (planes + NUD_LOW + NUD_HIGH, rows, lanes), (planes + 2 * (ITERS_R - 1), rows, lanes)
        ],
        [VMEM] * 3,
        [
            (3, planes + A_LOW[0] + A_HIGH[0], rows, lanes),
            (3, planes + A_LOW[1] + A_HIGH[1], rows, lanes),
            (3, planes + S_LOW + S_HIGH, rows, lanes),
            known,
            known,
            (KNOTS + 1, *known),
            known,
        ],
        "bias",
        BIAS_WORK,
    )

    lead = ripple_start.shape[:3]
    sweeps = (harmonic_numbers, nud, sigma, ripple_start, ripple_source)
    held = [nud.shape, sigma.shape]
    ripple, inner_edge, inner_loss = call(
        inner_kernel, sweeps, [SMEM] + [ANY] * 4,
        [ripple_start.shape, lead + (4, rows, lanes), (planes, rows, lanes)], [ANY, ANY, VMEM],
        [lead + (planes, rows, lanes)] * 4 + [(6, planes, rows, lanes), (count, 2, planes, rows, lanes)] + held
        + [pltpu.SemaphoreType.DMA((planes,))] * 3 + [pltpu.SemaphoreType.DMA((2,))],
        "inner_ripple",
    )
    ripple, *losses = call(
        functools.partial(outer_kernel, shares, meshes),
        (*sweeps, ripple_first, ripple_second, ripple_paired, inner_edge, inner_loss, ripple), [SMEM] + [ANY] * 10,
        [ripple_start.shape] + [(planes, rows_each, lanes)] * shares, [ANY] + [VMEM] * shares,
        [lead + (slots, rows, lanes) for slots in (8, 8, 4, 6)] + [(6, 6, rows, lanes), (count, 2, 6, rows, lanes)] + held
        + [(planes, rows, lanes), pltpu.SemaphoreType.DMA((8,)), pltpu.SemaphoreType.DMA((4,))],
        "outer_ripple", aliases={10: 0},
    )
    loss = losses[0]
    for turn, pairs in enumerate(turned):
        loss = loss + lax.ppermute(losses[turn + 1], "harm", pairs)
    return field, ripple, loss


def solution(mesh):
    return jax.shard_map(
        functools.partial(body, mesh.shape["mesh"], mesh.shape["harm"]),
        mesh=mesh,
        in_specs=(
            P(None, "mesh", "harm", None),
            P(None, "mesh", "harm", None),
            P("mesh", "harm", None),
            P(),
            P(),
            P(),
            P(),
            P(),
            P("harm", None, None, "mesh", None, None),
            P("harm", None, None, "mesh", None, None),
        ),
        out_specs=(
            P(None, "mesh", "harm", None),
            P("harm", None, None, "mesh", None, None),
            P("mesh", "harm", None),
        ),
        check_vma=False,
    )
```

```python
import functools
import math

import jax
import jax.numpy as jnp
from jax import lax
from jax.experimental import pallas as pl
from jax.experimental.pallas import tpu as pltpu
from jax.sharding import PartitionSpec as P

ITERS_B = 2
ITERS_R = 2
KNOTS = 8
MATS = 4

kappa = 0.05
knot_step = 1.5
soft_width = 0.5
omega_step = 0.25
CAP = 80.0

NUD_LOW, NUD_HIGH = ITERS_R, ITERS_R
A_LOW = [NUD_LOW + ITERS_B - step for step in range(ITERS_B + 1)]
A_HIGH = [NUD_HIGH + 1 + 2 * (ITERS_B - step) for step in range(ITERS_B + 1)]
S_LOW, S_HIGH = A_LOW[1], A_HIGH[1]
G_LOW, G_HIGH = A_LOW[0], A_HIGH[0] - 1

BIAS_WORK = 20000000
PACK_ROOM = 62 * 2**20
RP_ROOM = 58 * 2**20
NEAR_ROOM = 58 * 2**20
VMEM = pl.BlockSpec(memory_space=pltpu.VMEM)
SMEM = pl.BlockSpec(memory_space=pltpu.SMEM)
ANY = pl.BlockSpec(memory_space=pl.ANY)


TILE = (8, 128)


class Tiles:
    def __init__(self, rows, lanes):
        self.grid = (rows // TILE[0], lanes // TILE[1])
        self.spots = [(i, j) for i in range(self.grid[0]) for j in range(self.grid[1])]
        self.at_end, self.at_start = [], []
        for axis in range(2):
            place = lax.broadcasted_iota(jnp.int32, TILE, axis)
            self.at_end.append(place == TILE[axis] - 1)
            self.at_start.append(place == 0)

    def where(self, spot):
        return (slice(spot[0] * TILE[0], (spot[0] + 1) * TILE[0]), slice(spot[1] * TILE[1], (spot[1] + 1) * TILE[1]))

    def load(self, ref, *lead):
        return {spot: ref[lead + self.where(spot)] for spot in self.spots}

    def store(self, ref, lead, values):
        for spot in self.spots:
            ref[lead + self.where(spot)] = values[spot]

    def each(self, function, *values):
        return {spot: function(*(value[spot] for value in values)) for spot in self.spots}

    def side(self, step, axis):
        return (self.at_end if step > 0 else self.at_start)[axis]

    def is_edge(self, spot, step, axis):
        return spot[axis] == (self.grid[axis] - 1 if step > 0 else 0)

    def move(self, values, step, axis, fill):
        rolled = self.each(lambda tile: pltpu.roll(tile, TILE[axis] - 1 if step > 0 else 1, axis), values)
        side, moved = self.side(step, axis), {}
        for spot in self.spots:
            if self.is_edge(spot, step, axis):
                moved[spot] = jnp.where(side, 0.0, rolled[spot]) if fill else rolled[spot]
            else:
                other = (spot[0] + step, spot[1]) if axis == 0 else (spot[0], spot[1] + step)
                moved[spot] = jnp.where(side, rolled[other], rolled[spot])
        return moved

    def inner(self, values, step, axis):
        side = self.side(step, axis)
        return {
            spot: jnp.where(side, 0.0, values[spot]) if self.is_edge(spot, step, axis) else values[spot]
            for spot in self.spots
        }


SIDES = ((1, 0), (-1, 0), (1, 1), (-1, 1))


def double_couplings(tiles, center, above, below):
    add = lambda one, other: one + other
    weights = [tiles.each(add, center, above), tiles.each(add, center, below)]
    total = tiles.each(add, *weights)
    for step, axis in SIDES:
        weight = tiles.each(add, center, tiles.move(center, step, axis, True))
        total = tiles.each(add, total, weight)
        weights.append(tiles.inner(weight, step, axis))
    return weights, tiles.each(lambda value: value + 2.0 * kappa, total)


def pull(tiles, start, weights, center, above, below):
    moved = [above, below] + [tiles.move(center, step, axis, False) for step, axis in SIDES]
    total = start
    for weight, other in zip(weights, moved):
        total = tiles.each(lambda so_far, w, value: so_far + w * value, total, weight, other)
    return total


def flux_squared(tiles, field, plane):
    ax, ay, az = (tiles.load(field, part, plane) for part in range(3))
    ay_first, az_first = tiles.load(field, 1, plane + 1), tiles.load(field, 2, plane + 1)
    ax_second, az_second = tiles.move(ax, 1, 0, True), tiles.move(az, 1, 0, True)
    ax_third, ay_third = tiles.move(ax, 1, 1, True), tiles.move(ay, 1, 1, True)

    def square(x, y, z, y1, z1, x2, z2, x3, y3):
        flux_one = (z2 - z) - (y3 - y)
        flux_two = (x3 - x) - (z1 - z)
        flux_three = (y1 - y) - (x2 - x)
        return flux_one * flux_one + flux_two * flux_two + flux_three * flux_three

    return tiles.each(square, ax, ay, az, ay_first, az_first, ax_second, az_second, ax_third, ay_third)


def reluctivity(tiles, flux_sq, base, slope_of, slope_total, incremental):
    doubled = tiles.each(lambda value: value * (1.0 / soft_width), flux_sq)
    excess = tiles.each(lambda value: jnp.maximum(value - CAP, 0.0), doubled)
    floor = tiles.each(lambda value: jnp.exp(-value), excess)
    rising = tiles.each(lambda value: jnp.exp(jnp.minimum(value, CAP)), doubled)
    nu = tiles.each(lambda start, slope, value: start + slope * value, base, slope_total, excess)
    slope_sum = None
    for knot in range(KNOTS):
        factor = math.exp(-knot_step * knot / soft_width)
        slope = slope_of(knot)
        high = tiles.each(lambda value: value * factor, rising)
        both = tiles.each(lambda one, other: one + other, high, floor)
        nu = tiles.each(lambda so_far, weight, value: so_far + weight * jnp.log(value), nu, slope, both)
        if incremental:
            part = tiles.each(lambda weight, one, other: weight * (one / other), slope, high, both)
            slope_sum = tiles.each(lambda one, other: one + other, slope_sum, part) if knot else part
    if incremental:
        nu = tiles.each(lambda value, s, slope: value + (2.0 / soft_width) * (s * slope), nu, flux_sq, slope_sum)
    return nu


def loop_in_pairs(count, body):
    def step(at, carry):
        body(2 * at)
        body(2 * at + 1)
        return carry

    lax.fori_loop(0, count // 2, step, 0)
    if count % 2:
        body(count - 1)


LOW_SIZE = 3 * (A_LOW[0] + S_LOW) + G_LOW
HIGH_SIZE = 3 * (A_HIGH[0] + S_HIGH) + G_HIGH


def edge_parts(planes, low):
    halo_of = ((A_LOW if low else A_HIGH)[0], S_LOW if low else S_HIGH, G_LOW if low else G_HIGH)
    at, parts = 0, []
    for array in range(7):
        halo = halo_of[0 if array < 3 else 1 if array < 6 else 2]
        parts.append((array * planes + (planes - halo if low else 0), at, halo))
        at += halo
    return parts


def write_edge(target, whole, low):
    for first, at, halo in edge_parts(whole.shape[0] // 7, low):
        target[at:at + halo] = whole[first:first + halo]


def is_odd():
    return lax.rem(lax.axis_index("mesh"), 2) == 1


def pack_kernel(start, source, region, whole, apart, paired, token, marks, sems):
    token[...] = jnp.zeros(token.shape, token.dtype)
    planes = region.shape[0]
    copies = [pltpu.make_async_copy(region, marks, sems.at[0])]
    for part in range(3):
        for at, origin in ((part, start), (3 + part, source)):
            target = whole.at[at * planes:(at + 1) * planes]
            copies.append(pltpu.make_async_copy(origin.at[part], target, sems.at[at + 1]))
    for copy in copies:
        copy.start()
    for copy in copies:
        copy.wait()
    whole[6 * planes:] = marks[...].astype(jnp.float32)
    for odd in (False, True):
        pl.when(is_odd() == odd)(functools.partial(write_edge, apart, whole, odd))
        pl.when(is_odd() == odd)(functools.partial(write_edge, paired, whole, not odd))


def pair_kernel(*refs):
    wholes, (paired, token) = refs[:-3], refs[-2:]
    token[...] = jnp.zeros(token.shape, token.dtype)
    for odd in (False, True):

        @pl.when(is_odd() == odd)
        def write():
            for turn, whole in enumerate(wholes):
                write_edge(paired.at[turn], whole, not odd)


def is_second():
    return lax.rem(lax.axis_index("mesh") + 1, 4) < 2


def edge_copies(start, source, buffer, target, top, sems, harmonics):
    planes = start.shape[3]
    ways_in = []
    for part, (origin, count, onto) in enumerate(((start, 2, 0), (source, 1, 2))):
        at = jnp.where(top, planes - count, 0)
        ways_in.append(
            pltpu.make_async_copy(
                planes_of(origin.at[harmonics], at, count), planes_of(buffer.at[harmonics], onto, count), sems.at[part]
            )
        )
        ways_in[-1].start()
    return ways_in, pltpu.make_async_copy(buffer.at[harmonics], target, sems.at[2])


def send_edges(start, source, buffer, targets, top, sems, parts):
    ways = [
        edge_copies(start, source, buffer, target, top, sems.at[at], harmonics)
        for at, (target, harmonics) in enumerate(zip(targets, parts))
    ]
    for ways_in, way_out in ways:
        for copy in ways_in:
            copy.wait()
        way_out.start()
    for unused, way_out in ways:
        way_out.wait()


def send_near_edges(start, source, targets, buffers, sems):
    planes = start.shape[3]
    ways = []
    for number, (origin, buffer, target) in enumerate(zip((start, source), buffers, targets)):
        count = target.shape[3]
        first = jnp.where(is_odd(), 0, planes - count)
        held = planes_of(buffer, 0, count)
        ways.append(
            (
                pltpu.make_async_copy(planes_of(origin, first, count), held, sems.at[2 * number]),
                pltpu.make_async_copy(held, target, sems.at[2 * number + 1]),
            )
        )
    for way_in, unused in ways:
        way_in.start()
    for way_in, way_out in ways:
        way_in.wait()
        way_out.start()
    for unused, way_out in ways:
        way_out.wait()


def first_edges_kernel(parts, start, source, after, *refs):
    aparts, (paired_start, paired_source, token, buffer, other_buffer, sems, near_sems) = refs[:len(parts)], refs[len(parts):]
    token[...] = jnp.zeros(token.shape, token.dtype)

    @pl.when(jnp.logical_not(is_second()))
    def send_apart():
        send_edges(start, source, buffer, aparts, is_odd(), sems, parts)

    @pl.when(is_second())
    def send_near():
        send_near_edges(start, source, (paired_start, paired_source), (buffer, other_buffer), near_sems)


def near_edges_kernel(start, source, after, start_in, source_in, paired_start, paired_source, buffer, other_buffer, sems):
    @pl.when(jnp.logical_not(is_second()))
    def send_near():
        send_near_edges(start, source, (paired_start, paired_source), (buffer, other_buffer), sems)


def second_edges_kernel(parts, start, source, after, *refs):
    aparts, (buffer, sems) = refs[:len(parts)], refs[len(parts):]

    @pl.when(is_second())
    def send_apart():
        send_edges(start, source, buffer, aparts, is_odd(), sems, parts)


def bias_kernel(shares, meshes, *refs):
    wholes, aparts, (paired, others) = refs[:shares], refs[shares:2 * shares], refs[2 * shares:2 * shares + 2]
    paireds = [paired] + [others.at[at] for at in range(shares - 1)]
    table_index, bh_base, bh_slope, conductivity, field_out, nud_out, sigma_out = refs[2 * shares + 2:2 * shares + 9]
    a0, a1, src, marks, nu, slopes, bases = refs[2 * shares + 9:]
    planes = wholes[0].shape[0] // 7
    rows_each, lanes = wholes[0].shape[1:]
    rows = rows_each * shares
    mine = lax.axis_index("harm")
    here = lax.axis_index("mesh")
    arrays = [(a0.at[part], A_LOW[0]) for part in range(3)]
    arrays += [(src.at[part], S_LOW) for part in range(3)] + [(marks, G_LOW)]
    for turn in range(shares):
        owner = lax.rem(mine + shares - turn, shares)
        at = pl.ds(pl.multiple_of(owner * rows_each, rows_each), rows_each)

        def fill(low, high):
            for (target, onto), (unused, first, halo) in zip(arrays, edge_parts(planes, True)):
                target[0:halo, at, :] = low[first:first + halo]
            for (target, onto), (unused, first, halo) in zip(arrays, edge_parts(planes, False)):
                target[onto + planes:onto + planes + halo, at, :] = high[first:first + halo]

        for number, (target, onto) in enumerate(arrays):
            target[onto:onto + planes, at, :] = wholes[turn][number * planes:(number + 1) * planes]
        pl.when(is_odd())(functools.partial(fill, paireds[turn], aparts[turn]))
        pl.when(jnp.logical_not(is_odd()))(functools.partial(fill, aparts[turn], paireds[turn]))

    tiles = Tiles(rows, lanes)
    tables = [table_index[member] for member in range(MATS)]
    base_of = [bh_base[table] for table in tables]
    slope_of = [[soft_width * bh_slope[table, knot] for table in tables] for knot in range(KNOTS)]
    sigma_of = [conductivity[member] for member in range(MATS)]

    def inside(plane):
        low_ok = jnp.logical_or(plane >= 0, here > 0)
        high_ok = jnp.logical_or(plane < planes, here < meshes - 1)
        return jnp.where(jnp.logical_and(low_ok, high_ok), 1.0, 0.0)

    def choose(marks_are, values):
        def one(*marked):
            chosen = jnp.where(marked[0], values[1], values[0])
            for member in range(2, MATS):
                chosen = jnp.where(marked[member - 1], values[member], chosen)
            return chosen

        return tiles.each(one, *marks_are)

    def members(mark):
        return [tiles.each(lambda value: value == float(member), mark) for member in range(1, MATS)]

    def relax_into(target, step, old):
        def body(at):
            plane = at - A_LOW[step]
            near = at + 1
            weights, total = double_couplings(
                tiles, tiles.load(nu, near), tiles.load(nu, near + 1), tiles.load(nu, near - 1)
            )
            keep = inside(plane)
            scale = tiles.each(lambda value: keep / value, total)
            from_old = plane + A_LOW[step - 1]
            for part in range(3):
                twice = tiles.each(lambda value: value + value, tiles.load(src, part, plane + S_LOW))
                near_old = [tiles.load(old, part, from_old + move) for move in (0, 1, -1)]
                moved = pull(tiles, twice, weights, *near_old)
                tiles.store(target, (part, at), tiles.each(lambda value, by: value * by, moved, scale))

        loop_in_pairs(planes + A_LOW[step] + A_HIGH[step], body)

    def first_nu(at):
        marked = members(tiles.load(marks, at))
        base, slope = choose(marked, base_of), [choose(marked, slope_of[knot]) for knot in range(KNOTS)]
        whole_slope = slope[0]
        tiles.store(bases, (at,), base)
        for knot in range(KNOTS):
            tiles.store(slopes, (knot, at), slope[knot])
            if knot:
                whole_slope = tiles.each(lambda one, other: one + other, whole_slope, slope[knot])
        tiles.store(slopes, (KNOTS, at), whole_slope)
        value = reluctivity(tiles, flux_squared(tiles, a0, at), base, lambda knot: slope[knot], whole_slope, False)
        keep = inside(at - G_LOW)
        tiles.store(nu, (at,), tiles.each(lambda one: one * keep, value))

    loop_in_pairs(planes + G_LOW + G_HIGH, first_nu)
    fields = (a0, a1)
    for step in range(1, ITERS_B + 1):
        old, new = fields[(step - 1) % 2], fields[step % 2]
        relax_into(new, step, old)
        last = step == ITERS_B
        lower = NUD_LOW if last else A_LOW[step + 1] + 1
        upper = NUD_HIGH if last else A_HIGH[step + 1] + 1

        def next_nu(at):
            plane = at - lower
            known = plane + G_LOW
            value = reluctivity(
                tiles, flux_squared(tiles, new, plane + A_LOW[step]), tiles.load(bases, known),
                lambda knot: tiles.load(slopes, knot, known), tiles.load(slopes, KNOTS, known), last,
            )
            keep = inside(plane)
            tiles.store(nud_out if last else nu, (at,), tiles.each(lambda one: one * keep, value))

        loop_in_pairs(planes + lower + upper, next_nu)

    def sigma_at(at):
        marked = members(tiles.load(marks, at - (ITERS_R - 1) + G_LOW))
        tiles.store(sigma_out, (at,), choose(marked, sigma_of))

    loop_in_pairs(planes + 2 * (ITERS_R - 1), sigma_at)
    own_rows = pl.ds(pl.multiple_of(mine * rows_each, rows_each), rows_each)
    final = fields[ITERS_B % 2]
    for part in range(3):
        field_out[part] = final[part, A_LOW[ITERS_B]:A_LOW[ITERS_B] + planes, own_rows, :]


def planes_of(ref, first, count):
    return ref.at[:, :, :, pl.ds(first, count)]


class Ripple:
    def __init__(self, rows, lanes, harmonic_numbers, count, sides, answer):
        self.sides, self.answer, self.tiles = sides, answer, Tiles(rows, lanes)
        first = lax.axis_index("harm") * count
        self.omegas = [omega_step * harmonic_numbers[first + at].astype(jnp.float32) for at in range(count)]

    def prepare(self, nud, sigma, slot, keep):
        tiles, near = self.tiles, slot + NUD_LOW - 1
        weights, total = double_couplings(tiles, *(tiles.load(nud, near + move) for move in (0, 1, -1)))
        for number, weight in enumerate(weights):
            tiles.store(self.sides, (number, slot), tiles.each(lambda value: 0.5 * value, weight))
        total = tiles.each(lambda value: 0.5 * value, total)
        square = tiles.each(lambda value: value * value, total)
        conduct = tiles.load(sigma, slot)
        for harmonic, omega in enumerate(self.omegas):
            damp = tiles.each(lambda value: omega * value, conduct)
            inverse = tiles.each(lambda one, other: keep / (one + other * other), square, damp)
            for part, value in enumerate((total, damp)):
                scaled = tiles.each(lambda one, other: one * other, value, inverse)
                tiles.store(self.answer, (harmonic, part, slot), scaled)

    def sweep(self, slot, harmonics, old, source, put):
        tiles, loss = self.tiles, None
        weights = [tiles.load(self.sides, number, slot) for number in range(6)]
        for harmonic in harmonics:
            straight, turned = (tiles.load(self.answer, harmonic, part, slot) for part in range(2))
            power = None
            for part in range(3):
                both = []
                for piece in range(2):
                    near_old = [tiles.load(*old(move, harmonic, piece, part)) for move in (0, 1, -1)]
                    both.append(pull(tiles, tiles.load(*source(harmonic, piece, part)), weights, *near_old))
                real = tiles.each(lambda re, im, a, b: re * a + im * b, *both, straight, turned)
                imag = tiles.each(lambda re, im, a, b: im * a - re * b, *both, straight, turned)
                for piece, value in enumerate((real, imag)):
                    where = put(harmonic, piece, part)
                    tiles.store(where[0], where[1:], value)
                squared = tiles.each(lambda re, im: re * re + im * im, real, imag)
                power = tiles.each(lambda one, other: one + other, power, squared) if part else squared
            factor = 0.5 * self.omegas[harmonic] * self.omegas[harmonic]
            scaled = tiles.each(lambda value: factor * value, power)
            loss = tiles.each(lambda one, other: one + other, loss, scaled) if loss else scaled
        return loss


def inner_kernel(
    meshes, harmonic_numbers, nud, sigma, start, source, ripple_out, edge_out, loss_out, sides, answer, r1, r2, sems
):
    count, planes = start.shape[0], start.shape[3]
    here = lax.axis_index("mesh")
    ripple = Ripple(*start.shape[4:], harmonic_numbers, count, sides, answer)
    tiles = ripple.tiles

    def prepare(slot):
        low_ok = jnp.logical_or(slot > 0, here > 0)
        high_ok = jnp.logical_or(slot < planes + 1, here < meshes - 1)
        ripple.prepare(nud, sigma, slot, jnp.where(jnp.logical_and(low_ok, high_ok), 1.0, 0.0))

    def drain(plane):
        return pltpu.make_async_copy(planes_of(r2, plane, 1), planes_of(ripple_out, plane, 1), sems.at[plane])

    def sweep(plane, old, new):
        return ripple.sweep(
            plane + 1, range(count), lambda move, *lead: (old, *lead, plane + move), lambda *lead: (source, *lead, plane),
            lambda *lead: (new, *lead, plane),
        )

    def first(plane, carry):
        sweep(plane, start, r1)
        return carry

    def second(plane, carry):
        loss = sweep(plane, r1, r2)
        tiles.store(loss_out, (plane,), tiles.each(lambda one, other: one * other, tiles.load(sigma, plane + 1), loss))
        drain(plane).start()
        return carry

    loop_in_pairs(planes + 2, prepare)
    lax.fori_loop(1, planes - 1, first, 0)
    lax.fori_loop(2, planes - 2, second, 0)
    for place, onto in ((1, 0), (planes - 3, 2)):
        edge_out[:, :, :, onto:onto + 2] = r1[:, :, :, place:place + 2]
    for plane in range(2, planes - 2):
        drain(plane).wait()


def outer_kernel(
    harmonics, shares, harmonic_numbers, sigma, start, source, first_apart, second_apart, paired_start, paired_source, edge, sides, answer,
    loss_in, so_far, ripple_in, ripple_out, *refs
):
    losses, (r0, r1, r2, src, loss, sems, halo_sems) = refs[:-7], refs[-7:]
    count, planes = start.shape[0], start.shape[3]
    rows, lanes = start.shape[4:]
    begin, chosen = harmonics.start, slice(harmonics.start, harmonics.stop)
    odd = is_odd()

    def halo(start_part, source_part, above, number):
        return [
            pltpu.make_async_copy(start_part, planes_of(r0, jnp.where(above, 2, 0), 2), halo_sems.at[number]),
            pltpu.make_async_copy(source_part, planes_of(src, jnp.where(above, 1, 0), 1), halo_sems.at[number + 1]),
        ]

    def apart_halo(origin):
        return halo(planes_of(origin, 0, 2), planes_of(origin, 2, 1), odd, 0)

    for second, origin in ((False, first_apart), (True, second_apart.at[chosen])):

        @pl.when(is_second() == second)
        def start_apart():
            for copy in apart_halo(origin):
                copy.start()

    near = halo(paired_start.at[chosen], paired_source.at[chosen], jnp.logical_not(odd), 2)
    for copy in near:
        copy.start()
    for copy in apart_halo(first_apart) + near:
        copy.wait()
    ripple = Ripple(rows, lanes, harmonic_numbers, count, sides, answer)
    tiles = ripple.tiles
    old = {-2: (r0, 0), -1: (r0, 1), planes: (r0, 2), planes + 1: (r0, 3)}
    old.update({plane: (start, plane) for plane in (0, 1, planes - 2, planes - 1)})
    new = {-1: (r1, 0), 0: (r1, 1), planes - 1: (r1, 2), planes: (r1, 3)}
    new.update({1: (edge, 0), 2: (edge, 1), planes - 3: (edge, 2), planes - 2: (edge, 3)})
    given = {-1: (src, 0), planes: (src, 1)}
    given.update({plane: (source, plane) for plane in (0, 1, planes - 2, planes - 1)})

    def at(place, harmonic, *lead):
        ref, slot = place
        shift = 0 if ref.shape[0] == count else begin
        return (ref, harmonic - shift, *lead, slot)

    for plane in (-1, 0, planes - 1, planes):
        ripple.sweep(
            plane + 1, harmonics, lambda move, *lead: at(old[plane + move], *lead), lambda *lead: at(given[plane], *lead),
            lambda *lead: at(new[plane], *lead),
        )

    def drain(slot, plane):
        return pltpu.make_async_copy(
            planes_of(r2, slot, 1), planes_of(ripple_out.at[chosen], plane, 1), sems.at[slot]
        )

    edges = list(enumerate((0, 1, planes - 2, planes - 1)))
    last = harmonics.stop == count
    for slot, plane in edges:
        added = ripple.sweep(
            plane + 1, harmonics, lambda move, *lead: at(new[plane + move], *lead), lambda *lead: at(given[plane], *lead),
            lambda *lead: at((r2, slot), *lead),
        )
        drain(slot, plane).start()
        if begin:
            added = tiles.each(lambda one, other: one + other, added, tiles.load(so_far, slot))
        if last:
            added = tiles.each(lambda one, other: one * other, tiles.load(sigma, plane + 1), added)
            tiles.store(loss, (slot,), added)
        else:
            tiles.store(losses[0], (slot,), added)
    if last:
        rows_each = rows // shares
        for turn in range(shares):
            owner = lax.rem(lax.axis_index("harm") + turn, shares)
            part = pl.ds(pl.multiple_of(owner * rows_each, rows_each), rows_each)
            losses[turn][2:planes - 2] = loss_in[2:planes - 2, part, :]
            for slot, plane in edges:
                losses[turn][plane] = loss[slot, part, :]
    for slot, plane in edges:
        drain(slot, plane).wait()


def call(kernel, operands, in_specs, out_shapes, out_specs, scratch, name, work=0, aliases={}, room=0):
    f32 = jnp.float32
    shapes = [o.shape for o, spec in zip(operands, in_specs) if spec is VMEM]
    shapes += [shape for shape, spec in zip(out_shapes, out_specs) if spec is VMEM]
    shapes += [shape for shape in scratch if isinstance(shape, tuple)]
    held = 4 * sum(math.prod(shape) for shape in shapes)
    return pl.pallas_call(
        kernel,
        out_shape=[jax.ShapeDtypeStruct(shape, f32) for shape in out_shapes],
        in_specs=in_specs,
        out_specs=out_specs,
        scratch_shapes=[pltpu.VMEM(shape, f32) if isinstance(shape, tuple) else shape for shape in scratch],
        compiler_params=pltpu.CompilerParams(vmem_limit_bytes=room or held + 4 * 2**20),
        cost_estimate=pl.CostEstimate(flops=work * 300, bytes_accessed=work, transcendentals=0),
        input_output_aliases=aliases,
        name=name,
    )(*operands)


def body(
    meshes, shares, bias_source, bias_start, region, table_index, bh_base, bh_slope, conductivity, harmonic_numbers,
    ripple_source, ripple_start,
):
    unused, planes, rows_each, lanes = bias_start.shape
    rows = rows_each * shares
    count = ripple_start.shape[0]
    near = [(i, i + 1) for i in range(0, meshes - 1, 2)]
    far = [(i, i + 1) for i in range(1, meshes - 1, 2)]
    near += [(j, i) for i, j in near]
    far += [(j, i) for i, j in far]
    turned = [[(i, (i + turn) % shares) for i in range(shares)] for turn in range(1, shares)]

    def around(block):
        return [block] + [lax.ppermute(block, "harm", pairs) for pairs in turned]

    whole, apart, paired, token = call(
        pack_kernel, (bias_start, bias_source, region), [ANY] * 3,
        [(7 * planes, rows_each, lanes), (HIGH_SIZE, rows_each, lanes), (HIGH_SIZE, rows_each, lanes), TILE], [VMEM] * 4,
        [pltpu.VMEM(region.shape, region.dtype), pltpu.SemaphoreType.DMA((7,))], "pack", room=PACK_ROOM,
    )
    wholes = around(whole)
    aparts = around(lax.ppermute(apart, "mesh", far))
    edge = ripple_start.shape[:3] + (3, rows, lanes)
    parts = [range(0, count)]
    spans = [slice(part.start, part.stop) for part in parts]
    near_edges = [edge[:3] + (size, rows, lanes) for size in (2, 1)]
    part_edges = [(len(part), *edge[1:]) for part in parts]
    *ripple_firsts, paired_start, paired_source, token = call(
        functools.partial(first_edges_kernel, spans), (ripple_start, ripple_source, token), [ANY] * 3,
        part_edges + near_edges + [TILE], [ANY] * (len(parts) + 2) + [VMEM],
        [edge, edge, pltpu.SemaphoreType.DMA((len(parts), 3)), pltpu.SemaphoreType.DMA((4,))], "first_edges", room=RP_ROOM,
    )
    ripple_seconds = call(
        functools.partial(second_edges_kernel, spans), (ripple_start, ripple_source, token), [ANY] * 3,
        part_edges, [ANY] * len(parts), [edge, pltpu.SemaphoreType.DMA((len(parts), 3))], "second_edges", room=RP_ROOM,
    )
    others, token = call(
        pair_kernel, (*wholes[1:], aparts[0]), [VMEM] * (shares - 1) + [ANY],
        [(shares - 1, HIGH_SIZE, rows_each, lanes), TILE], [VMEM] * 2, [], "pair",
    )
    ripple_paireds = call(
        near_edges_kernel, (ripple_start, ripple_source, token, paired_start, paired_source), [ANY] * 5,
        near_edges, [ANY] * 2, [edge, edge, pltpu.SemaphoreType.DMA((4,))], "near_edges", aliases={3: 0, 4: 1},
        room=NEAR_ROOM,
    )
    paireds = [lax.ppermute(paired, "mesh", near), lax.ppermute(others, "mesh", near)]
    first_pairs, second_pairs = ([pair for pair in far if min(pair) % 4 == kind] for kind in (1, 3))
    ripple_firsts = [lax.ppermute(part, "mesh", first_pairs) for part in ripple_firsts]
    ripple_seconds = [lax.ppermute(part, "mesh", second_pairs) for part in ripple_seconds]
    ripple_paireds = [lax.ppermute(part, "mesh", near) for part in ripple_paireds]

    known = (planes + G_LOW + G_HIGH, rows, lanes)
    field, nud, sigma = call(
        functools.partial(bias_kernel, shares, meshes),
        (*wholes, *aparts, *paireds, table_index, bh_base, bh_slope, conductivity),
        [VMEM] * (2 * shares + 2) + [SMEM] * 4,
        [
            bias_start.shape, (planes + NUD_LOW + NUD_HIGH, rows, lanes), (planes + 2 * (ITERS_R - 1), rows, lanes)
        ],
        [VMEM] * 3,
        [
            (3, planes + A_LOW[0] + A_HIGH[0], rows, lanes),
            (3, planes + A_LOW[1] + A_HIGH[1], rows, lanes),
            (3, planes + S_LOW + S_HIGH, rows, lanes),
            known,
            known,
            (KNOTS + 1, *known),
            known,
        ],
        "bias",
        BIAS_WORK,
    )

    lead = ripple_start.shape[:3]
    slots = (planes + 2, rows, lanes)
    ripple, inner_edge, inner_loss, sides, answer = call(
        functools.partial(inner_kernel, meshes), (harmonic_numbers, nud, sigma, ripple_start, ripple_source),
        [SMEM] + [VMEM] * 4,
        [ripple_start.shape, lead + (4, rows, lanes), (planes, rows, lanes), (6, *slots), (count, 2, *slots)],
        [ANY] + [VMEM] * 4, [lead + (planes, rows, lanes)] * 2 + [pltpu.SemaphoreType.DMA((planes,))], "inner_ripple",
    )
    so_far = inner_loss
    for part, ripple_first, ripple_second in zip(parts, ripple_firsts, ripple_seconds):
        last = part.stop == count
        here = (len(part), *lead[1:])
        ripple, *losses = call(
            functools.partial(outer_kernel, part, shares),
            (
                harmonic_numbers, sigma, ripple_start, ripple_source, ripple_first, ripple_second, *ripple_paireds,
                inner_edge, sides, answer, inner_loss, so_far, ripple,
            ),
            [SMEM] + [VMEM] * 3 + [ANY] * 4 + [VMEM] * 5 + [ANY],
            [ripple_start.shape] + ([(planes, rows_each, lanes)] * shares if last else [(4, rows, lanes)]),
            [ANY] + [VMEM] * (shares if last else 1),
            [here + (4, rows, lanes)] * 3 + [here + (2, rows, lanes), (4, rows, lanes)]
            + [pltpu.SemaphoreType.DMA((4,))] * 2,
            "outer_ripple", aliases={13: 0},
        )
        so_far = losses[0]
    loss = losses[0]
    for turn, pairs in enumerate(turned):
        loss = loss + lax.ppermute(losses[turn + 1], "harm", pairs)
    return field, ripple, loss


def solution(mesh):
    return jax.shard_map(
        functools.partial(body, mesh.shape["mesh"], mesh.shape["harm"]),
        mesh=mesh,
        in_specs=(
            P(None, "mesh", "harm", None),
            P(None, "mesh", "harm", None),
            P("mesh", "harm", None),
            P(),
            P(),
            P(),
            P(),
            P(),
            P("harm", None, None, "mesh", None, None),
            P("harm", None, None, "mesh", None, None),
        ),
        out_specs=(
            P(None, "mesh", "harm", None),
            P("harm", None, None, "mesh", None, None),
            P("mesh", "harm", None),
        ),
        check_vma=False,
    )
```

```python
import functools
import math

import jax
import jax.numpy as jnp
from jax import lax
from jax.experimental import pallas as pl
from jax.experimental.pallas import tpu as pltpu
from jax.sharding import PartitionSpec as P

ITERS_B = 2
ITERS_R = 2
KNOTS = 8
MATS = 4

kappa = 0.05
knot_step = 1.5
soft_width = 0.5
omega_step = 0.25
CAP = 80.0

NUD_LOW, NUD_HIGH = ITERS_R, ITERS_R
A_LOW = [NUD_LOW + ITERS_B - step for step in range(ITERS_B + 1)]
A_HIGH = [NUD_HIGH + 1 + 2 * (ITERS_B - step) for step in range(ITERS_B + 1)]
S_LOW, S_HIGH = A_LOW[1], A_HIGH[1]
G_LOW, G_HIGH = A_LOW[0], A_HIGH[0] - 1

BIAS_WORK = 20000000
PACK_ROOM = 62 * 2**20
RP_ROOM = 58 * 2**20
NEAR_ROOM = 58 * 2**20
VMEM = pl.BlockSpec(memory_space=pltpu.VMEM)
SMEM = pl.BlockSpec(memory_space=pltpu.SMEM)
ANY = pl.BlockSpec(memory_space=pl.ANY)


TILE = (8, 128)


class Tiles:
    def __init__(self, rows, lanes):
        self.grid = (rows // TILE[0], lanes // TILE[1])
        self.spots = [(i, j) for i in range(self.grid[0]) for j in range(self.grid[1])]
        self.at_end, self.at_start = [], []
        for axis in range(2):
            place = lax.broadcasted_iota(jnp.int32, TILE, axis)
            self.at_end.append(place == TILE[axis] - 1)
            self.at_start.append(place == 0)

    def where(self, spot):
        return (slice(spot[0] * TILE[0], (spot[0] + 1) * TILE[0]), slice(spot[1] * TILE[1], (spot[1] + 1) * TILE[1]))

    def load(self, ref, *lead):
        return {spot: ref[lead + self.where(spot)] for spot in self.spots}

    def store(self, ref, lead, values):
        for spot in self.spots:
            ref[lead + self.where(spot)] = values[spot]

    def each(self, function, *values):
        return {spot: function(*(value[spot] for value in values)) for spot in self.spots}

    def side(self, step, axis):
        return (self.at_end if step > 0 else self.at_start)[axis]

    def is_edge(self, spot, step, axis):
        return spot[axis] == (self.grid[axis] - 1 if step > 0 else 0)

    def move(self, values, step, axis, fill):
        rolled = self.each(lambda tile: pltpu.roll(tile, TILE[axis] - 1 if step > 0 else 1, axis), values)
        side, moved = self.side(step, axis), {}
        for spot in self.spots:
            if self.is_edge(spot, step, axis):
                moved[spot] = jnp.where(side, 0.0, rolled[spot]) if fill else rolled[spot]
            else:
                other = (spot[0] + step, spot[1]) if axis == 0 else (spot[0], spot[1] + step)
                moved[spot] = jnp.where(side, rolled[other], rolled[spot])
        return moved

    def inner(self, values, step, axis):
        side = self.side(step, axis)
        return {
            spot: jnp.where(side, 0.0, values[spot]) if self.is_edge(spot, step, axis) else values[spot]
            for spot in self.spots
        }


SIDES = ((1, 0), (-1, 0), (1, 1), (-1, 1))


def double_couplings(tiles, center, above, below):
    add = lambda one, other: one + other
    weights = [tiles.each(add, center, above), tiles.each(add, center, below)]
    total = tiles.each(add, *weights)
    for step, axis in SIDES:
        weight = tiles.each(add, center, tiles.move(center, step, axis, True))
        total = tiles.each(add, total, weight)
        weights.append(tiles.inner(weight, step, axis))
    return weights, tiles.each(lambda value: value + 2.0 * kappa, total)


def pull(tiles, start, weights, center, above, below):
    moved = [above, below] + [tiles.move(center, step, axis, False) for step, axis in SIDES]
    total = start
    for weight, other in zip(weights, moved):
        total = tiles.each(lambda so_far, w, value: so_far + w * value, total, weight, other)
    return total


def flux_squared(tiles, field, plane):
    ax, ay, az = (tiles.load(field, part, plane) for part in range(3))
    ay_first, az_first = tiles.load(field, 1, plane + 1), tiles.load(field, 2, plane + 1)
    ax_second, az_second = tiles.move(ax, 1, 0, True), tiles.move(az, 1, 0, True)
    ax_third, ay_third = tiles.move(ax, 1, 1, True), tiles.move(ay, 1, 1, True)

    def square(x, y, z, y1, z1, x2, z2, x3, y3):
        flux_one = (z2 - z) - (y3 - y)
        flux_two = (x3 - x) - (z1 - z)
        flux_three = (y1 - y) - (x2 - x)
        return flux_one * flux_one + flux_two * flux_two + flux_three * flux_three

    return tiles.each(square, ax, ay, az, ay_first, az_first, ax_second, az_second, ax_third, ay_third)


def reluctivity(tiles, flux_sq, base, slope_of, slope_total, incremental):
    doubled = tiles.each(lambda value: value * (1.0 / soft_width), flux_sq)
    excess = tiles.each(lambda value: jnp.maximum(value - CAP, 0.0), doubled)
    floor = tiles.each(lambda value: jnp.exp(-value), excess)
    rising = tiles.each(lambda value: jnp.exp(jnp.minimum(value, CAP)), doubled)
    nu = tiles.each(lambda start, slope, value: start + slope * value, base, slope_total, excess)
    slope_sum = None
    for knot in range(KNOTS):
        factor = math.exp(-knot_step * knot / soft_width)
        slope = slope_of(knot)
        high = tiles.each(lambda value: value * factor, rising)
        both = tiles.each(lambda one, other: one + other, high, floor)
        nu = tiles.each(lambda so_far, weight, value: so_far + weight * jnp.log(value), nu, slope, both)
        if incremental:
            part = tiles.each(lambda weight, one, other: weight * (one / other), slope, high, both)
            slope_sum = tiles.each(lambda one, other: one + other, slope_sum, part) if knot else part
    if incremental:
        nu = tiles.each(lambda value, s, slope: value + (2.0 / soft_width) * (s * slope), nu, flux_sq, slope_sum)
    return nu


def loop_in_pairs(count, body):
    def step(at, carry):
        body(2 * at)
        body(2 * at + 1)
        return carry

    lax.fori_loop(0, count // 2, step, 0)
    if count % 2:
        body(count - 1)


LOW_SIZE = 3 * (A_LOW[0] + S_LOW) + G_LOW
HIGH_SIZE = 3 * (A_HIGH[0] + S_HIGH) + G_HIGH


def edge_parts(planes, low):
    halo_of = ((A_LOW if low else A_HIGH)[0], S_LOW if low else S_HIGH, G_LOW if low else G_HIGH)
    at, parts = 0, []
    for array in range(7):
        halo = halo_of[0 if array < 3 else 1 if array < 6 else 2]
        parts.append((array * planes + (planes - halo if low else 0), at, halo))
        at += halo
    return parts


def write_edge(target, whole, low):
    for first, at, halo in edge_parts(whole.shape[0] // 7, low):
        target[at:at + halo] = whole[first:first + halo]


def is_odd():
    return lax.rem(lax.axis_index("mesh"), 2) == 1


def pack_kernel(start, source, region, whole, apart, paired, token, marks, sems):
    token[...] = jnp.zeros(token.shape, token.dtype)
    planes = region.shape[0]
    copies = [pltpu.make_async_copy(region, marks, sems.at[0])]
    for part in range(3):
        for at, origin in ((part, start), (3 + part, source)):
            target = whole.at[at * planes:(at + 1) * planes]
            copies.append(pltpu.make_async_copy(origin.at[part], target, sems.at[at + 1]))
    for copy in copies:
        copy.start()
    for copy in copies:
        copy.wait()
    whole[6 * planes:] = marks[...].astype(jnp.float32)
    for odd in (False, True):
        pl.when(is_odd() == odd)(functools.partial(write_edge, apart, whole, odd))
        pl.when(is_odd() == odd)(functools.partial(write_edge, paired, whole, not odd))


def pair_kernel(*refs):
    wholes, (paired, token) = refs[:-3], refs[-2:]
    token[...] = jnp.zeros(token.shape, token.dtype)
    for odd in (False, True):

        @pl.when(is_odd() == odd)
        def write():
            for turn, whole in enumerate(wholes):
                write_edge(paired.at[turn], whole, not odd)


def is_second():
    return lax.rem(lax.axis_index("mesh") + 1, 4) < 2


def send_edges(start, source, buffer, target, top, sems):
    planes = start.shape[3]
    ways_in = []
    for part, (origin, count, onto) in enumerate(((start, 2, 0), (source, 1, 2))):
        at = jnp.where(top, planes - count, 0)
        ways_in.append(
            pltpu.make_async_copy(planes_of(origin, at, count), planes_of(buffer, onto, count), sems.at[part])
        )
        ways_in[-1].start()
    for copy in ways_in:
        copy.wait()
    way_out = pltpu.make_async_copy(buffer, target, sems.at[2])
    way_out.start()
    way_out.wait()


def send_near_edges(start, source, targets, buffers, sems):
    planes = start.shape[3]
    ways = []
    for number, (origin, buffer, target) in enumerate(zip((start, source), buffers, targets)):
        count = target.shape[3]
        first = jnp.where(is_odd(), 0, planes - count)
        held = planes_of(buffer, 0, count)
        ways.append(
            (
                pltpu.make_async_copy(planes_of(origin, first, count), held, sems.at[2 * number]),
                pltpu.make_async_copy(held, target, sems.at[2 * number + 1]),
            )
        )
    for way_in, unused in ways:
        way_in.start()
    for way_in, way_out in ways:
        way_in.wait()
        way_out.start()
    for unused, way_out in ways:
        way_out.wait()


def first_edges_kernel(
    start, source, after, apart, paired_start, paired_source, token, buffer, other_buffer, sems, near_sems
):
    token[...] = jnp.zeros(token.shape, token.dtype)

    @pl.when(jnp.logical_not(is_second()))
    def send_apart():
        send_edges(start, source, buffer, apart, is_odd(), sems)

    @pl.when(is_second())
    def send_near():
        send_near_edges(start, source, (paired_start, paired_source), (buffer, other_buffer), near_sems)


def near_edges_kernel(start, source, after, start_in, source_in, paired_start, paired_source, buffer, other_buffer, sems):
    @pl.when(jnp.logical_not(is_second()))
    def send_near():
        send_near_edges(start, source, (paired_start, paired_source), (buffer, other_buffer), sems)


def second_edges_kernel(start, source, after, apart, buffer, sems):
    @pl.when(is_second())
    def send_apart():
        send_edges(start, source, buffer, apart, is_odd(), sems)


def bias_kernel(shares, meshes, *refs):
    wholes, aparts, (paired, others) = refs[:shares], refs[shares:2 * shares], refs[2 * shares:2 * shares + 2]
    paireds = [paired] + [others.at[at] for at in range(shares - 1)]
    table_index, bh_base, bh_slope, conductivity, field_out, nud_out, sigma_out = refs[2 * shares + 2:2 * shares + 9]
    a0, a1, src, marks, nu, slopes, bases = refs[2 * shares + 9:]
    planes = wholes[0].shape[0] // 7
    rows_each, lanes = wholes[0].shape[1:]
    rows = rows_each * shares
    mine = lax.axis_index("harm")
    here = lax.axis_index("mesh")
    arrays = [(a0.at[part], A_LOW[0]) for part in range(3)]
    arrays += [(src.at[part], S_LOW) for part in range(3)] + [(marks, G_LOW)]
    for turn in range(shares):
        owner = lax.rem(mine + shares - turn, shares)
        at = pl.ds(pl.multiple_of(owner * rows_each, rows_each), rows_each)

        def fill(low, high):
            for (target, onto), (unused, first, halo) in zip(arrays, edge_parts(planes, True)):
                target[0:halo, at, :] = low[first:first + halo]
            for (target, onto), (unused, first, halo) in zip(arrays, edge_parts(planes, False)):
                target[onto + planes:onto + planes + halo, at, :] = high[first:first + halo]

        for number, (target, onto) in enumerate(arrays):
            target[onto:onto + planes, at, :] = wholes[turn][number * planes:(number + 1) * planes]
        pl.when(is_odd())(functools.partial(fill, paireds[turn], aparts[turn]))
        pl.when(jnp.logical_not(is_odd()))(functools.partial(fill, aparts[turn], paireds[turn]))

    tiles = Tiles(rows, lanes)
    tables = [table_index[member] for member in range(MATS)]
    base_of = [bh_base[table] for table in tables]
    slope_of = [[soft_width * bh_slope[table, knot] for table in tables] for knot in range(KNOTS)]
    sigma_of = [conductivity[member] for member in range(MATS)]

    def inside(plane):
        low_ok = jnp.logical_or(plane >= 0, here > 0)
        high_ok = jnp.logical_or(plane < planes, here < meshes - 1)
        return jnp.where(jnp.logical_and(low_ok, high_ok), 1.0, 0.0)

    def choose(marks_are, values):
        def one(*marked):
            chosen = jnp.where(marked[0], values[1], values[0])
            for member in range(2, MATS):
                chosen = jnp.where(marked[member - 1], values[member], chosen)
            return chosen

        return tiles.each(one, *marks_are)

    def members(mark):
        return [tiles.each(lambda value: value == float(member), mark) for member in range(1, MATS)]

    def relax_into(target, step, old):
        def body(at):
            plane = at - A_LOW[step]
            near = at + 1
            weights, total = double_couplings(
                tiles, tiles.load(nu, near), tiles.load(nu, near + 1), tiles.load(nu, near - 1)
            )
            keep = inside(plane)
            scale = tiles.each(lambda value: keep / value, total)
            from_old = plane + A_LOW[step - 1]
            for part in range(3):
                twice = tiles.each(lambda value: value + value, tiles.load(src, part, plane + S_LOW))
                near_old = [tiles.load(old, part, from_old + move) for move in (0, 1, -1)]
                moved = pull(tiles, twice, weights, *near_old)
                tiles.store(target, (part, at), tiles.each(lambda value, by: value * by, moved, scale))

        loop_in_pairs(planes + A_LOW[step] + A_HIGH[step], body)

    def first_nu(at):
        marked = members(tiles.load(marks, at))
        base, slope = choose(marked, base_of), [choose(marked, slope_of[knot]) for knot in range(KNOTS)]
        whole_slope = slope[0]
        tiles.store(bases, (at,), base)
        for knot in range(KNOTS):
            tiles.store(slopes, (knot, at), slope[knot])
            if knot:
                whole_slope = tiles.each(lambda one, other: one + other, whole_slope, slope[knot])
        tiles.store(slopes, (KNOTS, at), whole_slope)
        value = reluctivity(tiles, flux_squared(tiles, a0, at), base, lambda knot: slope[knot], whole_slope, False)
        keep = inside(at - G_LOW)
        tiles.store(nu, (at,), tiles.each(lambda one: one * keep, value))

    loop_in_pairs(planes + G_LOW + G_HIGH, first_nu)
    fields = (a0, a1)
    for step in range(1, ITERS_B + 1):
        old, new = fields[(step - 1) % 2], fields[step % 2]
        relax_into(new, step, old)
        last = step == ITERS_B
        lower = NUD_LOW if last else A_LOW[step + 1] + 1
        upper = NUD_HIGH if last else A_HIGH[step + 1] + 1

        def next_nu(at):
            plane = at - lower
            known = plane + G_LOW
            value = reluctivity(
                tiles, flux_squared(tiles, new, plane + A_LOW[step]), tiles.load(bases, known),
                lambda knot: tiles.load(slopes, knot, known), tiles.load(slopes, KNOTS, known), last,
            )
            keep = inside(plane)
            tiles.store(nud_out if last else nu, (at,), tiles.each(lambda one: one * keep, value))

        loop_in_pairs(planes + lower + upper, next_nu)

    def sigma_at(at):
        marked = members(tiles.load(marks, at - (ITERS_R - 1) + G_LOW))
        tiles.store(sigma_out, (at,), choose(marked, sigma_of))

    loop_in_pairs(planes + 2 * (ITERS_R - 1), sigma_at)
    own_rows = pl.ds(pl.multiple_of(mine * rows_each, rows_each), rows_each)
    final = fields[ITERS_B % 2]
    for part in range(3):
        field_out[part] = final[part, A_LOW[ITERS_B]:A_LOW[ITERS_B] + planes, own_rows, :]


def planes_of(ref, first, count):
    return ref.at[:, :, :, pl.ds(first, count)]


class Ripple:
    def __init__(self, rows, lanes, harmonic_numbers, count, sides, answer):
        self.sides, self.answer, self.tiles = sides, answer, Tiles(rows, lanes)
        first = lax.axis_index("harm") * count
        self.omegas = [omega_step * harmonic_numbers[first + at].astype(jnp.float32) for at in range(count)]

    def prepare(self, nud, sigma, slot, keep):
        tiles, near = self.tiles, slot + NUD_LOW - 1
        weights, total = double_couplings(tiles, *(tiles.load(nud, near + move) for move in (0, 1, -1)))
        for number, weight in enumerate(weights):
            tiles.store(self.sides, (number, slot), tiles.each(lambda value: 0.5 * value, weight))
        total = tiles.each(lambda value: 0.5 * value, total)
        square = tiles.each(lambda value: value * value, total)
        conduct = tiles.load(sigma, slot)
        for harmonic, omega in enumerate(self.omegas):
            damp = tiles.each(lambda value: omega * value, conduct)
            inverse = tiles.each(lambda one, other: keep / (one + other * other), square, damp)
            for part, value in enumerate((total, damp)):
                scaled = tiles.each(lambda one, other: one * other, value, inverse)
                tiles.store(self.answer, (harmonic, part, slot), scaled)

    def sweep(self, slot, old, source, put, turned_round=0):
        tiles, loss = self.tiles, None
        weights = [tiles.load(self.sides, number, slot) for number in (turned_round, 1 - turned_round, 2, 3, 4, 5)]
        for harmonic in range(len(self.omegas)):
            straight, turned = (tiles.load(self.answer, harmonic, part, slot) for part in range(2))
            power = None
            for part in range(3):
                both = []
                for piece in range(2):
                    lead = (harmonic, piece, part)
                    near_old = [tiles.load(ref, *lead, at) for ref, at in old]
                    both.append(pull(tiles, tiles.load(source[0], *lead, source[1]), weights, *near_old))
                real = tiles.each(lambda re, im, a, b: re * a + im * b, *both, straight, turned)
                imag = tiles.each(lambda re, im, a, b: im * a - re * b, *both, straight, turned)
                for piece, value in enumerate((real, imag)):
                    tiles.store(put[0], (harmonic, piece, part, put[1]), value)
                squared = tiles.each(lambda re, im: re * re + im * im, real, imag)
                power = tiles.each(lambda one, other: one + other, power, squared) if part else squared
            factor = 0.5 * self.omegas[harmonic] * self.omegas[harmonic]
            scaled = tiles.each(lambda value: factor * value, power)
            loss = tiles.each(lambda one, other: one + other, loss, scaled) if loss else scaled
        return loss


class Side:
    def __init__(self, planes, high):
        pick = lambda above, below: jnp.where(high, above, below)
        self.turned_round = pick(1, 0)
        self.own, self.second = pick(planes - 1, 0), pick(planes - 2, 1)
        self.beyond_slot, self.own_slot, self.second_slot = pick(planes + 1, 0), pick(planes, 1), pick(planes - 1, 2)
        self.halo, self.far_halo = pick(0, 1), pick(1, 0)
        self.third = pick(planes - 3, 2)


def first_on_side(ripple, side, start, source, halo_start, halo_source, put_beyond, put_own):
    ripple.sweep(
        side.beyond_slot, [(halo_start, side.halo), (start, side.own), (halo_start, side.far_halo)], (halo_source, 0),
        put_beyond, side.turned_round,
    )
    ripple.sweep(
        side.own_slot, [(start, side.own), (start, side.second), (halo_start, side.halo)], (source, side.own),
        put_own, side.turned_round,
    )


def inner_kernel(
    meshes, harmonic_numbers, nud, sigma, start, source, paired_start, paired_source, ripple_out, edge_out, loss_out,
    sides, answer, r1, r2, sems
):
    count, planes = start.shape[0], start.shape[3]
    here = lax.axis_index("mesh")
    odd = is_odd()
    ripple = Ripple(*start.shape[4:], harmonic_numbers, count, sides, answer)
    tiles = ripple.tiles

    def prepare(slot):
        low_ok = jnp.logical_or(slot > 0, here > 0)
        high_ok = jnp.logical_or(slot < planes + 1, here < meshes - 1)
        ripple.prepare(nud, sigma, slot, jnp.where(jnp.logical_and(low_ok, high_ok), 1.0, 0.0))

    def drain(plane):
        return pltpu.make_async_copy(planes_of(r2, plane, 1), planes_of(ripple_out, plane, 1), sems.at[plane])

    def first(plane, carry):
        ripple.sweep(
            plane + 1, [(start, plane), (start, plane + 1), (start, plane - 1)], (source, plane), (r1, plane + 1)
        )
        return carry

    def second(plane, carry):
        loss = ripple.sweep(
            plane + 1, [(r1, plane + 1), (r1, plane + 2), (r1, plane)], (source, plane), (r2, plane)
        )
        tiles.store(loss_out, (plane,), tiles.each(lambda one, other: one * other, tiles.load(sigma, plane + 1), loss))
        drain(plane).start()
        return carry

    def finish(plane, carry):
        drain(plane).wait()
        return carry

    near, far = Side(planes, jnp.logical_not(odd)), Side(planes, odd)
    loop_in_pairs(planes + 2, prepare)
    lax.fori_loop(1, planes - 1, first, 0)
    first_on_side(
        ripple, near, start, source, paired_start, paired_source, (r1, near.beyond_slot), (r1, near.own_slot)
    )
    begin, end = jnp.where(odd, 0, 2), jnp.where(odd, planes - 2, planes)
    lax.fori_loop(begin, end, second, 0)
    for onto, plane in enumerate((far.second, far.third)):
        edge_out[:, :, :, onto] = r1[:, :, :, plane + 1]
    lax.fori_loop(begin, end, finish, 0)


def outer_kernel(
    shares, harmonic_numbers, sigma, start, source, first_apart, second_apart, edge, sides, answer, loss_in, ripple_in,
    ripple_out, *refs
):
    losses, (halo_start, halo_source, r1, r2, loss, sems, halo_sems) = refs[:shares], refs[shares:]
    count, planes = start.shape[0], start.shape[3]
    rows, lanes = start.shape[4:]

    def halo(origin):
        return [
            pltpu.make_async_copy(planes_of(origin, 0, 2), halo_start, halo_sems.at[0]),
            pltpu.make_async_copy(planes_of(origin, 2, 1), halo_source, halo_sems.at[1]),
        ]

    for second, origin in ((False, first_apart), (True, second_apart)):

        @pl.when(is_second() == second)
        def bring_halo():
            for copy in halo(origin):
                copy.start()
            for copy in halo(origin):
                copy.wait()

    far = Side(planes, is_odd())
    ripple = Ripple(rows, lanes, harmonic_numbers, count, sides, answer)
    tiles = ripple.tiles
    first_on_side(ripple, far, start, source, halo_start, halo_source, (r1, 0), (r1, 1))

    def drain(slot, plane):
        return pltpu.make_async_copy(planes_of(r2, slot, 1), planes_of(ripple_out, plane, 1), sems.at[slot])

    steps = (
        (far.own, far.own_slot, [(r1, 1), (edge, 0), (r1, 0)]),
        (far.second, far.second_slot, [(edge, 0), (edge, 1), (r1, 1)]),
    )
    for at, (plane, slot, old) in enumerate(steps):
        added = ripple.sweep(slot, old, (source, plane), (r2, at), far.turned_round)
        drain(at, plane).start()
        tiles.store(loss, (at,), tiles.each(lambda one, other: one * other, tiles.load(sigma, slot), added))
    rows_each = rows // shares
    for turn in range(shares):
        owner = lax.rem(lax.axis_index("harm") + turn, shares)
        part = pl.ds(pl.multiple_of(owner * rows_each, rows_each), rows_each)
        losses[turn][...] = loss_in[:, part, :]
        for at, (plane, unused, unused_too) in enumerate(steps):
            losses[turn][plane] = loss[at, part, :]
    for at, (plane, unused, unused_too) in enumerate(steps):
        drain(at, plane).wait()


def call(kernel, operands, in_specs, out_shapes, out_specs, scratch, name, work=0, aliases={}, room=0):
    f32 = jnp.float32
    shapes = [o.shape for o, spec in zip(operands, in_specs) if spec is VMEM]
    shapes += [shape for shape, spec in zip(out_shapes, out_specs) if spec is VMEM]
    shapes += [shape for shape in scratch if isinstance(shape, tuple)]
    held = 4 * sum(math.prod(shape) for shape in shapes)
    return pl.pallas_call(
        kernel,
        out_shape=[jax.ShapeDtypeStruct(shape, f32) for shape in out_shapes],
        in_specs=in_specs,
        out_specs=out_specs,
        scratch_shapes=[pltpu.VMEM(shape, f32) if isinstance(shape, tuple) else shape for shape in scratch],
        compiler_params=pltpu.CompilerParams(vmem_limit_bytes=room or held + 4 * 2**20),
        cost_estimate=pl.CostEstimate(flops=work * 300, bytes_accessed=work, transcendentals=0),
        input_output_aliases=aliases,
        name=name,
    )(*operands)


def body(
    meshes, shares, bias_source, bias_start, region, table_index, bh_base, bh_slope, conductivity, harmonic_numbers,
    ripple_source, ripple_start,
):
    unused, planes, rows_each, lanes = bias_start.shape
    rows = rows_each * shares
    count = ripple_start.shape[0]
    near = [(i, i + 1) for i in range(0, meshes - 1, 2)]
    far = [(i, i + 1) for i in range(1, meshes - 1, 2)]
    near += [(j, i) for i, j in near]
    far += [(j, i) for i, j in far]
    turned = [[(i, (i + turn) % shares) for i in range(shares)] for turn in range(1, shares)]

    def around(block):
        return [block] + [lax.ppermute(block, "harm", pairs) for pairs in turned]

    whole, apart, paired, token = call(
        pack_kernel, (bias_start, bias_source, region), [ANY] * 3,
        [(7 * planes, rows_each, lanes), (HIGH_SIZE, rows_each, lanes), (HIGH_SIZE, rows_each, lanes), TILE], [VMEM] * 4,
        [pltpu.VMEM(region.shape, region.dtype), pltpu.SemaphoreType.DMA((7,))], "pack", room=PACK_ROOM,
    )
    wholes = around(whole)
    aparts = around(lax.ppermute(apart, "mesh", far))
    edge = ripple_start.shape[:3] + (3, rows, lanes)
    near_edges = [edge[:3] + (size, rows, lanes) for size in (2, 1)]
    ripple_first, paired_start, paired_source, token = call(
        first_edges_kernel, (ripple_start, ripple_source, token), [ANY] * 3,
        [edge] + near_edges + [TILE], [ANY] * 3 + [VMEM],
        [edge, edge, pltpu.SemaphoreType.DMA((3,)), pltpu.SemaphoreType.DMA((4,))], "first_edges", room=RP_ROOM,
    )
    ripple_second, = call(
        second_edges_kernel, (ripple_start, ripple_source, token), [ANY] * 3, [edge], [ANY],
        [edge, pltpu.SemaphoreType.DMA((3,))], "second_edges", room=RP_ROOM,
    )
    others, token = call(
        pair_kernel, (*wholes[1:], aparts[0]), [VMEM] * (shares - 1) + [ANY],
        [(shares - 1, HIGH_SIZE, rows_each, lanes), TILE], [VMEM] * 2, [], "pair",
    )
    ripple_paireds = call(
        near_edges_kernel, (ripple_start, ripple_source, token, paired_start, paired_source), [ANY] * 5,
        near_edges, [ANY] * 2, [edge, edge, pltpu.SemaphoreType.DMA((4,))], "near_edges", aliases={3: 0, 4: 1},
        room=NEAR_ROOM,
    )
    paireds = [lax.ppermute(paired, "mesh", near), lax.ppermute(others, "mesh", near)]
    first_pairs, second_pairs = ([pair for pair in far if min(pair) % 4 == kind] for kind in (1, 3))
    ripple_first = lax.ppermute(ripple_first, "mesh", first_pairs)
    ripple_second = lax.ppermute(ripple_second, "mesh", second_pairs)
    ripple_paireds = [lax.ppermute(part, "mesh", near) for part in ripple_paireds]

    known = (planes + G_LOW + G_HIGH, rows, lanes)
    field, nud, sigma = call(
        functools.partial(bias_kernel, shares, meshes),
        (*wholes, *aparts, *paireds, table_index, bh_base, bh_slope, conductivity),
        [VMEM] * (2 * shares + 2) + [SMEM] * 4,
        [
            bias_start.shape, (planes + NUD_LOW + NUD_HIGH, rows, lanes), (planes + 2 * (ITERS_R - 1), rows, lanes)
        ],
        [VMEM] * 3,
        [
            (3, planes + A_LOW[0] + A_HIGH[0], rows, lanes),
            (3, planes + A_LOW[1] + A_HIGH[1], rows, lanes),
            (3, planes + S_LOW + S_HIGH, rows, lanes),
            known,
            known,
            (KNOTS + 1, *known),
            known,
        ],
        "bias",
        BIAS_WORK,
    )

    lead = ripple_start.shape[:3]
    slots = (planes + 2, rows, lanes)
    ripple, edge, inner_loss, sides, answer = call(
        functools.partial(inner_kernel, meshes),
        (harmonic_numbers, nud, sigma, ripple_start, ripple_source, *ripple_paireds), [SMEM] + [VMEM] * 6,
        [ripple_start.shape, lead + (2, rows, lanes), (planes, rows, lanes), (6, *slots), (count, 2, *slots)],
        [ANY] + [VMEM] * 4, [lead + slots, lead + (planes, rows, lanes), pltpu.SemaphoreType.DMA((planes,))],
        "inner_ripple",
    )
    ripple, *losses = call(
        functools.partial(outer_kernel, shares),
        (
            harmonic_numbers, sigma, ripple_start, ripple_source, ripple_first, ripple_second, edge, sides, answer,
            inner_loss, ripple,
        ),
        [SMEM] + [VMEM] * 3 + [ANY] * 2 + [VMEM] * 4 + [ANY],
        [ripple_start.shape] + [(planes, rows_each, lanes)] * shares, [ANY] + [VMEM] * shares,
        [lead + (size, rows, lanes) for size in (2, 1, 2, 2)] + [(2, rows, lanes)]
        + [pltpu.SemaphoreType.DMA((2,))] * 2,
        "outer_ripple", aliases={10: 0},
    )
    loss = losses[0]
    for turn, pairs in enumerate(turned):
        loss = loss + lax.ppermute(losses[turn + 1], "harm", pairs)
    return field, ripple, loss


def solution(mesh):
    return jax.shard_map(
        functools.partial(body, mesh.shape["mesh"], mesh.shape["harm"]),
        mesh=mesh,
        in_specs=(
            P(None, "mesh", "harm", None),
            P(None, "mesh", "harm", None),
            P("mesh", "harm", None),
            P(),
            P(),
            P(),
            P(),
            P(),
            P("harm", None, None, "mesh", None, None),
            P("harm", None, None, "mesh", None, None),
        ),
        out_specs=(
            P(None, "mesh", "harm", None),
            P("harm", None, None, "mesh", None, None),
            P("mesh", "harm", None),
        ),
        check_vma=False,
    )
```

```python
import functools
import math

import jax
import jax.numpy as jnp
from jax import lax
from jax.experimental import pallas as pl
from jax.experimental.pallas import tpu as pltpu
from jax.sharding import PartitionSpec as P

ITERS_B = 2
ITERS_R = 2
KNOTS = 8
MATS = 4

kappa = 0.05
knot_step = 1.5
soft_width = 0.5
omega_step = 0.25
CAP = 80.0

NUD_LOW, NUD_HIGH = ITERS_R, ITERS_R
A_LOW = [NUD_LOW + ITERS_B - step for step in range(ITERS_B + 1)]
A_HIGH = [NUD_HIGH + 1 + 2 * (ITERS_B - step) for step in range(ITERS_B + 1)]
S_LOW, S_HIGH = A_LOW[1], A_HIGH[1]
G_LOW, G_HIGH = A_LOW[0], A_HIGH[0] - 1

BIAS_WORK = 20000000
PACK_ROOM = 62 * 2**20
RP_ROOM = 58 * 2**20
NEAR_ROOM = 58 * 2**20
VMEM = pl.BlockSpec(memory_space=pltpu.VMEM)
SMEM = pl.BlockSpec(memory_space=pltpu.SMEM)
ANY = pl.BlockSpec(memory_space=pl.ANY)


TILE = (8, 128)


class Tiles:
    def __init__(self, rows, lanes):
        self.grid = (rows // TILE[0], lanes // TILE[1])
        self.spots = [(i, j) for i in range(self.grid[0]) for j in range(self.grid[1])]
        self.at_end, self.at_start = [], []
        for axis in range(2):
            place = lax.broadcasted_iota(jnp.int32, TILE, axis)
            self.at_end.append(place == TILE[axis] - 1)
            self.at_start.append(place == 0)

    def where(self, spot):
        return (slice(spot[0] * TILE[0], (spot[0] + 1) * TILE[0]), slice(spot[1] * TILE[1], (spot[1] + 1) * TILE[1]))

    def load(self, ref, *lead):
        return {spot: ref[lead + self.where(spot)] for spot in self.spots}

    def store(self, ref, lead, values):
        for spot in self.spots:
            ref[lead + self.where(spot)] = values[spot]

    def each(self, function, *values):
        return {spot: function(*(value[spot] for value in values)) for spot in self.spots}

    def side(self, step, axis):
        return (self.at_end if step > 0 else self.at_start)[axis]

    def is_edge(self, spot, step, axis):
        return spot[axis] == (self.grid[axis] - 1 if step > 0 else 0)

    def move(self, values, step, axis, fill):
        rolled = self.each(lambda tile: pltpu.roll(tile, TILE[axis] - 1 if step > 0 else 1, axis), values)
        side, moved = self.side(step, axis), {}
        for spot in self.spots:
            if self.is_edge(spot, step, axis):
                moved[spot] = jnp.where(side, 0.0, rolled[spot]) if fill else rolled[spot]
            else:
                other = (spot[0] + step, spot[1]) if axis == 0 else (spot[0], spot[1] + step)
                moved[spot] = jnp.where(side, rolled[other], rolled[spot])
        return moved

    def inner(self, values, step, axis):
        side = self.side(step, axis)
        return {
            spot: jnp.where(side, 0.0, values[spot]) if self.is_edge(spot, step, axis) else values[spot]
            for spot in self.spots
        }


SIDES = ((1, 0), (-1, 0), (1, 1), (-1, 1))


def double_couplings(tiles, center, above, below):
    add = lambda one, other: one + other
    weights = [tiles.each(add, center, above), tiles.each(add, center, below)]
    total = tiles.each(add, *weights)
    for step, axis in SIDES:
        weight = tiles.each(add, center, tiles.move(center, step, axis, True))
        total = tiles.each(add, total, weight)
        weights.append(tiles.inner(weight, step, axis))
    return weights, tiles.each(lambda value: value + 2.0 * kappa, total)


def pull(tiles, start, weights, center, above, below):
    moved = [above, below] + [tiles.move(center, step, axis, False) for step, axis in SIDES]
    total = start
    for weight, other in zip(weights, moved):
        total = tiles.each(lambda so_far, w, value: so_far + w * value, total, weight, other)
    return total


def flux_squared(tiles, field, plane):
    ax, ay, az = (tiles.load(field, part, plane) for part in range(3))
    ay_first, az_first = tiles.load(field, 1, plane + 1), tiles.load(field, 2, plane + 1)
    ax_second, az_second = tiles.move(ax, 1, 0, True), tiles.move(az, 1, 0, True)
    ax_third, ay_third = tiles.move(ax, 1, 1, True), tiles.move(ay, 1, 1, True)

    def square(x, y, z, y1, z1, x2, z2, x3, y3):
        flux_one = (z2 - z) - (y3 - y)
        flux_two = (x3 - x) - (z1 - z)
        flux_three = (y1 - y) - (x2 - x)
        return flux_one * flux_one + flux_two * flux_two + flux_three * flux_three

    return tiles.each(square, ax, ay, az, ay_first, az_first, ax_second, az_second, ax_third, ay_third)


def reluctivity(tiles, flux_sq, base, slope_of, slope_total, incremental):
    doubled = tiles.each(lambda value: value * (1.0 / soft_width), flux_sq)
    excess = tiles.each(lambda value: jnp.maximum(value - CAP, 0.0), doubled)
    floor = tiles.each(lambda value: jnp.exp(-value), excess)
    rising = tiles.each(lambda value: jnp.exp(jnp.minimum(value, CAP)), doubled)
    nu = tiles.each(lambda start, slope, value: start + slope * value, base, slope_total, excess)
    slope_sum = None
    for knot in range(KNOTS):
        factor = math.exp(-knot_step * knot / soft_width)
        slope = slope_of(knot)
        high = tiles.each(lambda value: value * factor, rising)
        both = tiles.each(lambda one, other: one + other, high, floor)
        nu = tiles.each(lambda so_far, weight, value: so_far + weight * jnp.log(value), nu, slope, both)
        if incremental:
            part = tiles.each(lambda weight, one, other: weight * (one / other), slope, high, both)
            slope_sum = tiles.each(lambda one, other: one + other, slope_sum, part) if knot else part
    if incremental:
        nu = tiles.each(lambda value, s, slope: value + (2.0 / soft_width) * (s * slope), nu, flux_sq, slope_sum)
    return nu


def loop_in_pairs(count, body):
    def step(at, carry):
        body(2 * at)
        body(2 * at + 1)
        return carry

    lax.fori_loop(0, count // 2, step, 0)
    if count % 2:
        body(count - 1)


LOW_SIZE = 3 * (A_LOW[0] + S_LOW) + G_LOW
HIGH_SIZE = 3 * (A_HIGH[0] + S_HIGH) + G_HIGH - 2


def edge_parts(planes, low):
    halo_of = ((A_LOW if low else A_HIGH)[0], S_LOW if low else S_HIGH, G_LOW if low else G_HIGH)
    at, parts = 0, []
    for array in range(7):
        halo = halo_of[0 if array < 3 else 1 if array < 6 else 2]
        if not low and array in (0, 3):
            halo -= 1
        parts.append((array * planes + (planes - halo if low else 0), at, halo))
        at += halo
    return parts


def write_edge(target, whole, low):
    for first, at, halo in edge_parts(whole.shape[0] // 7, low):
        target[at:at + halo] = whole[first:first + halo]


def is_odd():
    return lax.rem(lax.axis_index("mesh"), 2) == 1


def pack_kernel(start, source, region, whole, apart, paired, token, marks, sems):
    token[...] = jnp.zeros(token.shape, token.dtype)
    planes = region.shape[0]
    copies = [pltpu.make_async_copy(region, marks, sems.at[0])]
    for part in range(3):
        for at, origin in ((part, start), (3 + part, source)):
            target = whole.at[at * planes:(at + 1) * planes]
            copies.append(pltpu.make_async_copy(origin.at[part], target, sems.at[at + 1]))
    for copy in copies:
        copy.start()
    for copy in copies:
        copy.wait()
    whole[6 * planes:] = marks[...].astype(jnp.float32)
    for odd in (False, True):
        pl.when(is_odd() == odd)(functools.partial(write_edge, apart, whole, odd))
        pl.when(is_odd() == odd)(functools.partial(write_edge, paired, whole, not odd))


def pair_kernel(*refs):
    wholes, (paired, token) = refs[:-3], refs[-2:]
    token[...] = jnp.zeros(token.shape, token.dtype)
    for odd in (False, True):

        @pl.when(is_odd() == odd)
        def write():
            for turn, whole in enumerate(wholes):
                write_edge(paired.at[turn], whole, not odd)


def is_second():
    return lax.rem(lax.axis_index("mesh") + 1, 4) < 2


def send_edges(start, source, buffer, target, top, sems):
    planes = start.shape[3]
    ways_in = []
    for part, (origin, count, onto) in enumerate(((start, 2, 0), (source, 1, 2))):
        at = jnp.where(top, planes - count, 0)
        ways_in.append(
            pltpu.make_async_copy(planes_of(origin, at, count), planes_of(buffer, onto, count), sems.at[part])
        )
        ways_in[-1].start()
    for copy in ways_in:
        copy.wait()
    way_out = pltpu.make_async_copy(buffer, target, sems.at[2])
    way_out.start()
    way_out.wait()


def send_near_edges(start, source, targets, buffers, sems):
    planes = start.shape[3]
    ways = []
    for number, (origin, buffer, target) in enumerate(zip((start, source), buffers, targets)):
        count = target.shape[3]
        first = jnp.where(is_odd(), 0, planes - count)
        held = planes_of(buffer, 0, count)
        ways.append(
            (
                pltpu.make_async_copy(planes_of(origin, first, count), held, sems.at[2 * number]),
                pltpu.make_async_copy(held, target, sems.at[2 * number + 1]),
            )
        )
    for way_in, unused in ways:
        way_in.start()
    for way_in, way_out in ways:
        way_in.wait()
        way_out.start()
    for unused, way_out in ways:
        way_out.wait()


def first_edges_kernel(
    start, source, after, apart, paired_start, paired_source, token, buffer, other_buffer, sems, near_sems
):
    token[...] = jnp.zeros(token.shape, token.dtype)

    @pl.when(jnp.logical_not(is_second()))
    def send_apart():
        send_edges(start, source, buffer, apart, is_odd(), sems)

    @pl.when(is_second())
    def send_near():
        send_near_edges(start, source, (paired_start, paired_source), (buffer, other_buffer), near_sems)


def near_edges_kernel(start, source, after, start_in, source_in, paired_start, paired_source, buffer, other_buffer, sems):
    @pl.when(jnp.logical_not(is_second()))
    def send_near():
        send_near_edges(start, source, (paired_start, paired_source), (buffer, other_buffer), sems)


def second_edges_kernel(start, source, after, apart_in, apart, buffer, sems):
    @pl.when(is_second())
    def send_apart():
        send_edges(start, source, buffer, apart, is_odd(), sems)


def bias_kernel(shares, meshes, *refs):
    wholes, aparts, (paired, others) = refs[:shares], refs[shares:2 * shares], refs[2 * shares:2 * shares + 2]
    paireds = [paired] + [others.at[at] for at in range(shares - 1)]
    table_index, bh_base, bh_slope, conductivity, field_out, nud_out, sigma_out = refs[2 * shares + 2:2 * shares + 9]
    a0, a1, src, marks, nu, slopes, bases = refs[2 * shares + 9:]
    planes = wholes[0].shape[0] // 7
    rows_each, lanes = wholes[0].shape[1:]
    rows = rows_each * shares
    mine = lax.axis_index("harm")
    here = lax.axis_index("mesh")
    arrays = [(a0.at[part], A_LOW[0]) for part in range(3)]
    arrays += [(src.at[part], S_LOW) for part in range(3)] + [(marks, G_LOW)]
    for turn in range(shares):
        owner = lax.rem(mine + shares - turn, shares)
        at = pl.ds(pl.multiple_of(owner * rows_each, rows_each), rows_each)

        def fill(low, high):
            for (target, onto), (unused, first, halo) in zip(arrays, edge_parts(planes, True)):
                target[0:halo, at, :] = low[first:first + halo]
            for (target, onto), (unused, first, halo) in zip(arrays, edge_parts(planes, False)):
                target[onto + planes:onto + planes + halo, at, :] = high[first:first + halo]

        for number, (target, onto) in enumerate(arrays):
            target[onto:onto + planes, at, :] = wholes[turn][number * planes:(number + 1) * planes]
        pl.when(is_odd())(functools.partial(fill, paireds[turn], aparts[turn]))
        pl.when(jnp.logical_not(is_odd()))(functools.partial(fill, aparts[turn], paireds[turn]))

    tiles = Tiles(rows, lanes)
    tables = [table_index[member] for member in range(MATS)]
    base_of = [bh_base[table] for table in tables]
    slope_of = [[soft_width * bh_slope[table, knot] for table in tables] for knot in range(KNOTS)]
    sigma_of = [conductivity[member] for member in range(MATS)]

    def inside(plane):
        low_ok = jnp.logical_or(plane >= 0, here > 0)
        high_ok = jnp.logical_or(plane < planes, here < meshes - 1)
        return jnp.where(jnp.logical_and(low_ok, high_ok), 1.0, 0.0)

    def choose(marks_are, values):
        def one(*marked):
            chosen = jnp.where(marked[0], values[1], values[0])
            for member in range(2, MATS):
                chosen = jnp.where(marked[member - 1], values[member], chosen)
            return chosen

        return tiles.each(one, *marks_are)

    def members(mark):
        return [tiles.each(lambda value: value == float(member), mark) for member in range(1, MATS)]

    def relax_into(target, step, old):
        def body(at):
            plane = at - A_LOW[step]
            near = at + 1
            weights, total = double_couplings(
                tiles, tiles.load(nu, near), tiles.load(nu, near + 1), tiles.load(nu, near - 1)
            )
            keep = inside(plane)
            scale = tiles.each(lambda value: keep / value, total)
            from_old = plane + A_LOW[step - 1]
            for part in range(3):
                twice = tiles.each(lambda value: value + value, tiles.load(src, part, plane + S_LOW))
                near_old = [tiles.load(old, part, from_old + move) for move in (0, 1, -1)]
                moved = pull(tiles, twice, weights, *near_old)
                tiles.store(target, (part, at), tiles.each(lambda value, by: value * by, moved, scale))

        loop_in_pairs(planes + A_LOW[step] + A_HIGH[step], body)

    def first_nu(at):
        marked = members(tiles.load(marks, at))
        base, slope = choose(marked, base_of), [choose(marked, slope_of[knot]) for knot in range(KNOTS)]
        whole_slope = slope[0]
        tiles.store(bases, (at,), base)
        for knot in range(KNOTS):
            tiles.store(slopes, (knot, at), slope[knot])
            if knot:
                whole_slope = tiles.each(lambda one, other: one + other, whole_slope, slope[knot])
        tiles.store(slopes, (KNOTS, at), whole_slope)
        value = reluctivity(tiles, flux_squared(tiles, a0, at), base, lambda knot: slope[knot], whole_slope, False)
        keep = inside(at - G_LOW)
        tiles.store(nu, (at,), tiles.each(lambda one: one * keep, value))

    loop_in_pairs(planes + G_LOW + G_HIGH, first_nu)
    fields = (a0, a1)
    for step in range(1, ITERS_B + 1):
        old, new = fields[(step - 1) % 2], fields[step % 2]
        relax_into(new, step, old)
        last = step == ITERS_B
        lower = NUD_LOW if last else A_LOW[step + 1] + 1
        upper = NUD_HIGH if last else A_HIGH[step + 1] + 1

        def next_nu(at):
            plane = at - lower
            known = plane + G_LOW
            value = reluctivity(
                tiles, flux_squared(tiles, new, plane + A_LOW[step]), tiles.load(bases, known),
                lambda knot: tiles.load(slopes, knot, known), tiles.load(slopes, KNOTS, known), last,
            )
            keep = inside(plane)
            tiles.store(nud_out if last else nu, (at,), tiles.each(lambda one: one * keep, value))

        loop_in_pairs(planes + lower + upper, next_nu)

    def sigma_at(at):
        marked = members(tiles.load(marks, at - (ITERS_R - 1) + G_LOW))
        tiles.store(sigma_out, (at,), choose(marked, sigma_of))

    loop_in_pairs(planes + 2 * (ITERS_R - 1), sigma_at)
    own_rows = pl.ds(pl.multiple_of(mine * rows_each, rows_each), rows_each)
    final = fields[ITERS_B % 2]
    for part in range(3):
        field_out[part] = final[part, A_LOW[ITERS_B]:A_LOW[ITERS_B] + planes, own_rows, :]


def planes_of(ref, first, count):
    return ref.at[:, :, :, pl.ds(first, count)]


class Ripple:
    def __init__(self, rows, lanes, harmonic_numbers, count, sides, answer):
        self.sides, self.answer, self.tiles = sides, answer, Tiles(rows, lanes)
        first = lax.axis_index("harm") * count
        self.omegas = [omega_step * harmonic_numbers[first + at].astype(jnp.float32) for at in range(count)]

    def prepare(self, nud, sigma, slot, keep):
        tiles, near = self.tiles, slot + NUD_LOW - 1
        weights, total = double_couplings(tiles, *(tiles.load(nud, near + move) for move in (0, 1, -1)))
        for number, weight in enumerate(weights):
            tiles.store(self.sides, (number, slot), tiles.each(lambda value: 0.5 * value, weight))
        total = tiles.each(lambda value: 0.5 * value, total)
        square = tiles.each(lambda value: value * value, total)
        conduct = tiles.load(sigma, slot)
        for harmonic, omega in enumerate(self.omegas):
            damp = tiles.each(lambda value: omega * value, conduct)
            inverse = tiles.each(lambda one, other: keep / (one + other * other), square, damp)
            for part, value in enumerate((total, damp)):
                scaled = tiles.each(lambda one, other: one * other, value, inverse)
                tiles.store(self.answer, (harmonic, part, slot), scaled)

    def sweep(self, slot, old, source, put, turned_round=0):
        tiles, loss = self.tiles, None
        weights = [tiles.load(self.sides, number, slot) for number in (turned_round, 1 - turned_round, 2, 3, 4, 5)]
        for harmonic in range(len(self.omegas)):
            straight, turned = (tiles.load(self.answer, harmonic, part, slot) for part in range(2))
            power = None
            for part in range(3):
                both = []
                for piece in range(2):
                    lead = (harmonic, piece, part)
                    near_old = [tiles.load(ref, *lead, at) for ref, at in old]
                    both.append(pull(tiles, tiles.load(source[0], *lead, source[1]), weights, *near_old))
                real = tiles.each(lambda re, im, a, b: re * a + im * b, *both, straight, turned)
                imag = tiles.each(lambda re, im, a, b: im * a - re * b, *both, straight, turned)
                for piece, value in enumerate((real, imag)):
                    tiles.store(put[0], (harmonic, piece, part, put[1]), value)
                squared = tiles.each(lambda re, im: re * re + im * im, real, imag)
                power = tiles.each(lambda one, other: one + other, power, squared) if part else squared
            factor = 0.5 * self.omegas[harmonic] * self.omegas[harmonic]
            scaled = tiles.each(lambda value: factor * value, power)
            loss = tiles.each(lambda one, other: one + other, loss, scaled) if loss else scaled
        return loss


class Side:
    def __init__(self, planes, high):
        pick = lambda above, below: jnp.where(high, above, below)
        self.turned_round = pick(1, 0)
        self.own, self.second = pick(planes - 1, 0), pick(planes - 2, 1)
        self.beyond_slot, self.own_slot, self.second_slot = pick(planes + 1, 0), pick(planes, 1), pick(planes - 1, 2)
        self.halo, self.far_halo = pick(0, 1), pick(1, 0)
        self.third = pick(planes - 3, 2)


def first_on_side(ripple, side, start, source, halo_start, halo_source, put_beyond, put_own, source_at=0):
    ripple.sweep(
        side.beyond_slot, [(halo_start, side.halo), (start, side.own), (halo_start, side.far_halo)],
        (halo_source, source_at),
        put_beyond, side.turned_round,
    )
    ripple.sweep(
        side.own_slot, [(start, side.own), (start, side.second), (halo_start, side.halo)], (source, side.own),
        put_own, side.turned_round,
    )


def inner_kernel(
    meshes, harmonic_numbers, nud, sigma, start, source, paired_start, paired_source, ripple_out, edge_out, loss_out,
    sides, answer, r1, r2, sems
):
    count, planes = start.shape[0], start.shape[3]
    here = lax.axis_index("mesh")
    odd = is_odd()
    ripple = Ripple(*start.shape[4:], harmonic_numbers, count, sides, answer)
    tiles = ripple.tiles

    def prepare(slot):
        low_ok = jnp.logical_or(slot > 0, here > 0)
        high_ok = jnp.logical_or(slot < planes + 1, here < meshes - 1)
        ripple.prepare(nud, sigma, slot, jnp.where(jnp.logical_and(low_ok, high_ok), 1.0, 0.0))

    def drain(plane):
        return pltpu.make_async_copy(planes_of(r2, plane, 1), planes_of(ripple_out, plane, 1), sems.at[plane])

    def first(plane, carry):
        ripple.sweep(
            plane + 1, [(start, plane), (start, plane + 1), (start, plane - 1)], (source, plane), (r1, plane + 1)
        )
        return carry

    def second(plane, carry):
        loss = ripple.sweep(
            plane + 1, [(r1, plane + 1), (r1, plane + 2), (r1, plane)], (source, plane), (r2, plane)
        )
        tiles.store(loss_out, (plane,), tiles.each(lambda one, other: one * other, tiles.load(sigma, plane + 1), loss))
        drain(plane).start()
        return carry

    def finish(plane, carry):
        drain(plane).wait()
        return carry

    near, far = Side(planes, jnp.logical_not(odd)), Side(planes, odd)
    loop_in_pairs(planes + 2, prepare)
    lax.fori_loop(1, planes - 1, first, 0)
    first_on_side(
        ripple, near, start, source, paired_start, paired_source, (r1, near.beyond_slot), (r1, near.own_slot)
    )
    begin, end = jnp.where(odd, 0, 2), jnp.where(odd, planes - 2, planes)
    lax.fori_loop(begin, end, second, 0)
    for onto, plane in enumerate((far.second, far.third)):
        edge_out[:, :, :, onto] = r1[:, :, :, plane + 1]
    lax.fori_loop(begin, end, finish, 0)


def outer_kernel(
    shares, harmonic_numbers, sigma, start, source, apart, edge, sides, answer, loss_in, ripple_in,
    ripple_out, *refs
):
    losses, (r1, r2, loss, sems) = refs[:shares], refs[shares:]
    count, planes = start.shape[0], start.shape[3]
    rows, lanes = start.shape[4:]

    far = Side(planes, is_odd())
    ripple = Ripple(rows, lanes, harmonic_numbers, count, sides, answer)
    tiles = ripple.tiles
    first_on_side(ripple, far, start, source, apart, apart, (r1, 0), (r1, 1), 2)

    def drain(slot, plane):
        return pltpu.make_async_copy(planes_of(r2, slot, 1), planes_of(ripple_out, plane, 1), sems.at[slot])

    steps = (
        (far.own, far.own_slot, [(r1, 1), (edge, 0), (r1, 0)]),
        (far.second, far.second_slot, [(edge, 0), (edge, 1), (r1, 1)]),
    )
    for at, (plane, slot, old) in enumerate(steps):
        added = ripple.sweep(slot, old, (source, plane), (r2, at), far.turned_round)
        drain(at, plane).start()
        tiles.store(loss, (at,), tiles.each(lambda one, other: one * other, tiles.load(sigma, slot), added))
    rows_each = rows // shares
    for turn in range(shares):
        owner = lax.rem(lax.axis_index("harm") + turn, shares)
        part = pl.ds(pl.multiple_of(owner * rows_each, rows_each), rows_each)
        losses[turn][...] = loss_in[:, part, :]
        for at, (plane, unused, unused_too) in enumerate(steps):
            losses[turn][plane] = loss[at, part, :]
    for at, (plane, unused, unused_too) in enumerate(steps):
        drain(at, plane).wait()


def call(kernel, operands, in_specs, out_shapes, out_specs, scratch, name, work=0, aliases={}, room=0):
    f32 = jnp.float32
    shapes = [o.shape for o, spec in zip(operands, in_specs) if spec is VMEM]
    shapes += [shape for shape, spec in zip(out_shapes, out_specs) if spec is VMEM]
    shapes += [shape for shape in scratch if isinstance(shape, tuple)]
    held = 4 * sum(math.prod(shape) for shape in shapes)
    return pl.pallas_call(
        kernel,
        out_shape=[jax.ShapeDtypeStruct(shape, f32) for shape in out_shapes],
        in_specs=in_specs,
        out_specs=out_specs,
        scratch_shapes=[pltpu.VMEM(shape, f32) if isinstance(shape, tuple) else shape for shape in scratch],
        compiler_params=pltpu.CompilerParams(vmem_limit_bytes=room or held + 4 * 2**20),
        cost_estimate=pl.CostEstimate(flops=work * 300, bytes_accessed=work, transcendentals=0),
        input_output_aliases=aliases,
        name=name,
    )(*operands)


def body(
    meshes, shares, bias_source, bias_start, region, table_index, bh_base, bh_slope, conductivity, harmonic_numbers,
    ripple_source, ripple_start,
):
    unused, planes, rows_each, lanes = bias_start.shape
    rows = rows_each * shares
    count = ripple_start.shape[0]
    near = [(i, i + 1) for i in range(0, meshes - 1, 2)]
    far = [(i, i + 1) for i in range(1, meshes - 1, 2)]
    near += [(j, i) for i, j in near]
    far += [(j, i) for i, j in far]
    turned = [[(i, (i + turn) % shares) for i in range(shares)] for turn in range(1, shares)]

    def around(block):
        return [block] + [lax.ppermute(block, "harm", pairs) for pairs in turned]

    whole, apart, paired, token = call(
        pack_kernel, (bias_start, bias_source, region), [ANY] * 3,
        [(7 * planes, rows_each, lanes), (HIGH_SIZE, rows_each, lanes), (HIGH_SIZE, rows_each, lanes), TILE], [VMEM] * 4,
        [pltpu.VMEM(region.shape, region.dtype), pltpu.SemaphoreType.DMA((7,))], "pack", room=PACK_ROOM,
    )
    wholes = around(whole)
    aparts = around(lax.ppermute(apart, "mesh", far))
    edge = ripple_start.shape[:3] + (3, rows, lanes)
    near_edges = [edge[:3] + (size, rows, lanes) for size in (2, 1)]
    ripple_apart, paired_start, paired_source, token = call(
        first_edges_kernel, (ripple_start, ripple_source, token), [ANY] * 3,
        [edge] + near_edges + [TILE], [ANY] * 3 + [VMEM],
        [edge, edge, pltpu.SemaphoreType.DMA((3,)), pltpu.SemaphoreType.DMA((4,))], "first_edges", room=RP_ROOM,
    )
    ripple_apart, = call(
        second_edges_kernel, (ripple_start, ripple_source, token, ripple_apart), [ANY] * 4, [edge], [ANY],
        [edge, pltpu.SemaphoreType.DMA((3,))], "second_edges", aliases={3: 0}, room=RP_ROOM,
    )
    others, token = call(
        pair_kernel, (*wholes[1:], aparts[0]), [VMEM] * (shares - 1) + [ANY],
        [(shares - 1, HIGH_SIZE, rows_each, lanes), TILE], [VMEM] * 2, [], "pair",
    )
    ripple_paireds = call(
        near_edges_kernel, (ripple_start, ripple_source, token, paired_start, paired_source), [ANY] * 5,
        near_edges, [ANY] * 2, [edge, edge, pltpu.SemaphoreType.DMA((4,))], "near_edges", aliases={3: 0, 4: 1},
        room=NEAR_ROOM,
    )
    paireds = [lax.ppermute(paired, "mesh", near), lax.ppermute(others, "mesh", near)]
    ripple_apart = lax.ppermute(ripple_apart, "mesh", far)
    ripple_paireds = [lax.ppermute(part, "mesh", near) for part in ripple_paireds]

    known = (planes + G_LOW + G_HIGH, rows, lanes)
    field, nud, sigma = call(
        functools.partial(bias_kernel, shares, meshes),
        (*wholes, *aparts, *paireds, table_index, bh_base, bh_slope, conductivity),
        [VMEM] * (2 * shares + 2) + [SMEM] * 4,
        [
            bias_start.shape, (planes + NUD_LOW + NUD_HIGH, rows, lanes), (planes + 2 * (ITERS_R - 1), rows, lanes)
        ],
        [VMEM] * 3,
        [
            (3, planes + A_LOW[0] + A_HIGH[0], rows, lanes),
            (3, planes + A_LOW[1] + A_HIGH[1], rows, lanes),
            (3, planes + S_LOW + S_HIGH, rows, lanes),
            known,
            known,
            (KNOTS + 1, *known),
            known,
        ],
        "bias",
        BIAS_WORK,
    )

    lead = ripple_start.shape[:3]
    slots = (planes + 2, rows, lanes)
    ripple, edge, inner_loss, sides, answer = call(
        functools.partial(inner_kernel, meshes),
        (harmonic_numbers, nud, sigma, ripple_start, ripple_source, *ripple_paireds), [SMEM] + [VMEM] * 6,
        [ripple_start.shape, lead + (2, rows, lanes), (planes, rows, lanes), (6, *slots), (count, 2, *slots)],
        [ANY] + [VMEM] * 4, [lead + slots, lead + (planes, rows, lanes), pltpu.SemaphoreType.DMA((planes,))],
        "inner_ripple",
    )
    ripple, *losses = call(
        functools.partial(outer_kernel, shares),
        (
            harmonic_numbers, sigma, ripple_start, ripple_source, ripple_apart, edge, sides, answer, inner_loss, ripple,
        ),
        [SMEM] + [VMEM] * 8 + [ANY],
        [ripple_start.shape] + [(planes, rows_each, lanes)] * shares, [ANY] + [VMEM] * shares,
        [lead + (2, rows, lanes)] * 2 + [(2, rows, lanes), pltpu.SemaphoreType.DMA((2,))],
        "outer_ripple", aliases={9: 0},
    )
    loss = losses[0]
    for turn, pairs in enumerate(turned):
        loss = loss + lax.ppermute(losses[turn + 1], "harm", pairs)
    return field, ripple, loss


def solution(mesh):
    return jax.shard_map(
        functools.partial(body, mesh.shape["mesh"], mesh.shape["harm"]),
        mesh=mesh,
        in_specs=(
            P(None, "mesh", "harm", None),
            P(None, "mesh", "harm", None),
            P("mesh", "harm", None),
            P(),
            P(),
            P(),
            P(),
            P(),
            P("harm", None, None, "mesh", None, None),
            P("harm", None, None, "mesh", None, None),
        ),
        out_specs=(
            P(None, "mesh", "harm", None),
            P("harm", None, None, "mesh", None, None),
            P("mesh", "harm", None),
        ),
        check_vma=False,
    )
```

```python
import functools
import math

import jax
import jax.numpy as jnp
from jax import lax
from jax.experimental import pallas as pl
from jax.experimental.pallas import tpu as pltpu
from jax.sharding import PartitionSpec as P

ITERS_B = 2
ITERS_R = 2
KNOTS = 8
MATS = 4

kappa = 0.05
knot_step = 1.5
soft_width = 0.5
omega_step = 0.25
CAP = 80.0

NUD_LOW, NUD_HIGH = ITERS_R, ITERS_R
A_LOW = [NUD_LOW + ITERS_B - step for step in range(ITERS_B + 1)]
A_HIGH = [NUD_HIGH + 1 + 2 * (ITERS_B - step) for step in range(ITERS_B + 1)]
S_LOW, S_HIGH = A_LOW[1], A_HIGH[1]
G_LOW, G_HIGH = A_LOW[0], A_HIGH[0] - 1

BIAS_WORK = 20000000
PACK_ROOM = 62 * 2**20
RP_ROOM = 58 * 2**20
NEAR_ROOM = 58 * 2**20
VMEM = pl.BlockSpec(memory_space=pltpu.VMEM)
SMEM = pl.BlockSpec(memory_space=pltpu.SMEM)
ANY = pl.BlockSpec(memory_space=pl.ANY)


TILE = (8, 128)


class Tiles:
    def __init__(self, rows, lanes):
        self.grid = (rows // TILE[0], lanes // TILE[1])
        self.spots = [(i, j) for i in range(self.grid[0]) for j in range(self.grid[1])]
        self.at_end, self.at_start = [], []
        for axis in range(2):
            place = lax.broadcasted_iota(jnp.int32, TILE, axis)
            self.at_end.append(place == TILE[axis] - 1)
            self.at_start.append(place == 0)

    def where(self, spot):
        return (slice(spot[0] * TILE[0], (spot[0] + 1) * TILE[0]), slice(spot[1] * TILE[1], (spot[1] + 1) * TILE[1]))

    def load(self, ref, *lead):
        return {spot: ref[lead + self.where(spot)] for spot in self.spots}

    def store(self, ref, lead, values):
        for spot in self.spots:
            ref[lead + self.where(spot)] = values[spot]

    def each(self, function, *values):
        return {spot: function(*(value[spot] for value in values)) for spot in self.spots}

    def side(self, step, axis):
        return (self.at_end if step > 0 else self.at_start)[axis]

    def is_edge(self, spot, step, axis):
        return spot[axis] == (self.grid[axis] - 1 if step > 0 else 0)

    def move(self, values, step, axis, fill):
        rolled = self.each(lambda tile: pltpu.roll(tile, TILE[axis] - 1 if step > 0 else 1, axis), values)
        side, moved = self.side(step, axis), {}
        for spot in self.spots:
            if self.is_edge(spot, step, axis):
                moved[spot] = jnp.where(side, 0.0, rolled[spot]) if fill else rolled[spot]
            else:
                other = (spot[0] + step, spot[1]) if axis == 0 else (spot[0], spot[1] + step)
                moved[spot] = jnp.where(side, rolled[other], rolled[spot])
        return moved

    def inner(self, values, step, axis):
        side = self.side(step, axis)
        return {
            spot: jnp.where(side, 0.0, values[spot]) if self.is_edge(spot, step, axis) else values[spot]
            for spot in self.spots
        }


SIDES = ((1, 0), (-1, 0), (1, 1), (-1, 1))


def double_couplings(tiles, center, above, below):
    add = lambda one, other: one + other
    weights = [tiles.each(add, center, above), tiles.each(add, center, below)]
    total = tiles.each(add, *weights)
    for step, axis in SIDES:
        weight = tiles.each(add, center, tiles.move(center, step, axis, True))
        total = tiles.each(add, total, weight)
        weights.append(tiles.inner(weight, step, axis))
    return weights, tiles.each(lambda value: value + 2.0 * kappa, total)


def pull(tiles, start, weights, center, beside):
    moved = list(beside) + [tiles.move(center, step, axis, False) for step, axis in SIDES]
    total = start
    for weight, other in zip(weights, moved):
        total = tiles.each(lambda so_far, w, value: so_far + w * value, total, weight, other)
    return total


def flux_squared(tiles, field, plane):
    ax, ay, az = (tiles.load(field, part, plane) for part in range(3))
    ay_first, az_first = tiles.load(field, 1, plane + 1), tiles.load(field, 2, plane + 1)
    ax_second, az_second = tiles.move(ax, 1, 0, True), tiles.move(az, 1, 0, True)
    ax_third, ay_third = tiles.move(ax, 1, 1, True), tiles.move(ay, 1, 1, True)

    def square(x, y, z, y1, z1, x2, z2, x3, y3):
        flux_one = (z2 - z) - (y3 - y)
        flux_two = (x3 - x) - (z1 - z)
        flux_three = (y1 - y) - (x2 - x)
        return flux_one * flux_one + flux_two * flux_two + flux_three * flux_three

    return tiles.each(square, ax, ay, az, ay_first, az_first, ax_second, az_second, ax_third, ay_third)


def reluctivity(tiles, flux_sq, base, slope_of, slope_total, incremental):
    doubled = tiles.each(lambda value: value * (1.0 / soft_width), flux_sq)
    excess = tiles.each(lambda value: jnp.maximum(value - CAP, 0.0), doubled)
    floor = tiles.each(lambda value: jnp.exp(-value), excess)
    rising = tiles.each(lambda value: jnp.exp(jnp.minimum(value, CAP)), doubled)
    nu = tiles.each(lambda start, slope, value: start + slope * value, base, slope_total, excess)
    slope_sum = None
    for knot in range(KNOTS):
        factor = math.exp(-knot_step * knot / soft_width)
        slope = slope_of(knot)
        high = tiles.each(lambda value: value * factor, rising)
        both = tiles.each(lambda one, other: one + other, high, floor)
        nu = tiles.each(lambda so_far, weight, value: so_far + weight * jnp.log(value), nu, slope, both)
        if incremental:
            part = tiles.each(lambda weight, one, other: weight * (one / other), slope, high, both)
            slope_sum = tiles.each(lambda one, other: one + other, slope_sum, part) if knot else part
    if incremental:
        nu = tiles.each(lambda value, s, slope: value + (2.0 / soft_width) * (s * slope), nu, flux_sq, slope_sum)
    return nu


def loop_in_pairs(count, body):
    def step(at, carry):
        body(2 * at)
        body(2 * at + 1)
        return carry

    lax.fori_loop(0, count // 2, step, 0)
    if count % 2:
        body(count - 1)


LOW_SIZE = 3 * (A_LOW[0] + S_LOW) + G_LOW
HIGH_SIZE = 3 * (A_HIGH[0] + S_HIGH) + G_HIGH - 2


def edge_parts(planes, low):
    halo_of = ((A_LOW if low else A_HIGH)[0], S_LOW if low else S_HIGH, G_LOW if low else G_HIGH)
    at, parts = 0, []
    for array in range(7):
        halo = halo_of[0 if array < 3 else 1 if array < 6 else 2]
        if not low and array in (0, 3):
            halo -= 1
        parts.append((array * planes + (planes - halo if low else 0), at, halo))
        at += halo
    return parts


def write_edge(target, whole, low):
    for first, at, halo in edge_parts(whole.shape[0] // 7, low):
        target[at:at + halo] = whole[first:first + halo]


def is_odd():
    return lax.rem(lax.axis_index("mesh"), 2) == 1


def pack_kernel(start, source, region, whole, apart, paired, token, marks, sems):
    token[...] = jnp.zeros(token.shape, token.dtype)
    planes = region.shape[0]
    copies = [pltpu.make_async_copy(region, marks, sems.at[0])]
    for part in range(3):
        for at, origin in ((part, start), (3 + part, source)):
            target = whole.at[at * planes:(at + 1) * planes]
            copies.append(pltpu.make_async_copy(origin.at[part], target, sems.at[at + 1]))
    for copy in copies:
        copy.start()
    for copy in copies:
        copy.wait()
    whole[6 * planes:] = marks[...].astype(jnp.float32)
    for odd in (False, True):
        pl.when(is_odd() == odd)(functools.partial(write_edge, apart, whole, odd))
        pl.when(is_odd() == odd)(functools.partial(write_edge, paired, whole, not odd))


def pair_kernel(*refs):
    wholes, (paired, token) = refs[:-3], refs[-2:]
    token[...] = jnp.zeros(token.shape, token.dtype)
    for odd in (False, True):

        @pl.when(is_odd() == odd)
        def write():
            for turn, whole in enumerate(wholes):
                write_edge(paired.at[turn], whole, not odd)


def is_second():
    return lax.rem(lax.axis_index("mesh") + 1, 4) < 2


def send_edges(start, source, buffer, target, top, sems):
    planes = start.shape[3]
    ways_in = []
    for part, (origin, count, onto) in enumerate(((start, 2, 0), (source, 1, 2))):
        at = jnp.where(top, planes - count, 0)
        ways_in.append(
            pltpu.make_async_copy(planes_of(origin, at, count), planes_of(buffer, onto, count), sems.at[part])
        )
        ways_in[-1].start()
    for copy in ways_in:
        copy.wait()
    way_out = pltpu.make_async_copy(buffer, target, sems.at[2])
    way_out.start()
    way_out.wait()


def send_near_edges(origins, targets, buffers, sems):
    ways = []
    for number, (origin, buffer, target) in enumerate(zip(origins, buffers, targets)):
        planes, count = origin.shape[3], target.shape[3]
        first = jnp.where(is_odd(), 0, planes - count)
        held = planes_of(buffer, 0, count)
        ways.append(
            (
                pltpu.make_async_copy(planes_of(origin, first, count), held, sems.at[2 * number]),
                pltpu.make_async_copy(held, target, sems.at[2 * number + 1]),
            )
        )
    for way_in, unused in ways:
        way_in.start()
    for way_in, way_out in ways:
        way_in.wait()
        way_out.start()
    for unused, way_out in ways:
        way_out.wait()


def first_edges_kernel(
    start, source, after, apart, paired_start, paired_source, token, buffer, sems, near_sems
):
    token[...] = jnp.zeros(token.shape, token.dtype)

    @pl.when(jnp.logical_not(is_second()))
    def send_apart():
        send_edges(start, source, buffer, apart, is_odd(), sems)

    @pl.when(is_second())
    def send_near():
        send_near_edges([source], [paired_source], [buffer], near_sems)


def near_edges_kernel(start, source, after, start_in, source_in, paired_start, paired_source, buffer, other_buffer, sems):
    @pl.when(jnp.logical_not(is_second()))
    def send_both():
        send_near_edges([start, source], [paired_start, paired_source], [buffer, other_buffer], sems)

    @pl.when(is_second())
    def send_start():
        send_near_edges([start], [paired_start], [buffer], sems)


def second_edges_kernel(start, source, after, apart_in, apart, buffer, sems):
    @pl.when(is_second())
    def send_apart():
        send_edges(start, source, buffer, apart, is_odd(), sems)


def bias_kernel(shares, meshes, *refs):
    wholes, aparts, (paired, others) = refs[:shares], refs[shares:2 * shares], refs[2 * shares:2 * shares + 2]
    paireds = [paired] + [others.at[at] for at in range(shares - 1)]
    table_index, bh_base, bh_slope, conductivity, field_out, nud_out, sigma_out = refs[2 * shares + 2:2 * shares + 9]
    a0, a1, src, marks, nu, slopes, bases = refs[2 * shares + 9:]
    planes = wholes[0].shape[0] // 7
    rows_each, lanes = wholes[0].shape[1:]
    rows = rows_each * shares
    mine = lax.axis_index("harm")
    here = lax.axis_index("mesh")
    arrays = [(a0.at[part], A_LOW[0]) for part in range(3)]
    arrays += [(src.at[part], S_LOW) for part in range(3)] + [(marks, G_LOW)]
    for turn in range(shares):
        owner = lax.rem(mine + shares - turn, shares)
        at = pl.ds(pl.multiple_of(owner * rows_each, rows_each), rows_each)

        def fill(low, high):
            for (target, onto), (unused, first, halo) in zip(arrays, edge_parts(planes, True)):
                target[0:halo, at, :] = low[first:first + halo]
            for (target, onto), (unused, first, halo) in zip(arrays, edge_parts(planes, False)):
                target[onto + planes:onto + planes + halo, at, :] = high[first:first + halo]

        for number, (target, onto) in enumerate(arrays):
            target[onto:onto + planes, at, :] = wholes[turn][number * planes:(number + 1) * planes]
        pl.when(is_odd())(functools.partial(fill, paireds[turn], aparts[turn]))
        pl.when(jnp.logical_not(is_odd()))(functools.partial(fill, aparts[turn], paireds[turn]))

    tiles = Tiles(rows, lanes)
    tables = [table_index[member] for member in range(MATS)]
    base_of = [bh_base[table] for table in tables]
    slope_of = [[soft_width * bh_slope[table, knot] for table in tables] for knot in range(KNOTS)]
    sigma_of = [conductivity[member] for member in range(MATS)]

    def inside(plane):
        low_ok = jnp.logical_or(plane >= 0, here > 0)
        high_ok = jnp.logical_or(plane < planes, here < meshes - 1)
        return jnp.where(jnp.logical_and(low_ok, high_ok), 1.0, 0.0)

    def choose(marks_are, values):
        def one(*marked):
            chosen = jnp.where(marked[0], values[1], values[0])
            for member in range(2, MATS):
                chosen = jnp.where(marked[member - 1], values[member], chosen)
            return chosen

        return tiles.each(one, *marks_are)

    def members(mark):
        return [tiles.each(lambda value: value == float(member), mark) for member in range(1, MATS)]

    def relax_into(target, step, old):
        def body(at):
            plane = at - A_LOW[step]
            near = at + 1
            weights, total = double_couplings(
                tiles, tiles.load(nu, near), tiles.load(nu, near + 1), tiles.load(nu, near - 1)
            )
            keep = inside(plane)
            scale = tiles.each(lambda value: keep / value, total)
            from_old = plane + A_LOW[step - 1]
            for part in range(3):
                twice = tiles.each(lambda value: value + value, tiles.load(src, part, plane + S_LOW))
                near_old = [tiles.load(old, part, from_old + move) for move in (0, 1, -1)]
                moved = pull(tiles, twice, weights, near_old[0], near_old[1:])
                tiles.store(target, (part, at), tiles.each(lambda value, by: value * by, moved, scale))

        loop_in_pairs(planes + A_LOW[step] + A_HIGH[step], body)

    def first_nu(at):
        marked = members(tiles.load(marks, at))
        base, slope = choose(marked, base_of), [choose(marked, slope_of[knot]) for knot in range(KNOTS)]
        whole_slope = slope[0]
        tiles.store(bases, (at,), base)
        for knot in range(KNOTS):
            tiles.store(slopes, (knot, at), slope[knot])
            if knot:
                whole_slope = tiles.each(lambda one, other: one + other, whole_slope, slope[knot])
        tiles.store(slopes, (KNOTS, at), whole_slope)
        value = reluctivity(tiles, flux_squared(tiles, a0, at), base, lambda knot: slope[knot], whole_slope, False)
        keep = inside(at - G_LOW)
        tiles.store(nu, (at,), tiles.each(lambda one: one * keep, value))

    loop_in_pairs(planes + G_LOW + G_HIGH, first_nu)
    fields = (a0, a1)
    for step in range(1, ITERS_B + 1):
        old, new = fields[(step - 1) % 2], fields[step % 2]
        relax_into(new, step, old)
        last = step == ITERS_B
        lower = NUD_LOW if last else A_LOW[step + 1] + 1
        upper = NUD_HIGH if last else A_HIGH[step + 1] + 1

        def next_nu(at):
            plane = at - lower
            known = plane + G_LOW
            value = reluctivity(
                tiles, flux_squared(tiles, new, plane + A_LOW[step]), tiles.load(bases, known),
                lambda knot: tiles.load(slopes, knot, known), tiles.load(slopes, KNOTS, known), last,
            )
            keep = inside(plane)
            tiles.store(nud_out if last else nu, (at,), tiles.each(lambda one: one * keep, value))

        loop_in_pairs(planes + lower + upper, next_nu)

    def sigma_at(at):
        marked = members(tiles.load(marks, at - (ITERS_R - 1) + G_LOW))
        tiles.store(sigma_out, (at,), choose(marked, sigma_of))

    loop_in_pairs(planes + 2 * (ITERS_R - 1), sigma_at)
    own_rows = pl.ds(pl.multiple_of(mine * rows_each, rows_each), rows_each)
    final = fields[ITERS_B % 2]
    for part in range(3):
        field_out[part] = final[part, A_LOW[ITERS_B]:A_LOW[ITERS_B] + planes, own_rows, :]


def planes_of(ref, first, count):
    return ref.at[:, :, :, pl.ds(first, count)]


class Ripple:
    def __init__(self, rows, lanes, harmonic_numbers, count, sides, answer):
        self.sides, self.answer, self.tiles = sides, answer, Tiles(rows, lanes)
        first = lax.axis_index("harm") * count
        self.omegas = [omega_step * harmonic_numbers[first + at].astype(jnp.float32) for at in range(count)]

    def prepare(self, nud, sigma, slot, keep):
        tiles, near = self.tiles, slot + NUD_LOW - 1
        weights, total = double_couplings(tiles, *(tiles.load(nud, near + move) for move in (0, 1, -1)))
        for number, weight in enumerate(weights):
            tiles.store(self.sides, (number, slot), tiles.each(lambda value: 0.5 * value, weight))
        total = tiles.each(lambda value: 0.5 * value, total)
        square = tiles.each(lambda value: value * value, total)
        conduct = tiles.load(sigma, slot)
        for harmonic, omega in enumerate(self.omegas):
            damp = tiles.each(lambda value: omega * value, conduct)
            inverse = tiles.each(lambda one, other: keep / (one + other * other), square, damp)
            for part, value in enumerate((total, damp)):
                scaled = tiles.each(lambda one, other: one * other, value, inverse)
                tiles.store(self.answer, (harmonic, part, slot), scaled)

    def sweep(self, slot, old, source, put, turned_round=0, begin=False, begun=False):
        tiles, loss = self.tiles, None
        weights = [tiles.load(self.sides, number, slot) for number in (turned_round, 1 - turned_round, 2, 3, 4, 5)]
        for harmonic in range(len(self.omegas)):
            straight, turned = (tiles.load(self.answer, harmonic, part, slot) for part in range(2))
            power = None
            for part in range(3):
                both = []
                for piece in range(2):
                    lead = (harmonic, piece, part)
                    near_old = [tiles.load(ref, *lead, at) for ref, at in old]
                    given = tiles.load(source[0], *lead, source[1])
                    if begun:
                        add_last = lambda so_far, weight, value: so_far + weight * value
                        both.append(tiles.each(add_last, given, weights[1], near_old[0]))
                        continue
                    used = weights[:1] + weights[2:] if begin else weights
                    both.append(pull(tiles, given, used, near_old[0], near_old[1:]))
                if begin:
                    for piece, value in enumerate(both):
                        tiles.store(put[0], (harmonic, piece, part, put[1]), value)
                    continue
                real = tiles.each(lambda re, im, a, b: re * a + im * b, *both, straight, turned)
                imag = tiles.each(lambda re, im, a, b: im * a - re * b, *both, straight, turned)
                for piece, value in enumerate((real, imag)):
                    tiles.store(put[0], (harmonic, piece, part, put[1]), value)
                squared = tiles.each(lambda re, im: re * re + im * im, real, imag)
                power = tiles.each(lambda one, other: one + other, power, squared) if part else squared
            if begin:
                continue
            factor = 0.5 * self.omegas[harmonic] * self.omegas[harmonic]
            scaled = tiles.each(lambda value: factor * value, power)
            loss = tiles.each(lambda one, other: one + other, loss, scaled) if loss else scaled
        return loss


class Side:
    def __init__(self, planes, high):
        pick = lambda above, below: jnp.where(high, above, below)
        self.turned_round = pick(1, 0)
        self.own, self.second = pick(planes - 1, 0), pick(planes - 2, 1)
        self.beyond_slot, self.own_slot, self.second_slot = pick(planes + 1, 0), pick(planes, 1), pick(planes - 1, 2)
        self.halo, self.far_halo = pick(0, 1), pick(1, 0)
        self.third = pick(planes - 3, 2)


def first_on_side(ripple, side, start, source, halo_start, halo_source, put_beyond, put_own):
    ripple.sweep(
        side.beyond_slot, [(halo_start, side.halo), (start, side.own), (halo_start, side.far_halo)],
        (halo_source, 0),
        put_beyond, side.turned_round,
    )
    ripple.sweep(
        side.own_slot, [(start, side.own), (start, side.second), (halo_start, side.halo)], (source, side.own),
        put_own, side.turned_round,
    )


def inner_kernel(
    meshes, harmonic_numbers, nud, sigma, start, source, paired_start, paired_source, ripple_out, edge_out, begun_out,
    loss_out, sides, answer, r1, r2, sems
):
    count, planes = start.shape[0], start.shape[3]
    here = lax.axis_index("mesh")
    odd = is_odd()
    ripple = Ripple(*start.shape[4:], harmonic_numbers, count, sides, answer)
    tiles = ripple.tiles

    def prepare(slot):
        low_ok = jnp.logical_or(slot > 0, here > 0)
        high_ok = jnp.logical_or(slot < planes + 1, here < meshes - 1)
        ripple.prepare(nud, sigma, slot, jnp.where(jnp.logical_and(low_ok, high_ok), 1.0, 0.0))

    def drain(plane):
        return pltpu.make_async_copy(planes_of(r2, plane, 1), planes_of(ripple_out, plane, 1), sems.at[plane])

    def first(plane, carry):
        ripple.sweep(
            plane + 1, [(start, plane), (start, plane + 1), (start, plane - 1)], (source, plane), (r1, plane + 1)
        )
        return carry

    def second(plane, carry):
        loss = ripple.sweep(
            plane + 1, [(r1, plane + 1), (r1, plane + 2), (r1, plane)], (source, plane), (r2, plane)
        )
        tiles.store(loss_out, (plane,), tiles.each(lambda one, other: one * other, tiles.load(sigma, plane + 1), loss))
        drain(plane).start()
        return carry

    def finish(plane, carry):
        drain(plane).wait()
        return carry

    near, far = Side(planes, jnp.logical_not(odd)), Side(planes, odd)
    loop_in_pairs(planes + 2, prepare)
    lax.fori_loop(1, planes - 1, first, 0)
    first_on_side(
        ripple, near, start, source, paired_start, paired_source, (r1, near.beyond_slot), (r1, near.own_slot)
    )
    begin, end = jnp.where(odd, 0, 2), jnp.where(odd, planes - 2, planes)
    lax.fori_loop(begin, end, second, 0)
    edge_out[:, :, :, 0] = r1[:, :, :, far.second_slot]
    ripple.sweep(
        far.own_slot, [(start, far.own), (start, far.second)], (source, far.own), (begun_out, 0), far.turned_round, begin=True
    )
    ripple.sweep(
        far.second_slot, [(r1, far.second_slot), (r1, far.third + 1)], (source, far.second), (begun_out, 1),
        far.turned_round, begin=True,
    )
    lax.fori_loop(begin, end, finish, 0)


def outer_kernel(
    shares, harmonic_numbers, sigma, start, source, apart, edge, begun, sides, answer, loss_in, ripple_in,
    ripple_out, *refs
):
    losses, (r1, r2, loss, sems) = refs[:shares], refs[shares:]
    count, planes = start.shape[0], start.shape[3]
    rows, lanes = start.shape[4:]

    far = Side(planes, is_odd())
    ripple = Ripple(rows, lanes, harmonic_numbers, count, sides, answer)
    tiles = ripple.tiles
    ripple.sweep(
        far.beyond_slot, [(apart, far.halo), (start, far.own), (apart, far.far_halo)], (apart, 2), (r1, 0), far.turned_round
    )
    ripple.sweep(far.own_slot, [(apart, far.halo)], (begun, 0), (r1, 1), far.turned_round, begun=True)

    def drain(slot, plane):
        return pltpu.make_async_copy(planes_of(r2, slot, 1), planes_of(ripple_out, plane, 1), sems.at[slot])

    steps = (
        (far.own, far.own_slot, [(r1, 1), (edge, 0), (r1, 0)], (source, far.own), False),
        (far.second, far.second_slot, [(r1, 1)], (begun, 1), True),
    )
    for at, (plane, slot, old, given, is_begun) in enumerate(steps):
        added = ripple.sweep(slot, old, given, (r2, at), far.turned_round, begun=is_begun)
        drain(at, plane).start()
        tiles.store(loss, (at,), tiles.each(lambda one, other: one * other, tiles.load(sigma, slot), added))
    rows_each = rows // shares
    for turn in range(shares):
        owner = lax.rem(lax.axis_index("harm") + turn, shares)
        part = pl.ds(pl.multiple_of(owner * rows_each, rows_each), rows_each)
        losses[turn][...] = loss_in[:, part, :]
        for at, (plane, *unused) in enumerate(steps):
            losses[turn][plane] = loss[at, part, :]
    for at, (plane, *unused) in enumerate(steps):
        drain(at, plane).wait()


def call(kernel, operands, in_specs, out_shapes, out_specs, scratch, name, work=0, aliases={}, room=0):
    f32 = jnp.float32
    shapes = [o.shape for o, spec in zip(operands, in_specs) if spec is VMEM]
    shapes += [shape for shape, spec in zip(out_shapes, out_specs) if spec is VMEM]
    shapes += [shape for shape in scratch if isinstance(shape, tuple)]
    held = 4 * sum(math.prod(shape) for shape in shapes)
    return pl.pallas_call(
        kernel,
        out_shape=[jax.ShapeDtypeStruct(shape, f32) for shape in out_shapes],
        in_specs=in_specs,
        out_specs=out_specs,
        scratch_shapes=[pltpu.VMEM(shape, f32) if isinstance(shape, tuple) else shape for shape in scratch],
        compiler_params=pltpu.CompilerParams(vmem_limit_bytes=room or held + 4 * 2**20),
        cost_estimate=pl.CostEstimate(flops=work * 300, bytes_accessed=work, transcendentals=0),
        input_output_aliases=aliases,
        name=name,
    )(*operands)


def body(
    meshes, shares, bias_source, bias_start, region, table_index, bh_base, bh_slope, conductivity, harmonic_numbers,
    ripple_source, ripple_start,
):
    unused, planes, rows_each, lanes = bias_start.shape
    rows = rows_each * shares
    count = ripple_start.shape[0]
    near = [(i, i + 1) for i in range(0, meshes - 1, 2)]
    far = [(i, i + 1) for i in range(1, meshes - 1, 2)]
    near += [(j, i) for i, j in near]
    far += [(j, i) for i, j in far]
    turned = [[(i, (i + turn) % shares) for i in range(shares)] for turn in range(1, shares)]

    def around(block):
        return [block] + [lax.ppermute(block, "harm", pairs) for pairs in turned]

    whole, apart, paired, token = call(
        pack_kernel, (bias_start, bias_source, region), [ANY] * 3,
        [(7 * planes, rows_each, lanes), (HIGH_SIZE, rows_each, lanes), (HIGH_SIZE, rows_each, lanes), TILE], [VMEM] * 4,
        [pltpu.VMEM(region.shape, region.dtype), pltpu.SemaphoreType.DMA((7,))], "pack", room=PACK_ROOM,
    )
    wholes = around(whole)
    aparts = around(lax.ppermute(apart, "mesh", far))
    edge = ripple_start.shape[:3] + (3, rows, lanes)
    near_edges = [edge[:3] + (size, rows, lanes) for size in (2, 1)]
    ripple_apart, paired_start, paired_source, token = call(
        first_edges_kernel, (ripple_start, ripple_source, token), [ANY] * 3,
        [edge] + near_edges + [TILE], [ANY] * 3 + [VMEM],
        [edge, pltpu.SemaphoreType.DMA((3,)), pltpu.SemaphoreType.DMA((2,))], "first_edges", room=RP_ROOM,
    )
    ripple_apart, = call(
        second_edges_kernel, (ripple_start, ripple_source, token, ripple_apart), [ANY] * 4, [edge], [ANY],
        [edge, pltpu.SemaphoreType.DMA((3,))], "second_edges", aliases={3: 0}, room=RP_ROOM,
    )
    others, token = call(
        pair_kernel, (*wholes[1:], aparts[0]), [VMEM] * (shares - 1) + [ANY],
        [(shares - 1, HIGH_SIZE, rows_each, lanes), TILE], [VMEM] * 2, [], "pair",
    )
    ripple_paireds = call(
        near_edges_kernel, (ripple_start, ripple_source, token, paired_start, paired_source), [ANY] * 5,
        near_edges, [ANY] * 2, [edge, edge, pltpu.SemaphoreType.DMA((4,))], "near_edges", aliases={3: 0, 4: 1},
        room=NEAR_ROOM,
    )
    paireds = [lax.ppermute(paired, "mesh", near), lax.ppermute(others, "mesh", near)]
    ripple_apart = lax.ppermute(ripple_apart, "mesh", far)
    ripple_paireds = [lax.ppermute(part, "mesh", near) for part in ripple_paireds]

    known = (planes + G_LOW + G_HIGH, rows, lanes)
    field, nud, sigma = call(
        functools.partial(bias_kernel, shares, meshes),
        (*wholes, *aparts, *paireds, table_index, bh_base, bh_slope, conductivity),
        [VMEM] * (2 * shares + 2) + [SMEM] * 4,
        [
            bias_start.shape, (planes + NUD_LOW + NUD_HIGH, rows, lanes), (planes + 2 * (ITERS_R - 1), rows, lanes)
        ],
        [VMEM] * 3,
        [
            (3, planes + A_LOW[0] + A_HIGH[0], rows, lanes),
            (3, planes + A_LOW[1] + A_HIGH[1], rows, lanes),
            (3, planes + S_LOW + S_HIGH, rows, lanes),
            known,
            known,
            (KNOTS + 1, *known),
            known,
        ],
        "bias",
        BIAS_WORK,
    )

    lead = ripple_start.shape[:3]
    slots = (planes + 2, rows, lanes)
    ripple, edge, begun, inner_loss, sides, answer = call(
        functools.partial(inner_kernel, meshes),
        (harmonic_numbers, nud, sigma, ripple_start, ripple_source, *ripple_paireds), [SMEM] + [VMEM] * 6,
        [
            ripple_start.shape, lead + (1, rows, lanes), lead + (2, rows, lanes), (planes, rows, lanes), (6, *slots),
            (count, 2, *slots),
        ],
        [ANY] + [VMEM] * 5, [lead + slots, lead + (planes, rows, lanes), pltpu.SemaphoreType.DMA((planes,))],
        "inner_ripple",
    )
    ripple, *losses = call(
        functools.partial(outer_kernel, shares),
        (
            harmonic_numbers, sigma, ripple_start, ripple_source, ripple_apart, edge, begun, sides, answer, inner_loss,
            ripple,
        ),
        [SMEM] + [VMEM] * 9 + [ANY],
        [ripple_start.shape] + [(planes, rows_each, lanes)] * shares, [ANY] + [VMEM] * shares,
        [lead + (2, rows, lanes)] * 2 + [(2, rows, lanes), pltpu.SemaphoreType.DMA((2,))],
        "outer_ripple", aliases={10: 0},
    )
    loss = losses[0]
    for turn, pairs in enumerate(turned):
        loss = loss + lax.ppermute(losses[turn + 1], "harm", pairs)
    return field, ripple, loss


def solution(mesh):
    return jax.shard_map(
        functools.partial(body, mesh.shape["mesh"], mesh.shape["harm"]),
        mesh=mesh,
        in_specs=(
            P(None, "mesh", "harm", None),
            P(None, "mesh", "harm", None),
            P("mesh", "harm", None),
            P(),
            P(),
            P(),
            P(),
            P(),
            P("harm", None, None, "mesh", None, None),
            P("harm", None, None, "mesh", None, None),
        ),
        out_specs=(
            P(None, "mesh", "harm", None),
            P("harm", None, None, "mesh", None, None),
            P("mesh", "harm", None),
        ),
        check_vma=False,
    )
```

```python
import functools
import math

import jax
import jax.numpy as jnp
from jax import lax
from jax.experimental import pallas as pl
from jax.experimental.pallas import tpu as pltpu
from jax.sharding import PartitionSpec as P

ITERS_B = 2
ITERS_R = 2
KNOTS = 8
MATS = 4

kappa = 0.05
knot_step = 1.5
soft_width = 0.5
omega_step = 0.25
CAP = 80.0

NUD_LOW, NUD_HIGH = ITERS_R, ITERS_R
A_LOW = [NUD_LOW + ITERS_B - step for step in range(ITERS_B + 1)]
A_HIGH = [NUD_HIGH + 1 + 2 * (ITERS_B - step) for step in range(ITERS_B + 1)]
S_LOW, S_HIGH = A_LOW[1], A_HIGH[1]
G_LOW, G_HIGH = A_LOW[0], A_HIGH[0] - 1

BIAS_WORK = 20000000
PLACE_WORK = 0
PACK_ROOM = 62 * 2**20
RP_ROOM = 58 * 2**20
NEAR_ROOM = 58 * 2**20
VMEM = pl.BlockSpec(memory_space=pltpu.VMEM)
SMEM = pl.BlockSpec(memory_space=pltpu.SMEM)
ANY = pl.BlockSpec(memory_space=pl.ANY)


TILE = (8, 128)


class Tiles:
    def __init__(self, rows, lanes):
        self.grid = (rows // TILE[0], lanes // TILE[1])
        self.spots = [(i, j) for i in range(self.grid[0]) for j in range(self.grid[1])]
        self.at_end, self.at_start = [], []
        for axis in range(2):
            place = lax.broadcasted_iota(jnp.int32, TILE, axis)
            self.at_end.append(place == TILE[axis] - 1)
            self.at_start.append(place == 0)

    def where(self, spot):
        return (slice(spot[0] * TILE[0], (spot[0] + 1) * TILE[0]), slice(spot[1] * TILE[1], (spot[1] + 1) * TILE[1]))

    def load(self, ref, *lead):
        return {spot: ref[lead + self.where(spot)] for spot in self.spots}

    def store(self, ref, lead, values):
        for spot in self.spots:
            ref[lead + self.where(spot)] = values[spot]

    def each(self, function, *values):
        return {spot: function(*(value[spot] for value in values)) for spot in self.spots}

    def side(self, step, axis):
        return (self.at_end if step > 0 else self.at_start)[axis]

    def is_edge(self, spot, step, axis):
        return spot[axis] == (self.grid[axis] - 1 if step > 0 else 0)

    def move(self, values, step, axis, fill):
        rolled = self.each(lambda tile: pltpu.roll(tile, TILE[axis] - 1 if step > 0 else 1, axis), values)
        side, moved = self.side(step, axis), {}
        for spot in self.spots:
            if self.is_edge(spot, step, axis):
                moved[spot] = jnp.where(side, 0.0, rolled[spot]) if fill else rolled[spot]
            else:
                other = (spot[0] + step, spot[1]) if axis == 0 else (spot[0], spot[1] + step)
                moved[spot] = jnp.where(side, rolled[other], rolled[spot])
        return moved

    def inner(self, values, step, axis):
        side = self.side(step, axis)
        return {
            spot: jnp.where(side, 0.0, values[spot]) if self.is_edge(spot, step, axis) else values[spot]
            for spot in self.spots
        }


SIDES = ((1, 0), (-1, 0), (1, 1), (-1, 1))


def double_couplings(tiles, center, above, below):
    add = lambda one, other: one + other
    weights = [tiles.each(add, center, above), tiles.each(add, center, below)]
    total = tiles.each(add, *weights)
    for step, axis in SIDES:
        weight = tiles.each(add, center, tiles.move(center, step, axis, True))
        total = tiles.each(add, total, weight)
        weights.append(tiles.inner(weight, step, axis))
    return weights, tiles.each(lambda value: value + 2.0 * kappa, total)


def pull(tiles, start, weights, center, beside):
    moved = list(beside) + [tiles.move(center, step, axis, False) for step, axis in SIDES]
    total = start
    for weight, other in zip(weights, moved):
        total = tiles.each(lambda so_far, w, value: so_far + w * value, total, weight, other)
    return total


def flux_squared(tiles, field, plane):
    ax, ay, az = (tiles.load(field, part, plane) for part in range(3))
    ay_first, az_first = tiles.load(field, 1, plane + 1), tiles.load(field, 2, plane + 1)
    ax_second, az_second = tiles.move(ax, 1, 0, True), tiles.move(az, 1, 0, True)
    ax_third, ay_third = tiles.move(ax, 1, 1, True), tiles.move(ay, 1, 1, True)

    def square(x, y, z, y1, z1, x2, z2, x3, y3):
        flux_one = (z2 - z) - (y3 - y)
        flux_two = (x3 - x) - (z1 - z)
        flux_three = (y1 - y) - (x2 - x)
        return flux_one * flux_one + flux_two * flux_two + flux_three * flux_three

    return tiles.each(square, ax, ay, az, ay_first, az_first, ax_second, az_second, ax_third, ay_third)


def reluctivity(tiles, flux_sq, base, slope_of, slope_total, incremental):
    doubled = tiles.each(lambda value: value * (1.0 / soft_width), flux_sq)
    excess = tiles.each(lambda value: jnp.maximum(value - CAP, 0.0), doubled)
    floor = tiles.each(lambda value: jnp.exp(-value), excess)
    rising = tiles.each(lambda value: jnp.exp(jnp.minimum(value, CAP)), doubled)
    nu = tiles.each(lambda start, slope, value: start + slope * value, base, slope_total, excess)
    slope_sum = None
    for knot in range(KNOTS):
        factor = math.exp(-knot_step * knot / soft_width)
        slope = slope_of(knot)
        high = tiles.each(lambda value: value * factor, rising)
        both = tiles.each(lambda one, other: one + other, high, floor)
        nu = tiles.each(lambda so_far, weight, value: so_far + weight * jnp.log(value), nu, slope, both)
        if incremental:
            part = tiles.each(lambda weight, one, other: weight * (one / other), slope, high, both)
            slope_sum = tiles.each(lambda one, other: one + other, slope_sum, part) if knot else part
    if incremental:
        nu = tiles.each(lambda value, s, slope: value + (2.0 / soft_width) * (s * slope), nu, flux_sq, slope_sum)
    return nu


def loop_in_pairs(count, body):
    def step(at, carry):
        body(2 * at)
        body(2 * at + 1)
        return carry

    lax.fori_loop(0, count // 2, step, 0)
    if count % 2:
        body(count - 1)


LOW_SIZE = 3 * (A_LOW[0] + S_LOW) + G_LOW
HIGH_SIZE = 3 * (A_HIGH[0] + S_HIGH) + G_HIGH - 2


def edge_parts(planes, low):
    halo_of = ((A_LOW if low else A_HIGH)[0], S_LOW if low else S_HIGH, G_LOW if low else G_HIGH)
    at, parts = 0, []
    for array in range(7):
        halo = halo_of[0 if array < 3 else 1 if array < 6 else 2]
        if not low and array in (0, 3):
            halo -= 1
        parts.append((array * planes + (planes - halo if low else 0), at, halo))
        at += halo
    return parts


def write_edge(target, whole, low):
    for first, at, halo in edge_parts(whole.shape[0] // 7, low):
        target[at:at + halo] = whole[first:first + halo]


def is_odd():
    return lax.rem(lax.axis_index("mesh"), 2) == 1


def pack_kernel(start, source, region, whole, apart, paired, token, marks, sems):
    token[...] = jnp.zeros(token.shape, token.dtype)
    planes = region.shape[0]
    copies = [pltpu.make_async_copy(region, marks, sems.at[0])]
    for part in range(3):
        for at, origin in ((part, start), (3 + part, source)):
            target = whole.at[at * planes:(at + 1) * planes]
            copies.append(pltpu.make_async_copy(origin.at[part], target, sems.at[at + 1]))
    for copy in copies:
        copy.start()
    for copy in copies:
        copy.wait()
    whole[6 * planes:] = marks[...].astype(jnp.float32)
    for odd in (False, True):
        pl.when(is_odd() == odd)(functools.partial(write_edge, apart, whole, odd))
        pl.when(is_odd() == odd)(functools.partial(write_edge, paired, whole, not odd))


def pair_kernel(*refs):
    wholes, (paired, token) = refs[:-3], refs[-2:]
    token[...] = jnp.zeros(token.shape, token.dtype)
    for odd in (False, True):

        @pl.when(is_odd() == odd)
        def write():
            for turn, whole in enumerate(wholes):
                write_edge(paired.at[turn], whole, not odd)


def is_second():
    return lax.rem(lax.axis_index("mesh") + 1, 4) < 2


def send_edges(start, source, buffer, target, top, sems):
    planes = start.shape[3]
    ways_in = []
    for part, (origin, count, onto) in enumerate(((start, 2, 0), (source, 1, 2))):
        at = jnp.where(top, planes - count, 0)
        ways_in.append(
            pltpu.make_async_copy(planes_of(origin, at, count), planes_of(buffer, onto, count), sems.at[part])
        )
        ways_in[-1].start()
    for copy in ways_in:
        copy.wait()
    way_out = pltpu.make_async_copy(buffer, target, sems.at[2])
    way_out.start()
    way_out.wait()


def send_near_edges(origins, targets, buffers, sems):
    ways = []
    for number, (origin, buffer, target) in enumerate(zip(origins, buffers, targets)):
        planes, count = origin.shape[3], target.shape[3]
        first = jnp.where(is_odd(), 0, planes - count)
        held = planes_of(buffer, 0, count)
        ways.append(
            (
                pltpu.make_async_copy(planes_of(origin, first, count), held, sems.at[2 * number]),
                pltpu.make_async_copy(held, target, sems.at[2 * number + 1]),
            )
        )
    for way_in, unused in ways:
        way_in.start()
    for way_in, way_out in ways:
        way_in.wait()
        way_out.start()
    for unused, way_out in ways:
        way_out.wait()


def first_edges_kernel(
    start, source, after, apart, paired_start, paired_source, token, buffer, sems, near_sems
):
    token[...] = jnp.zeros(token.shape, token.dtype)

    @pl.when(jnp.logical_not(is_second()))
    def send_apart():
        send_edges(start, source, buffer, apart, is_odd(), sems)

    @pl.when(is_second())
    def send_near():
        send_near_edges([source], [paired_source], [buffer], near_sems)


def near_edges_kernel(start, source, after, start_in, source_in, paired_start, paired_source, buffer, other_buffer, sems):
    @pl.when(jnp.logical_not(is_second()))
    def send_both():
        send_near_edges([start, source], [paired_start, paired_source], [buffer, other_buffer], sems)

    @pl.when(is_second())
    def send_start():
        send_near_edges([start], [paired_start], [buffer], sems)


def second_edges_kernel(start, source, after, apart_in, apart, buffer, sems):
    @pl.when(is_second())
    def send_apart():
        send_edges(start, source, buffer, apart, is_odd(), sems)


def bias_kernel(shares, meshes, *refs):
    wholes, aparts, (paired, others) = refs[:shares], refs[shares:2 * shares], refs[2 * shares:2 * shares + 2]
    paireds = [paired] + [others.at[at] for at in range(shares - 1)]
    table_index, bh_base, bh_slope, conductivity, field_out, nud_out, sigma_out = refs[2 * shares + 2:2 * shares + 9]
    a0, a1, src, marks, nu, slopes, bases = refs[2 * shares + 9:]
    planes = wholes[0].shape[0] // 7
    rows_each, lanes = wholes[0].shape[1:]
    rows = rows_each * shares
    mine = lax.axis_index("harm")
    here = lax.axis_index("mesh")
    arrays = [(a0.at[part], A_LOW[0]) for part in range(3)]
    arrays += [(src.at[part], S_LOW) for part in range(3)] + [(marks, G_LOW)]
    for turn in range(shares):
        owner = lax.rem(mine + shares - turn, shares)
        at = pl.ds(pl.multiple_of(owner * rows_each, rows_each), rows_each)

        def fill(low, high):
            for (target, onto), (unused, first, halo) in zip(arrays, edge_parts(planes, True)):
                target[0:halo, at, :] = low[first:first + halo]
            for (target, onto), (unused, first, halo) in zip(arrays, edge_parts(planes, False)):
                target[onto + planes:onto + planes + halo, at, :] = high[first:first + halo]

        for number, (target, onto) in enumerate(arrays):
            target[onto:onto + planes, at, :] = wholes[turn][number * planes:(number + 1) * planes]
        pl.when(is_odd())(functools.partial(fill, paireds[turn], aparts[turn]))
        pl.when(jnp.logical_not(is_odd()))(functools.partial(fill, aparts[turn], paireds[turn]))

    tiles = Tiles(rows, lanes)
    tables = [table_index[member] for member in range(MATS)]
    base_of = [bh_base[table] for table in tables]
    slope_of = [[soft_width * bh_slope[table, knot] for table in tables] for knot in range(KNOTS)]
    sigma_of = [conductivity[member] for member in range(MATS)]

    def inside(plane):
        low_ok = jnp.logical_or(plane >= 0, here > 0)
        high_ok = jnp.logical_or(plane < planes, here < meshes - 1)
        return jnp.where(jnp.logical_and(low_ok, high_ok), 1.0, 0.0)

    def choose(marks_are, values):
        def one(*marked):
            chosen = jnp.where(marked[0], values[1], values[0])
            for member in range(2, MATS):
                chosen = jnp.where(marked[member - 1], values[member], chosen)
            return chosen

        return tiles.each(one, *marks_are)

    def members(mark):
        return [tiles.each(lambda value: value == float(member), mark) for member in range(1, MATS)]

    def relax_into(target, step, old):
        def body(at):
            plane = at - A_LOW[step]
            near = at + 1
            weights, total = double_couplings(
                tiles, tiles.load(nu, near), tiles.load(nu, near + 1), tiles.load(nu, near - 1)
            )
            keep = inside(plane)
            scale = tiles.each(lambda value: keep / value, total)
            from_old = plane + A_LOW[step - 1]
            for part in range(3):
                twice = tiles.each(lambda value: value + value, tiles.load(src, part, plane + S_LOW))
                near_old = [tiles.load(old, part, from_old + move) for move in (0, 1, -1)]
                moved = pull(tiles, twice, weights, near_old[0], near_old[1:])
                tiles.store(target, (part, at), tiles.each(lambda value, by: value * by, moved, scale))

        loop_in_pairs(planes + A_LOW[step] + A_HIGH[step], body)

    def first_nu(at):
        marked = members(tiles.load(marks, at))
        base, slope = choose(marked, base_of), [choose(marked, slope_of[knot]) for knot in range(KNOTS)]
        whole_slope = slope[0]
        tiles.store(bases, (at,), base)
        for knot in range(KNOTS):
            tiles.store(slopes, (knot, at), slope[knot])
            if knot:
                whole_slope = tiles.each(lambda one, other: one + other, whole_slope, slope[knot])
        tiles.store(slopes, (KNOTS, at), whole_slope)
        value = reluctivity(tiles, flux_squared(tiles, a0, at), base, lambda knot: slope[knot], whole_slope, False)
        keep = inside(at - G_LOW)
        tiles.store(nu, (at,), tiles.each(lambda one: one * keep, value))

    loop_in_pairs(planes + G_LOW + G_HIGH, first_nu)
    fields = (a0, a1)
    for step in range(1, ITERS_B + 1):
        old, new = fields[(step - 1) % 2], fields[step % 2]
        relax_into(new, step, old)
        last = step == ITERS_B
        lower = NUD_LOW if last else A_LOW[step + 1] + 1
        upper = NUD_HIGH if last else A_HIGH[step + 1] + 1

        def next_nu(at):
            plane = at - lower
            known = plane + G_LOW
            value = reluctivity(
                tiles, flux_squared(tiles, new, plane + A_LOW[step]), tiles.load(bases, known),
                lambda knot: tiles.load(slopes, knot, known), tiles.load(slopes, KNOTS, known), last,
            )
            keep = inside(plane)
            tiles.store(nud_out if last else nu, (at,), tiles.each(lambda one: one * keep, value))

        loop_in_pairs(planes + lower + upper, next_nu)

    def sigma_at(at):
        marked = members(tiles.load(marks, at - (ITERS_R - 1) + G_LOW))
        tiles.store(sigma_out, (at,), choose(marked, sigma_of))

    loop_in_pairs(planes + 2 * (ITERS_R - 1), sigma_at)
    own_rows = pl.ds(pl.multiple_of(mine * rows_each, rows_each), rows_each)
    final = fields[ITERS_B % 2]
    for part in range(3):
        field_out[part] = final[part, A_LOW[ITERS_B]:A_LOW[ITERS_B] + planes, own_rows, :]


def planes_of(ref, first, count):
    return ref.at[:, :, :, pl.ds(first, count)]


class Ripple:
    def __init__(self, rows, lanes, harmonic_numbers, count, sides, answer):
        self.sides, self.answer, self.tiles = sides, answer, Tiles(rows, lanes)
        first = lax.axis_index("harm") * count
        self.omegas = [omega_step * harmonic_numbers[first + at].astype(jnp.float32) for at in range(count)]

    def prepare(self, nud, sigma, slot, keep):
        tiles, near = self.tiles, slot + NUD_LOW - 1
        weights, total = double_couplings(tiles, *(tiles.load(nud, near + move) for move in (0, 1, -1)))
        for number, weight in enumerate(weights):
            tiles.store(self.sides, (number, slot), tiles.each(lambda value: 0.5 * value, weight))
        total = tiles.each(lambda value: 0.5 * value, total)
        square = tiles.each(lambda value: value * value, total)
        conduct = tiles.load(sigma, slot)
        for harmonic, omega in enumerate(self.omegas):
            damp = tiles.each(lambda value: omega * value, conduct)
            inverse = tiles.each(lambda one, other: keep / (one + other * other), square, damp)
            for part, value in enumerate((total, damp)):
                scaled = tiles.each(lambda one, other: one * other, value, inverse)
                tiles.store(self.answer, (harmonic, part, slot), scaled)

    def sweep(self, slot, old, source, put, turned_round=0, begin=False, begun=False):
        tiles, loss = self.tiles, None
        weights = [tiles.load(self.sides, number, slot) for number in (turned_round, 1 - turned_round, 2, 3, 4, 5)]
        for harmonic in range(len(self.omegas)):
            straight, turned = (tiles.load(self.answer, harmonic, part, slot) for part in range(2))
            power = None
            for part in range(3):
                both = []
                for piece in range(2):
                    lead = (harmonic, piece, part)
                    near_old = [tiles.load(ref, *lead, at) for ref, at in old]
                    given = tiles.load(source[0], *lead, source[1])
                    if begun:
                        add_last = lambda so_far, weight, value: so_far + weight * value
                        both.append(tiles.each(add_last, given, weights[1], near_old[0]))
                        continue
                    used = weights[:1] + weights[2:] if begin else weights
                    both.append(pull(tiles, given, used, near_old[0], near_old[1:]))
                if begin:
                    for piece, value in enumerate(both):
                        tiles.store(put[0], (harmonic, piece, part, put[1]), value)
                    continue
                real = tiles.each(lambda re, im, a, b: re * a + im * b, *both, straight, turned)
                imag = tiles.each(lambda re, im, a, b: im * a - re * b, *both, straight, turned)
                for piece, value in enumerate((real, imag)):
                    tiles.store(put[0], (harmonic, piece, part, put[1]), value)
                squared = tiles.each(lambda re, im: re * re + im * im, real, imag)
                power = tiles.each(lambda one, other: one + other, power, squared) if part else squared
            if begin:
                continue
            factor = 0.5 * self.omegas[harmonic] * self.omegas[harmonic]
            scaled = tiles.each(lambda value: factor * value, power)
            loss = tiles.each(lambda one, other: one + other, loss, scaled) if loss else scaled
        return loss


class Side:
    def __init__(self, planes, high):
        pick = lambda above, below: jnp.where(high, above, below)
        self.turned_round = pick(1, 0)
        self.own, self.second = pick(planes - 1, 0), pick(planes - 2, 1)
        self.beyond_slot, self.own_slot, self.second_slot = pick(planes + 1, 0), pick(planes, 1), pick(planes - 1, 2)
        self.halo, self.far_halo = pick(0, 1), pick(1, 0)
        self.third = pick(planes - 3, 2)


def first_on_side(ripple, side, start, source, halo_start, halo_source, put_beyond, put_own):
    ripple.sweep(
        side.beyond_slot, [(halo_start, side.halo), (start, side.own), (halo_start, side.far_halo)],
        (halo_source, 0),
        put_beyond, side.turned_round,
    )
    ripple.sweep(
        side.own_slot, [(start, side.own), (start, side.second), (halo_start, side.halo)], (source, side.own),
        put_own, side.turned_round,
    )


def inner_kernel(
    meshes, harmonic_numbers, nud, sigma, start, source, paired_start, paired_source, ripple_out, edge_out, begun_out,
    loss_out, sides, answer, r1, r2, sems
):
    count, planes = start.shape[0], start.shape[3]
    here = lax.axis_index("mesh")
    odd = is_odd()
    ripple = Ripple(*start.shape[4:], harmonic_numbers, count, sides, answer)
    tiles = ripple.tiles

    def prepare(slot):
        low_ok = jnp.logical_or(slot > 0, here > 0)
        high_ok = jnp.logical_or(slot < planes + 1, here < meshes - 1)
        ripple.prepare(nud, sigma, slot, jnp.where(jnp.logical_and(low_ok, high_ok), 1.0, 0.0))

    def drain(plane):
        return pltpu.make_async_copy(planes_of(r2, plane, 1), planes_of(ripple_out, plane, 1), sems.at[plane])

    def first(plane, carry):
        ripple.sweep(
            plane + 1, [(start, plane), (start, plane + 1), (start, plane - 1)], (source, plane), (r1, plane + 1)
        )
        return carry

    def second(plane, carry):
        loss = ripple.sweep(
            plane + 1, [(r1, plane + 1), (r1, plane + 2), (r1, plane)], (source, plane), (r2, plane)
        )
        tiles.store(loss_out, (plane,), tiles.each(lambda one, other: one * other, tiles.load(sigma, plane + 1), loss))
        drain(plane).start()
        return carry

    def finish(plane, carry):
        drain(plane).wait()
        return carry

    near, far = Side(planes, jnp.logical_not(odd)), Side(planes, odd)
    loop_in_pairs(planes + 2, prepare)
    lax.fori_loop(1, planes - 1, first, 0)
    first_on_side(
        ripple, near, start, source, paired_start, paired_source, (r1, near.beyond_slot), (r1, near.own_slot)
    )
    begin, end = jnp.where(odd, 0, 2), jnp.where(odd, planes - 2, planes)
    lax.fori_loop(begin, end, second, 0)
    edge_out[:, :, :, 0] = r1[:, :, :, far.second_slot]
    ripple.sweep(
        far.own_slot, [(start, far.own), (start, far.second)], (source, far.own), (begun_out, 0), far.turned_round, begin=True
    )
    ripple.sweep(
        far.second_slot, [(r1, far.second_slot), (r1, far.third + 1)], (source, far.second), (begun_out, 1),
        far.turned_round, begin=True,
    )
    lax.fori_loop(begin, end, finish, 0)


def outer_kernel(
    shares, harmonic_numbers, sigma, start, source, apart, edge, begun, sides, answer, loss_in,
    r2, *refs
):
    losses, (r1, loss) = refs[:shares], refs[shares:]
    count, planes = start.shape[0], start.shape[3]
    rows, lanes = start.shape[4:]

    far = Side(planes, is_odd())
    ripple = Ripple(rows, lanes, harmonic_numbers, count, sides, answer)
    tiles = ripple.tiles
    ripple.sweep(
        far.beyond_slot, [(apart, far.halo), (start, far.own), (apart, far.far_halo)], (apart, 2), (r1, 0), far.turned_round
    )
    ripple.sweep(far.own_slot, [(apart, far.halo)], (begun, 0), (r1, 1), far.turned_round, begun=True)

    steps = (
        (far.own, far.own_slot, [(r1, 1), (edge, 0), (r1, 0)], (source, far.own), False),
        (far.second, far.second_slot, [(r1, 1)], (begun, 1), True),
    )
    for at, (plane, slot, old, given, is_begun) in enumerate(steps):
        added = ripple.sweep(slot, old, given, (r2, at), far.turned_round, begun=is_begun)
        tiles.store(loss, (at,), tiles.each(lambda one, other: one * other, tiles.load(sigma, slot), added))
    rows_each = rows // shares
    for turn in range(shares):
        owner = lax.rem(lax.axis_index("harm") + turn, shares)
        part = pl.ds(pl.multiple_of(owner * rows_each, rows_each), rows_each)
        losses[turn][...] = loss_in[:, part, :]
        for at, (plane, *unused) in enumerate(steps):
            losses[turn][plane] = loss[at, part, :]


def place_kernel(edge, ripple_in, ripple_out, sems):
    far = Side(ripple_out.shape[3], is_odd())
    copies = [
        pltpu.make_async_copy(planes_of(edge, at, 1), planes_of(ripple_out, plane, 1), sems.at[at])
        for at, plane in enumerate((far.own, far.second))
    ]
    for copy in copies:
        copy.start()
    for copy in copies:
        copy.wait()


def call(kernel, operands, in_specs, out_shapes, out_specs, scratch, name, work=0, aliases={}, room=0):
    f32 = jnp.float32
    shapes = [o.shape for o, spec in zip(operands, in_specs) if spec is VMEM]
    shapes += [shape for shape, spec in zip(out_shapes, out_specs) if spec is VMEM]
    shapes += [shape for shape in scratch if isinstance(shape, tuple)]
    held = 4 * sum(math.prod(shape) for shape in shapes)
    return pl.pallas_call(
        kernel,
        out_shape=[jax.ShapeDtypeStruct(shape, f32) for shape in out_shapes],
        in_specs=in_specs,
        out_specs=out_specs,
        scratch_shapes=[pltpu.VMEM(shape, f32) if isinstance(shape, tuple) else shape for shape in scratch],
        compiler_params=pltpu.CompilerParams(vmem_limit_bytes=room or held + 4 * 2**20),
        cost_estimate=pl.CostEstimate(flops=work * 300, bytes_accessed=work, transcendentals=0),
        input_output_aliases=aliases,
        name=name,
    )(*operands)


def body(
    meshes, shares, bias_source, bias_start, region, table_index, bh_base, bh_slope, conductivity, harmonic_numbers,
    ripple_source, ripple_start,
):
    unused, planes, rows_each, lanes = bias_start.shape
    rows = rows_each * shares
    count = ripple_start.shape[0]
    near = [(i, i + 1) for i in range(0, meshes - 1, 2)]
    far = [(i, i + 1) for i in range(1, meshes - 1, 2)]
    near += [(j, i) for i, j in near]
    far += [(j, i) for i, j in far]
    turned = [[(i, (i + turn) % shares) for i in range(shares)] for turn in range(1, shares)]

    def around(block):
        return [block] + [lax.ppermute(block, "harm", pairs) for pairs in turned]

    whole, apart, paired, token = call(
        pack_kernel, (bias_start, bias_source, region), [ANY] * 3,
        [(7 * planes, rows_each, lanes), (HIGH_SIZE, rows_each, lanes), (HIGH_SIZE, rows_each, lanes), TILE], [VMEM] * 4,
        [pltpu.VMEM(region.shape, region.dtype), pltpu.SemaphoreType.DMA((7,))], "pack", room=PACK_ROOM,
    )
    wholes = around(whole)
    aparts = around(lax.ppermute(apart, "mesh", far))
    edge = ripple_start.shape[:3] + (3, rows, lanes)
    near_edges = [edge[:3] + (size, rows, lanes) for size in (2, 1)]
    ripple_apart, paired_start, paired_source, token = call(
        first_edges_kernel, (ripple_start, ripple_source, token), [ANY] * 3,
        [edge] + near_edges + [TILE], [ANY] * 3 + [VMEM],
        [edge, pltpu.SemaphoreType.DMA((3,)), pltpu.SemaphoreType.DMA((2,))], "first_edges", room=RP_ROOM,
    )
    ripple_apart, = call(
        second_edges_kernel, (ripple_start, ripple_source, token, ripple_apart), [ANY] * 4, [edge], [ANY],
        [edge, pltpu.SemaphoreType.DMA((3,))], "second_edges", aliases={3: 0}, room=RP_ROOM,
    )
    others, token = call(
        pair_kernel, (*wholes[1:], aparts[0]), [VMEM] * (shares - 1) + [ANY],
        [(shares - 1, HIGH_SIZE, rows_each, lanes), TILE], [VMEM] * 2, [], "pair",
    )
    ripple_paireds = call(
        near_edges_kernel, (ripple_start, ripple_source, token, paired_start, paired_source), [ANY] * 5,
        near_edges, [ANY] * 2, [edge, edge, pltpu.SemaphoreType.DMA((4,))], "near_edges", aliases={3: 0, 4: 1},
        room=NEAR_ROOM,
    )
    paireds = [lax.ppermute(paired, "mesh", near), lax.ppermute(others, "mesh", near)]
    ripple_apart = lax.ppermute(ripple_apart, "mesh", far)
    ripple_paireds = [lax.ppermute(part, "mesh", near) for part in ripple_paireds]

    known = (planes + G_LOW + G_HIGH, rows, lanes)
    field, nud, sigma = call(
        functools.partial(bias_kernel, shares, meshes),
        (*wholes, *aparts, *paireds, table_index, bh_base, bh_slope, conductivity),
        [VMEM] * (2 * shares + 2) + [SMEM] * 4,
        [
            bias_start.shape, (planes + NUD_LOW + NUD_HIGH, rows, lanes), (planes + 2 * (ITERS_R - 1), rows, lanes)
        ],
        [VMEM] * 3,
        [
            (3, planes + A_LOW[0] + A_HIGH[0], rows, lanes),
            (3, planes + A_LOW[1] + A_HIGH[1], rows, lanes),
            (3, planes + S_LOW + S_HIGH, rows, lanes),
            known,
            known,
            (KNOTS + 1, *known),
            known,
        ],
        "bias",
        BIAS_WORK,
    )

    lead = ripple_start.shape[:3]
    slots = (planes + 2, rows, lanes)
    ripple, edge, begun, inner_loss, sides, answer = call(
        functools.partial(inner_kernel, meshes),
        (harmonic_numbers, nud, sigma, ripple_start, ripple_source, *ripple_paireds), [SMEM] + [VMEM] * 6,
        [
            ripple_start.shape, lead + (1, rows, lanes), lead + (2, rows, lanes), (planes, rows, lanes), (6, *slots),
            (count, 2, *slots),
        ],
        [ANY] + [VMEM] * 5, [lead + slots, lead + (planes, rows, lanes), pltpu.SemaphoreType.DMA((planes,))],
        "inner_ripple",
    )
    outer_edge, *losses = call(
        functools.partial(outer_kernel, shares),
        (harmonic_numbers, sigma, ripple_start, ripple_source, ripple_apart, edge, begun, sides, answer, inner_loss),
        [SMEM] + [VMEM] * 9, [lead + (2, rows, lanes)] + [(planes, rows_each, lanes)] * shares, [VMEM] * (shares + 1),
        [lead + (2, rows, lanes), (2, rows, lanes)], "outer_ripple",
    )
    ripple, = call(
        place_kernel, (outer_edge, ripple), [ANY] * 2, [ripple_start.shape], [ANY], [pltpu.SemaphoreType.DMA((2,))],
        "place", PLACE_WORK, aliases={1: 0},
    )
    loss = losses[0]
    for turn, pairs in enumerate(turned):
        loss = loss + lax.ppermute(losses[turn + 1], "harm", pairs)
    return field, ripple, loss


def solution(mesh):
    return jax.shard_map(
        functools.partial(body, mesh.shape["mesh"], mesh.shape["harm"]),
        mesh=mesh,
        in_specs=(
            P(None, "mesh", "harm", None),
            P(None, "mesh", "harm", None),
            P("mesh", "harm", None),
            P(),
            P(),
            P(),
            P(),
            P(),
            P("harm", None, None, "mesh", None, None),
            P("harm", None, None, "mesh", None, None),
        ),
        out_specs=(
            P(None, "mesh", "harm", None),
            P("harm", None, None, "mesh", None, None),
            P("mesh", "harm", None),
        ),
        check_vma=False,
    )
```

```python
import functools
import math

import jax
import jax.numpy as jnp
from jax import lax
from jax.experimental import pallas as pl
from jax.experimental.pallas import tpu as pltpu
from jax.sharding import PartitionSpec as P

ITERS_B = 2
ITERS_R = 2
KNOTS = 8
MATS = 4

kappa = 0.05
knot_step = 1.5
soft_width = 0.5
omega_step = 0.25
CAP = 80.0

NUD_LOW, NUD_HIGH = ITERS_R, ITERS_R
A_LOW = [NUD_LOW + ITERS_B - step for step in range(ITERS_B + 1)]
A_HIGH = [NUD_HIGH + 1 + 2 * (ITERS_B - step) for step in range(ITERS_B + 1)]
S_LOW, S_HIGH = A_LOW[1], A_HIGH[1]
G_LOW, G_HIGH = A_LOW[0], A_HIGH[0] - 1

BIAS_WORK = 20000000
PLACE_WORK = 0
PACK_ROOM = 62 * 2**20
RP_ROOM = 58 * 2**20
NEAR_ROOM = 58 * 2**20
VMEM = pl.BlockSpec(memory_space=pltpu.VMEM)
SMEM = pl.BlockSpec(memory_space=pltpu.SMEM)
ANY = pl.BlockSpec(memory_space=pl.ANY)


TILE = (8, 128)


class Tiles:
    def __init__(self, rows, lanes):
        self.grid = (rows // TILE[0], lanes // TILE[1])
        self.spots = [(i, j) for i in range(self.grid[0]) for j in range(self.grid[1])]
        self.at_end, self.at_start = [], []
        for axis in range(2):
            place = lax.broadcasted_iota(jnp.int32, TILE, axis)
            self.at_end.append(place == TILE[axis] - 1)
            self.at_start.append(place == 0)

    def where(self, spot):
        return (slice(spot[0] * TILE[0], (spot[0] + 1) * TILE[0]), slice(spot[1] * TILE[1], (spot[1] + 1) * TILE[1]))

    def load(self, ref, *lead):
        return {spot: ref[lead + self.where(spot)] for spot in self.spots}

    def store(self, ref, lead, values):
        for spot in self.spots:
            ref[lead + self.where(spot)] = values[spot]

    def each(self, function, *values):
        return {spot: function(*(value[spot] for value in values)) for spot in self.spots}

    def side(self, step, axis):
        return (self.at_end if step > 0 else self.at_start)[axis]

    def is_edge(self, spot, step, axis):
        return spot[axis] == (self.grid[axis] - 1 if step > 0 else 0)

    def move(self, values, step, axis, fill):
        rolled = self.each(lambda tile: pltpu.roll(tile, TILE[axis] - 1 if step > 0 else 1, axis), values)
        side, moved = self.side(step, axis), {}
        for spot in self.spots:
            if self.is_edge(spot, step, axis):
                moved[spot] = jnp.where(side, 0.0, rolled[spot]) if fill else rolled[spot]
            else:
                other = (spot[0] + step, spot[1]) if axis == 0 else (spot[0], spot[1] + step)
                moved[spot] = jnp.where(side, rolled[other], rolled[spot])
        return moved

    def inner(self, values, step, axis):
        side = self.side(step, axis)
        return {
            spot: jnp.where(side, 0.0, values[spot]) if self.is_edge(spot, step, axis) else values[spot]
            for spot in self.spots
        }


SIDES = ((1, 0), (-1, 0), (1, 1), (-1, 1))


def double_couplings(tiles, center, above, below):
    add = lambda one, other: one + other
    weights = [tiles.each(add, center, above), tiles.each(add, center, below)]
    total = tiles.each(add, *weights)
    for step, axis in SIDES:
        weight = tiles.each(add, center, tiles.move(center, step, axis, True))
        total = tiles.each(add, total, weight)
        weights.append(tiles.inner(weight, step, axis))
    return weights, tiles.each(lambda value: value + 2.0 * kappa, total)


def pull(tiles, start, weights, center, beside):
    moved = list(beside) + [tiles.move(center, step, axis, False) for step, axis in SIDES]
    total = start
    for weight, other in zip(weights, moved):
        total = tiles.each(lambda so_far, w, value: so_far + w * value, total, weight, other)
    return total


def flux_squared(tiles, field, plane):
    ax, ay, az = (tiles.load(field, part, plane) for part in range(3))
    ay_first, az_first = tiles.load(field, 1, plane + 1), tiles.load(field, 2, plane + 1)
    ax_second, az_second = tiles.move(ax, 1, 0, True), tiles.move(az, 1, 0, True)
    ax_third, ay_third = tiles.move(ax, 1, 1, True), tiles.move(ay, 1, 1, True)

    def square(x, y, z, y1, z1, x2, z2, x3, y3):
        flux_one = (z2 - z) - (y3 - y)
        flux_two = (x3 - x) - (z1 - z)
        flux_three = (y1 - y) - (x2 - x)
        return flux_one * flux_one + flux_two * flux_two + flux_three * flux_three

    return tiles.each(square, ax, ay, az, ay_first, az_first, ax_second, az_second, ax_third, ay_third)


def reluctivity(tiles, flux_sq, base, slope_of, slope_total, incremental):
    doubled = tiles.each(lambda value: value * (1.0 / soft_width), flux_sq)
    excess = tiles.each(lambda value: jnp.maximum(value - CAP, 0.0), doubled)
    floor = tiles.each(lambda value: jnp.exp(-value), excess)
    rising = tiles.each(lambda value: jnp.exp(jnp.minimum(value, CAP)), doubled)
    nu = tiles.each(lambda start, slope, value: start + slope * value, base, slope_total, excess)
    slope_sum = None
    for knot in range(KNOTS):
        factor = math.exp(-knot_step * knot / soft_width)
        slope = slope_of(knot)
        high = tiles.each(lambda value: value * factor, rising)
        both = tiles.each(lambda one, other: one + other, high, floor)
        nu = tiles.each(lambda so_far, weight, value: so_far + weight * jnp.log(value), nu, slope, both)
        if incremental:
            part = tiles.each(lambda weight, one, other: weight * (one / other), slope, high, both)
            slope_sum = tiles.each(lambda one, other: one + other, slope_sum, part) if knot else part
    if incremental:
        nu = tiles.each(lambda value, s, slope: value + (2.0 / soft_width) * (s * slope), nu, flux_sq, slope_sum)
    return nu


def loop_in_pairs(count, body):
    def step(at, carry):
        body(2 * at)
        body(2 * at + 1)
        return carry

    lax.fori_loop(0, count // 2, step, 0)
    if count % 2:
        body(count - 1)


LOW_SIZE = 3 * (A_LOW[0] + S_LOW) + G_LOW
HIGH_SIZE = 3 * (A_HIGH[0] + S_HIGH) + G_HIGH - 2


def edge_parts(planes, low):
    halo_of = ((A_LOW if low else A_HIGH)[0], S_LOW if low else S_HIGH, G_LOW if low else G_HIGH)
    at, parts = 0, []
    for array in range(7):
        halo = halo_of[0 if array < 3 else 1 if array < 6 else 2]
        if not low and array in (0, 3):
            halo -= 1
        parts.append((array * planes + (planes - halo if low else 0), at, halo))
        at += halo
    return parts


def write_edge(target, whole, low):
    for first, at, halo in edge_parts(whole.shape[0] // 7, low):
        target[at:at + halo] = whole[first:first + halo]


def is_odd():
    return lax.rem(lax.axis_index("mesh"), 2) == 1


def pack_kernel(start, source, region, whole, apart, paired, token, marks, sems):
    token[...] = jnp.zeros(token.shape, token.dtype)
    planes = region.shape[0]
    copies = [pltpu.make_async_copy(region, marks, sems.at[0])]
    for part in range(3):
        for at, origin in ((part, start), (3 + part, source)):
            target = whole.at[at * planes:(at + 1) * planes]
            copies.append(pltpu.make_async_copy(origin.at[part], target, sems.at[at + 1]))
    for copy in copies:
        copy.start()
    for copy in copies:
        copy.wait()
    whole[6 * planes:] = marks[...].astype(jnp.float32)
    for odd in (False, True):
        pl.when(is_odd() == odd)(functools.partial(write_edge, apart, whole, odd))
        pl.when(is_odd() == odd)(functools.partial(write_edge, paired, whole, not odd))


def pair_kernel(*refs):
    wholes, (paired, token) = refs[:-3], refs[-2:]
    token[...] = jnp.zeros(token.shape, token.dtype)
    for odd in (False, True):

        @pl.when(is_odd() == odd)
        def write():
            for turn, whole in enumerate(wholes):
                write_edge(paired.at[turn], whole, not odd)


def is_second():
    return lax.rem(lax.axis_index("mesh") + 1, 4) < 2


def send_edges(start, source, buffer, target, top, sems):
    harmonics, planes = start.shape[0], start.shape[3]
    middle = (harmonics + 1) // 2
    ways = []
    for chosen in (slice(0, middle), slice(middle, harmonics)):
        if chosen.start == chosen.stop:
            continue
        for origin, count, onto in ((start, 2, 0), (source, 1, 2)):
            at = jnp.where(top, planes - count, 0)
            held = planes_of(buffer.at[chosen], onto, count)
            ways.append(
                (
                    pltpu.make_async_copy(planes_of(origin.at[chosen], at, count), held, sems.at[0, len(ways)]),
                    pltpu.make_async_copy(held, planes_of(target.at[chosen], onto, count), sems.at[1, len(ways)]),
                )
            )
    for way_in, unused in ways:
        way_in.start()
    for way_in, way_out in ways:
        way_in.wait()
        way_out.start()
    for unused, way_out in ways:
        way_out.wait()


def send_near_edges(origins, targets, buffers, sems):
    ways = []
    for number, (origin, buffer, target) in enumerate(zip(origins, buffers, targets)):
        planes, count = origin.shape[3], target.shape[3]
        first = jnp.where(is_odd(), 0, planes - count)
        held = planes_of(buffer, 0, count)
        ways.append(
            (
                pltpu.make_async_copy(planes_of(origin, first, count), held, sems.at[2 * number]),
                pltpu.make_async_copy(held, target, sems.at[2 * number + 1]),
            )
        )
    for way_in, unused in ways:
        way_in.start()
    for way_in, way_out in ways:
        way_in.wait()
        way_out.start()
    for unused, way_out in ways:
        way_out.wait()


def first_edges_kernel(
    start, source, after, apart, paired_start, paired_source, token, buffer, sems, near_sems
):
    token[...] = jnp.zeros(token.shape, token.dtype)

    @pl.when(jnp.logical_not(is_second()))
    def send_apart():
        send_edges(start, source, buffer, apart, is_odd(), sems)

    @pl.when(is_second())
    def send_near():
        send_near_edges([source], [paired_source], [buffer], near_sems)


def near_edges_kernel(start, source, after, start_in, source_in, paired_start, paired_source, buffer, other_buffer, sems):
    @pl.when(jnp.logical_not(is_second()))
    def send_both():
        send_near_edges([start, source], [paired_start, paired_source], [buffer, other_buffer], sems)

    @pl.when(is_second())
    def send_start():
        send_near_edges([start], [paired_start], [buffer], sems)


def second_edges_kernel(start, source, after, apart_in, apart, buffer, sems):
    @pl.when(is_second())
    def send_apart():
        send_edges(start, source, buffer, apart, is_odd(), sems)


def bias_kernel(shares, meshes, *refs):
    wholes, aparts, (paired, others) = refs[:shares], refs[shares:2 * shares], refs[2 * shares:2 * shares + 2]
    paireds = [paired] + [others.at[at] for at in range(shares - 1)]
    table_index, bh_base, bh_slope, conductivity, field_out, nud_out, sigma_out = refs[2 * shares + 2:2 * shares + 9]
    a0, a1, src, marks, nu, slopes, bases = refs[2 * shares + 9:]
    planes = wholes[0].shape[0] // 7
    rows_each, lanes = wholes[0].shape[1:]
    rows = rows_each * shares
    mine = lax.axis_index("harm")
    here = lax.axis_index("mesh")
    arrays = [(a0.at[part], A_LOW[0]) for part in range(3)]
    arrays += [(src.at[part], S_LOW) for part in range(3)] + [(marks, G_LOW)]
    for turn in range(shares):
        owner = lax.rem(mine + shares - turn, shares)
        at = pl.ds(pl.multiple_of(owner * rows_each, rows_each), rows_each)

        def fill(low, high):
            for (target, onto), (unused, first, halo) in zip(arrays, edge_parts(planes, True)):
                target[0:halo, at, :] = low[first:first + halo]
            for (target, onto), (unused, first, halo) in zip(arrays, edge_parts(planes, False)):
                target[onto + planes:onto + planes + halo, at, :] = high[first:first + halo]

        for number, (target, onto) in enumerate(arrays):
            target[onto:onto + planes, at, :] = wholes[turn][number * planes:(number + 1) * planes]
        pl.when(is_odd())(functools.partial(fill, paireds[turn], aparts[turn]))
        pl.when(jnp.logical_not(is_odd()))(functools.partial(fill, aparts[turn], paireds[turn]))

    tiles = Tiles(rows, lanes)
    tables = [table_index[member] for member in range(MATS)]
    base_of = [bh_base[table] for table in tables]
    slope_of = [[soft_width * bh_slope[table, knot] for table in tables] for knot in range(KNOTS)]
    sigma_of = [conductivity[member] for member in range(MATS)]

    def inside(plane):
        low_ok = jnp.logical_or(plane >= 0, here > 0)
        high_ok = jnp.logical_or(plane < planes, here < meshes - 1)
        return jnp.where(jnp.logical_and(low_ok, high_ok), 1.0, 0.0)

    def choose(marks_are, values):
        def one(*marked):
            chosen = jnp.where(marked[0], values[1], values[0])
            for member in range(2, MATS):
                chosen = jnp.where(marked[member - 1], values[member], chosen)
            return chosen

        return tiles.each(one, *marks_are)

    def members(mark):
        return [tiles.each(lambda value: value == float(member), mark) for member in range(1, MATS)]

    def relax_into(target, step, old):
        def body(at):
            plane = at - A_LOW[step]
            near = at + 1
            weights, total = double_couplings(
                tiles, tiles.load(nu, near), tiles.load(nu, near + 1), tiles.load(nu, near - 1)
            )
            keep = inside(plane)
            scale = tiles.each(lambda value: keep / value, total)
            from_old = plane + A_LOW[step - 1]
            for part in range(3):
                twice = tiles.each(lambda value: value + value, tiles.load(src, part, plane + S_LOW))
                near_old = [tiles.load(old, part, from_old + move) for move in (0, 1, -1)]
                moved = pull(tiles, twice, weights, near_old[0], near_old[1:])
                tiles.store(target, (part, at), tiles.each(lambda value, by: value * by, moved, scale))

        loop_in_pairs(planes + A_LOW[step] + A_HIGH[step], body)

    def first_nu(at):
        marked = members(tiles.load(marks, at))
        base, slope = choose(marked, base_of), [choose(marked, slope_of[knot]) for knot in range(KNOTS)]
        whole_slope = slope[0]
        tiles.store(bases, (at,), base)
        for knot in range(KNOTS):
            tiles.store(slopes, (knot, at), slope[knot])
            if knot:
                whole_slope = tiles.each(lambda one, other: one + other, whole_slope, slope[knot])
        tiles.store(slopes, (KNOTS, at), whole_slope)
        value = reluctivity(tiles, flux_squared(tiles, a0, at), base, lambda knot: slope[knot], whole_slope, False)
        keep = inside(at - G_LOW)
        tiles.store(nu, (at,), tiles.each(lambda one: one * keep, value))

    loop_in_pairs(planes + G_LOW + G_HIGH, first_nu)
    fields = (a0, a1)
    for step in range(1, ITERS_B + 1):
        old, new = fields[(step - 1) % 2], fields[step % 2]
        relax_into(new, step, old)
        last = step == ITERS_B
        lower = NUD_LOW if last else A_LOW[step + 1] + 1
        upper = NUD_HIGH if last else A_HIGH[step + 1] + 1

        def next_nu(at):
            plane = at - lower
            known = plane + G_LOW
            value = reluctivity(
                tiles, flux_squared(tiles, new, plane + A_LOW[step]), tiles.load(bases, known),
                lambda knot: tiles.load(slopes, knot, known), tiles.load(slopes, KNOTS, known), last,
            )
            keep = inside(plane)
            tiles.store(nud_out if last else nu, (at,), tiles.each(lambda one: one * keep, value))

        loop_in_pairs(planes + lower + upper, next_nu)

    def sigma_at(at):
        marked = members(tiles.load(marks, at - (ITERS_R - 1) + G_LOW))
        tiles.store(sigma_out, (at,), choose(marked, sigma_of))

    loop_in_pairs(planes + 2 * (ITERS_R - 1), sigma_at)
    own_rows = pl.ds(pl.multiple_of(mine * rows_each, rows_each), rows_each)
    final = fields[ITERS_B % 2]
    for part in range(3):
        field_out[part] = final[part, A_LOW[ITERS_B]:A_LOW[ITERS_B] + planes, own_rows, :]


def planes_of(ref, first, count):
    return ref.at[:, :, :, pl.ds(first, count)]


class Ripple:
    def __init__(self, rows, lanes, harmonic_numbers, count, sides, answer):
        self.sides, self.answer, self.tiles = sides, answer, Tiles(rows, lanes)
        first = lax.axis_index("harm") * count
        self.omegas = [omega_step * harmonic_numbers[first + at].astype(jnp.float32) for at in range(count)]

    def prepare(self, nud, sigma, slot, keep):
        tiles, near = self.tiles, slot + NUD_LOW - 1
        weights, total = double_couplings(tiles, *(tiles.load(nud, near + move) for move in (0, 1, -1)))
        for number, weight in enumerate(weights):
            tiles.store(self.sides, (number, slot), tiles.each(lambda value: 0.5 * value, weight))
        total = tiles.each(lambda value: 0.5 * value, total)
        square = tiles.each(lambda value: value * value, total)
        conduct = tiles.load(sigma, slot)
        for harmonic, omega in enumerate(self.omegas):
            damp = tiles.each(lambda value: omega * value, conduct)
            inverse = tiles.each(lambda one, other: keep / (one + other * other), square, damp)
            for part, value in enumerate((total, damp)):
                scaled = tiles.each(lambda one, other: one * other, value, inverse)
                tiles.store(self.answer, (harmonic, part, slot), scaled)

    def sweep(self, slot, old, source, put, turned_round=0, begin=False, begun=False):
        tiles, loss = self.tiles, None
        weights = [tiles.load(self.sides, number, slot) for number in (turned_round, 1 - turned_round, 2, 3, 4, 5)]
        for harmonic in range(len(self.omegas)):
            straight, turned = (tiles.load(self.answer, harmonic, part, slot) for part in range(2))
            power = None
            for part in range(3):
                both = []
                for piece in range(2):
                    lead = (harmonic, piece, part)
                    near_old = [tiles.load(ref, *lead, at) for ref, at in old]
                    given = tiles.load(source[0], *lead, source[1])
                    if begun:
                        add_last = lambda so_far, weight, value: so_far + weight * value
                        both.append(tiles.each(add_last, given, weights[1], near_old[0]))
                        continue
                    used = weights[:1] + weights[2:] if begin else weights
                    both.append(pull(tiles, given, used, near_old[0], near_old[1:]))
                if begin:
                    for piece, value in enumerate(both):
                        tiles.store(put[0], (harmonic, piece, part, put[1]), value)
                    continue
                real = tiles.each(lambda re, im, a, b: re * a + im * b, *both, straight, turned)
                imag = tiles.each(lambda re, im, a, b: im * a - re * b, *both, straight, turned)
                for piece, value in enumerate((real, imag)):
                    tiles.store(put[0], (harmonic, piece, part, put[1]), value)
                squared = tiles.each(lambda re, im: re * re + im * im, real, imag)
                power = tiles.each(lambda one, other: one + other, power, squared) if part else squared
            if begin:
                continue
            factor = 0.5 * self.omegas[harmonic] * self.omegas[harmonic]
            scaled = tiles.each(lambda value: factor * value, power)
            loss = tiles.each(lambda one, other: one + other, loss, scaled) if loss else scaled
        return loss


class Side:
    def __init__(self, planes, high):
        pick = lambda above, below: jnp.where(high, above, below)
        self.turned_round = pick(1, 0)
        self.own, self.second = pick(planes - 1, 0), pick(planes - 2, 1)
        self.beyond_slot, self.own_slot, self.second_slot = pick(planes + 1, 0), pick(planes, 1), pick(planes - 1, 2)
        self.halo, self.far_halo = pick(0, 1), pick(1, 0)
        self.third = pick(planes - 3, 2)


def first_on_side(ripple, side, start, source, halo_start, halo_source, put_beyond, put_own):
    ripple.sweep(
        side.beyond_slot, [(halo_start, side.halo), (start, side.own), (halo_start, side.far_halo)],
        (halo_source, 0),
        put_beyond, side.turned_round,
    )
    ripple.sweep(
        side.own_slot, [(start, side.own), (start, side.second), (halo_start, side.halo)], (source, side.own),
        put_own, side.turned_round,
    )


def inner_kernel(
    meshes, harmonic_numbers, nud, sigma, start, source, paired_start, paired_source, ripple_out, edge_out, begun_out,
    loss_out, sides, answer, r1, r2, sems
):
    count, planes = start.shape[0], start.shape[3]
    here = lax.axis_index("mesh")
    odd = is_odd()
    ripple = Ripple(*start.shape[4:], harmonic_numbers, count, sides, answer)
    tiles = ripple.tiles

    def prepare(slot):
        low_ok = jnp.logical_or(slot > 0, here > 0)
        high_ok = jnp.logical_or(slot < planes + 1, here < meshes - 1)
        ripple.prepare(nud, sigma, slot, jnp.where(jnp.logical_and(low_ok, high_ok), 1.0, 0.0))

    def drain(plane):
        return pltpu.make_async_copy(planes_of(r2, plane, 1), planes_of(ripple_out, plane, 1), sems.at[plane])

    def first(plane, carry):
        ripple.sweep(
            plane + 1, [(start, plane), (start, plane + 1), (start, plane - 1)], (source, plane), (r1, plane + 1)
        )
        return carry

    def second(plane, carry):
        loss = ripple.sweep(
            plane + 1, [(r1, plane + 1), (r1, plane + 2), (r1, plane)], (source, plane), (r2, plane)
        )
        tiles.store(loss_out, (plane,), tiles.each(lambda one, other: one * other, tiles.load(sigma, plane + 1), loss))
        drain(plane).start()
        return carry

    def finish(plane, carry):
        drain(plane).wait()
        return carry

    near, far = Side(planes, jnp.logical_not(odd)), Side(planes, odd)
    loop_in_pairs(planes + 2, prepare)
    lax.fori_loop(1, planes - 1, first, 0)
    first_on_side(
        ripple, near, start, source, paired_start, paired_source, (r1, near.beyond_slot), (r1, near.own_slot)
    )
    begin, end = jnp.where(odd, 0, 2), jnp.where(odd, planes - 2, planes)
    lax.fori_loop(begin, end, second, 0)
    edge_out[:, :, :, 0] = r1[:, :, :, far.second_slot]
    ripple.sweep(
        far.own_slot, [(start, far.own), (start, far.second)], (source, far.own), (begun_out, 0), far.turned_round, begin=True
    )
    ripple.sweep(
        far.second_slot, [(r1, far.second_slot), (r1, far.third + 1)], (source, far.second), (begun_out, 1),
        far.turned_round, begin=True,
    )
    lax.fori_loop(begin, end, finish, 0)


def outer_kernel(
    shares, harmonic_numbers, sigma, start, source, apart, edge, begun, sides, answer, loss_in,
    r2, *refs
):
    losses, (r1, loss) = refs[:shares], refs[shares:]
    count, planes = start.shape[0], start.shape[3]
    rows, lanes = start.shape[4:]

    far = Side(planes, is_odd())
    ripple = Ripple(rows, lanes, harmonic_numbers, count, sides, answer)
    tiles = ripple.tiles
    ripple.sweep(
        far.beyond_slot, [(apart, far.halo), (start, far.own), (apart, far.far_halo)], (apart, 2), (r1, 0), far.turned_round
    )
    ripple.sweep(far.own_slot, [(apart, far.halo)], (begun, 0), (r1, 1), far.turned_round, begun=True)

    steps = (
        (far.own, far.own_slot, [(r1, 1), (edge, 0), (r1, 0)], (source, far.own), False),
        (far.second, far.second_slot, [(r1, 1)], (begun, 1), True),
    )
    for at, (plane, slot, old, given, is_begun) in enumerate(steps):
        added = ripple.sweep(slot, old, given, (r2, at), far.turned_round, begun=is_begun)
        tiles.store(loss, (at,), tiles.each(lambda one, other: one * other, tiles.load(sigma, slot), added))
    rows_each = rows // shares
    for turn in range(shares):
        owner = lax.rem(lax.axis_index("harm") + turn, shares)
        part = pl.ds(pl.multiple_of(owner * rows_each, rows_each), rows_each)
        losses[turn][...] = loss_in[:, part, :]
        for at, (plane, *unused) in enumerate(steps):
            losses[turn][plane] = loss[at, part, :]


def place_kernel(edge, ripple_in, ripple_out, sems):
    far = Side(ripple_out.shape[3], is_odd())
    copies = [
        pltpu.make_async_copy(planes_of(edge, at, 1), planes_of(ripple_out, plane, 1), sems.at[at])
        for at, plane in enumerate((far.own, far.second))
    ]
    for copy in copies:
        copy.start()
    for copy in copies:
        copy.wait()


def call(kernel, operands, in_specs, out_shapes, out_specs, scratch, name, work=0, aliases={}, room=0):
    f32 = jnp.float32
    shapes = [o.shape for o, spec in zip(operands, in_specs) if spec is VMEM]
    shapes += [shape for shape, spec in zip(out_shapes, out_specs) if spec is VMEM]
    shapes += [shape for shape in scratch if isinstance(shape, tuple)]
    held = 4 * sum(math.prod(shape) for shape in shapes)
    return pl.pallas_call(
        kernel,
        out_shape=[jax.ShapeDtypeStruct(shape, f32) for shape in out_shapes],
        in_specs=in_specs,
        out_specs=out_specs,
        scratch_shapes=[pltpu.VMEM(shape, f32) if isinstance(shape, tuple) else shape for shape in scratch],
        compiler_params=pltpu.CompilerParams(vmem_limit_bytes=room or held + 4 * 2**20),
        cost_estimate=pl.CostEstimate(flops=work * 300, bytes_accessed=work, transcendentals=0),
        input_output_aliases=aliases,
        name=name,
    )(*operands)


def body(
    meshes, shares, bias_source, bias_start, region, table_index, bh_base, bh_slope, conductivity, harmonic_numbers,
    ripple_source, ripple_start,
):
    unused, planes, rows_each, lanes = bias_start.shape
    rows = rows_each * shares
    count = ripple_start.shape[0]
    near = [(i, i + 1) for i in range(0, meshes - 1, 2)]
    far = [(i, i + 1) for i in range(1, meshes - 1, 2)]
    near += [(j, i) for i, j in near]
    far += [(j, i) for i, j in far]
    turned = [[(i, (i + turn) % shares) for i in range(shares)] for turn in range(1, shares)]

    def around(block):
        return [block] + [lax.ppermute(block, "harm", pairs) for pairs in turned]

    whole, apart, paired, token = call(
        pack_kernel, (bias_start, bias_source, region), [ANY] * 3,
        [(7 * planes, rows_each, lanes), (HIGH_SIZE, rows_each, lanes), (HIGH_SIZE, rows_each, lanes), TILE], [VMEM] * 4,
        [pltpu.VMEM(region.shape, region.dtype), pltpu.SemaphoreType.DMA((7,))], "pack", room=PACK_ROOM,
    )
    wholes = around(whole)
    aparts = around(lax.ppermute(apart, "mesh", far))
    edge = ripple_start.shape[:3] + (3, rows, lanes)
    near_edges = [edge[:3] + (size, rows, lanes) for size in (2, 1)]
    ripple_apart, paired_start, paired_source, token = call(
        first_edges_kernel, (ripple_start, ripple_source, token), [ANY] * 3,
        [edge] + near_edges + [TILE], [ANY] * 3 + [VMEM],
        [edge, pltpu.SemaphoreType.DMA((2, 4)), pltpu.SemaphoreType.DMA((2,))], "first_edges", room=RP_ROOM,
    )
    ripple_apart, = call(
        second_edges_kernel, (ripple_start, ripple_source, token, ripple_apart), [ANY] * 4, [edge], [ANY],
        [edge, pltpu.SemaphoreType.DMA((2, 4))], "second_edges", aliases={3: 0}, room=RP_ROOM,
    )
    others, token = call(
        pair_kernel, (*wholes[1:], aparts[0]), [VMEM] * (shares - 1) + [ANY],
        [(shares - 1, HIGH_SIZE, rows_each, lanes), TILE], [VMEM] * 2, [], "pair",
    )
    ripple_paireds = call(
        near_edges_kernel, (ripple_start, ripple_source, token, paired_start, paired_source), [ANY] * 5,
        near_edges, [ANY] * 2, [edge, edge, pltpu.SemaphoreType.DMA((4,))], "near_edges", aliases={3: 0, 4: 1},
        room=NEAR_ROOM,
    )
    paireds = [lax.ppermute(paired, "mesh", near), lax.ppermute(others, "mesh", near)]
    ripple_apart = lax.ppermute(ripple_apart, "mesh", far)
    ripple_paireds = [lax.ppermute(part, "mesh", near) for part in ripple_paireds]

    known = (planes + G_LOW + G_HIGH, rows, lanes)
    field, nud, sigma = call(
        functools.partial(bias_kernel, shares, meshes),
        (*wholes, *aparts, *paireds, table_index, bh_base, bh_slope, conductivity),
        [VMEM] * (2 * shares + 2) + [SMEM] * 4,
        [
            bias_start.shape, (planes + NUD_LOW + NUD_HIGH, rows, lanes), (planes + 2 * (ITERS_R - 1), rows, lanes)
        ],
        [VMEM] * 3,
        [
            (3, planes + A_LOW[0] + A_HIGH[0], rows, lanes),
            (3, planes + A_LOW[1] + A_HIGH[1], rows, lanes),
            (3, planes + S_LOW + S_HIGH, rows, lanes),
            known,
            known,
            (KNOTS + 1, *known),
            known,
        ],
        "bias",
        BIAS_WORK,
    )

    lead = ripple_start.shape[:3]
    slots = (planes + 2, rows, lanes)
    ripple, edge, begun, inner_loss, sides, answer = call(
        functools.partial(inner_kernel, meshes),
        (harmonic_numbers, nud, sigma, ripple_start, ripple_source, *ripple_paireds), [SMEM] + [VMEM] * 6,
        [
            ripple_start.shape, lead + (1, rows, lanes), lead + (2, rows, lanes), (planes, rows, lanes), (6, *slots),
            (count, 2, *slots),
        ],
        [ANY] + [VMEM] * 5, [lead + slots, lead + (planes, rows, lanes), pltpu.SemaphoreType.DMA((planes,))],
        "inner_ripple",
    )
    outer_edge, *losses = call(
        functools.partial(outer_kernel, shares),
        (harmonic_numbers, sigma, ripple_start, ripple_source, ripple_apart, edge, begun, sides, answer, inner_loss),
        [SMEM] + [VMEM] * 9, [lead + (2, rows, lanes)] + [(planes, rows_each, lanes)] * shares, [VMEM] * (shares + 1),
        [lead + (2, rows, lanes), (2, rows, lanes)], "outer_ripple",
    )
    ripple, = call(
        place_kernel, (outer_edge, ripple), [ANY] * 2, [ripple_start.shape], [ANY], [pltpu.SemaphoreType.DMA((2,))],
        "place", PLACE_WORK, aliases={1: 0},
    )
    loss = losses[0]
    for turn, pairs in enumerate(turned):
        loss = loss + lax.ppermute(losses[turn + 1], "harm", pairs)
    return field, ripple, loss


def solution(mesh):
    return jax.shard_map(
        functools.partial(body, mesh.shape["mesh"], mesh.shape["harm"]),
        mesh=mesh,
        in_specs=(
            P(None, "mesh", "harm", None),
            P(None, "mesh", "harm", None),
            P("mesh", "harm", None),
            P(),
            P(),
            P(),
            P(),
            P(),
            P("harm", None, None, "mesh", None, None),
            P("harm", None, None, "mesh", None, None),
        ),
        out_specs=(
            P(None, "mesh", "harm", None),
            P("harm", None, None, "mesh", None, None),
            P("mesh", "harm", None),
        ),
        check_vma=False,
    )
```
